32 devices in a mesh: depth: 16 (over z, x, core), shot: 2 (over y).
Axes of the slice: x: 2, y: 2, z: 4, core: 2. Of those that a mesh axis runs over, the one named last changes fastest.
Arguments:
- courant: float32 [256, 64, 128], P('depth'), may hold values from 0.04 to 0.2
- wave_before: float32 [2, 256, 64, 128], P('shot', 'depth'), may hold values from -10 to 10
- wave_current: float32 [2, 256, 64, 128], P('shot', 'depth'), may hold values from -10 to 10
- adjoint_after: float32 [2, 256, 64, 128], P('shot', 'depth'), may hold values from -10 to 10
- adjoint_current: float32 [2, 256, 64, 128], P('shot', 'depth'), may hold values from -10 to 10
- source_cell: int32 [2], P('shot'), may hold values from 0 to 2097151
- wavelet: float32 [2, 4], P('shot'), may hold values from -15 to 15
- receiver_cell: int32 [2, 256], P('shot'), may hold values from 0 to 2097151
- residual: float32 [2, 4, 256], P('shot'), may hold values from -12 to 12
- history: float32 [2, 5, 256, 64, 128], P(None, None, 'depth', 'shot'), may hold values from -23 to 23, as said below
Outputs:
- gradient: float32 [256, 64, 128], P('depth', 'shot')
- direction: float32 [256, 64, 128], P('depth', 'shot')
- courant_next: float32 [256, 64, 128], P('depth')
The draws below stay inside these ranges and needn't reach their ends.
Inputs may be any that keep to these rules, and one draw needn't show every extreme that they name: In every pair the sum over all cells of history[0] times history[1] is positive.
All inputs are finite; a program needn't handle non-finite values.
Results may differ from the reference program's by a relative error of at most 0.00026.
Values sent between devices are 32-bit elements; how exact they have to be, the bound alone decides.
No kernel may reach another device: no remote copies, remote signals or barrier semaphores. Data moves between devices by JAX's collectives and lax.ppermute only.
A program may use at most 128 MiB of HBM per device.

```python
import math
import jax
import jax.numpy as jnp

NX = 64
NY = 128
RECV = 256
STEPS = 4
PAIRS = 5
SHOTS = 2
NZ = 256


def shared_pattern(key):
    base = jax.random.fold_in(key, 7001)
    key_sign, key_phase, key_amp = jax.random.split(base, 3)
    signs = jax.random.randint(key_sign, (SHOTS, 3), 0, 2) * 2 - 1
    phase = jax.random.uniform(key_phase, (SHOTS, 1, 1, 1), jnp.float32, -math.pi, math.pi)
    amplitude = jax.random.uniform(key_amp, (SHOTS, 1, 1, 1), jnp.float32, 2.5, 3.5)
    depth_index = jnp.arange(NZ, dtype=jnp.int32)[None, :, None, None]
    across_index = jnp.arange(NX, dtype=jnp.int32)[None, None, :, None]
    along_index = jnp.arange(NY, dtype=jnp.int32)[None, None, None, :]
    sign_depth = signs[:, 0][:, None, None, None]
    sign_across = signs[:, 1][:, None, None, None]
    sign_along = signs[:, 2][:, None, None, None]
    cycle = (sign_depth * depth_index + sign_across * across_index + sign_along * along_index + 1024) % 16
    angle = cycle.astype(jnp.float32) * (2.0 * math.pi / 16.0) + phase
    return amplitude * jnp.cos(angle)


def rough_part(key, label):
    sub_key = jax.random.fold_in(key, label)
    array_shape = (SHOTS, NZ, NX, NY)
    return jnp.clip(jax.random.normal(sub_key, array_shape, jnp.float32), -6.0, 6.0)


def draw_wave_before(key, part):
    return (shared_pattern(key) + rough_part(key, 8101)).astype(jnp.float32)


def draw_wave_current(key, part):
    return (shared_pattern(key) + rough_part(key, 8102)).astype(jnp.float32)


def draw_adjoint_after(key, part):
    return (shared_pattern(key) + rough_part(key, 8103)).astype(jnp.float32)


def draw_adjoint_current(key, part):
    return (shared_pattern(key) + rough_part(key, 8104)).astype(jnp.float32)


def draw_history(key, part):
    key_steps, key_factor, key_offset = jax.random.split(key, 3)
    array_shape = (PAIRS, NZ, NX, NY)
    offsets = jax.random.uniform(key_offset, (PAIRS, 1, 1, 1), jnp.float32, 0.6, 1.4)
    noise = jnp.clip(jax.random.normal(key_steps, array_shape, jnp.float32), -6.0, 6.0)
    displaced = offsets + noise
    factor = jnp.exp(jax.random.uniform(key_factor, array_shape, jnp.float32, math.log(0.3), math.log(3.0)))
    return jnp.stack([displaced, displaced * factor]).astype(jnp.float32)


def set_ends(drawn, rng, smallest, largest):
    dims = drawn.shape
    spot = [jax.random.randint(jax.random.fold_in(rng, axis), (), 0, dims[axis]) for axis in range(len(dims))]
    drawn = drawn.at[tuple(spot)].set(smallest)
    longest = dims.index(max(dims))
    spot[longest] = (spot[longest] + 1) % dims[longest]
    return drawn.at[tuple(spot)].set(largest)


def level_of(stream_key, shape, cuts, low, largest):
    def one(dim, shards_of):
        draws = jax.random.uniform(jax.random.fold_in(jax.random.fold_in(stream_key, 6), dim), (shards_of,), jnp.float32, low / len(cuts), largest / len(cuts))
        return jnp.repeat(jnp.exp(draws), shape[dim] // shards_of).reshape((-1,) + (1,) * (len(shape) - dim - 1))

    loudness = one(*cuts[0])
    for cut in cuts[1:]:
        loudness = loudness * one(*cut)
    return loudness


def bell_draw(own_key, extent, scale, limit, shards=(), held_as=jnp.bfloat16):
    result = scale * jax.random.normal(own_key, extent, jnp.float32)
    if shards:
        result = result * level_of(own_key, extent, shards, -0.22, 0.18)
    return jnp.clip(result, -limit, limit).astype(held_as)


def setup_inputs(seed: int = 0) -> dict:
    keys = jax.random.split(jax.random.key(seed), 11)
    return {
        "courant": jnp.clip(jnp.exp(math.log(0.2) - 1.609438 * jax.random.uniform(keys[0], (NZ, NX, NY), jnp.float32) ** level_of(keys[0], (NZ, NX, NY), ((0, 16),), -0.2, 0.2)), 0.04, 0.2),
        "wave_before": draw_wave_before(jax.random.fold_in(keys[10], 71), 0),
        "wave_current": draw_wave_current(jax.random.fold_in(keys[10], 71), 0),
        "adjoint_after": draw_adjoint_after(jax.random.fold_in(keys[10], 71), 0),
        "adjoint_current": draw_adjoint_current(jax.random.fold_in(keys[10], 71), 0),
        "source_cell": jax.random.randint(keys[5], (SHOTS,), 0, NZ * NX * NY).astype(jnp.int32),
        "wavelet": bell_draw(keys[6], (SHOTS, STEPS), 5.0, 15.0, ((0, 2),), jnp.float32),
        "receiver_cell": set_ends(jax.random.randint(keys[7], (SHOTS, RECV), 0, NZ * NX * NY), jax.random.fold_in(keys[7], 1), 0, (NZ * NX * NY) - 1).astype(jnp.int32),
        "residual": bell_draw(keys[8], (SHOTS, STEPS, RECV), 3.0, 12.0, ((0, 2),), jnp.float32),
        "history": draw_history(jax.random.fold_in(keys[10], 71), 0),
    }


coefficients = (-205.0 / 72.0, 8.0 / 5.0, -1.0 / 5.0, 8.0 / 315.0, -1.0 / 560.0)


def laplace_core(extended):
    interior = extended[4:-4]
    count_rows = interior.shape[0]
    width_x = interior.shape[1]
    width_y = interior.shape[2]
    padded = jnp.pad(interior, ((0, 0), (4, 4), (4, 4)))
    summed = (3.0 * coefficients[0]) * interior
    for reach in range(1, 5):
        weight = coefficients[reach]
        summed = summed + weight * (extended[4 + reach:4 + reach + count_rows] + extended[4 - reach:4 - reach + count_rows])
        summed = summed + weight * (padded[:, 4 + reach:4 + reach + width_x, 4:4 + width_y] + padded[:, 4 - reach:4 - reach + width_x, 4:4 + width_y])
        summed = summed + weight * (padded[:, 4:4 + width_x, 4 + reach:4 + reach + width_y] + padded[:, 4:4 + width_x, 4 - reach:4 - reach + width_y])
    return summed


def inject(volume, cell_ids, values, offset):
    count_rows = volume.shape[0]
    plane_size = volume.shape[1] * volume.shape[2]
    depth_row = cell_ids // plane_size - offset
    remainder = cell_ids % plane_size
    inside = (depth_row >= 0) & (depth_row < count_rows)
    row_safe = jnp.clip(depth_row, 0, count_rows - 1)
    return volume.at[row_safe, remainder // volume.shape[2], remainder % volume.shape[2]].add(jnp.where(inside, values, jnp.zeros_like(values)))


def depth_pad(volume):
    return jnp.pad(volume, ((4, 4), (0, 0), (0, 0)))


def reference(courant, wave_before, wave_current, adjoint_after, adjoint_current, source_cell, wavelet, receiver_cell, residual, history):
    summed = jnp.zeros(courant.shape, jnp.float32)
    zero_offset = jnp.int32(0)
    for shot_num in range(SHOTS):
        wave_old = wave_before[shot_num]
        wave_now = wave_current[shot_num]
        laplacians = []
        for moment in range(STEPS):
            laplacian = laplace_core(depth_pad(wave_now))
            wave_new = 2.0 * wave_now - wave_old + courant * laplacian
            wave_new = inject(wave_new, source_cell[shot_num:shot_num + 1], wavelet[shot_num, moment:moment + 1], zero_offset)
            laplacians.append(laplacian)
            wave_old, wave_now = wave_now, wave_new
        adjoint_old = adjoint_after[shot_num]
        adjoint_now = adjoint_current[shot_num]
        for moment in reversed(range(STEPS)):
            adjoint_new = 2.0 * adjoint_now - adjoint_old + laplace_core(depth_pad(courant * adjoint_now))
            adjoint_new = inject(adjoint_new, receiver_cell[shot_num], residual[shot_num, moment], zero_offset)
            summed = summed + adjoint_new * laplacians[moment]
            adjoint_old, adjoint_now = adjoint_now, adjoint_new
    gradient = summed * (1.0 / (SHOTS * STEPS))
    displaced = history[0]
    changes = history[1]
    curvature = [jnp.sum(displaced[number] * changes[number]) for number in range(PAIRS)]
    inverse = [1.0 / value_sy for value_sy in curvature]
    search = gradient
    alphas = [None] * PAIRS
    for number in reversed(range(PAIRS)):
        alphas[number] = inverse[number] * jnp.sum(displaced[number] * search)
        search = search - alphas[number] * changes[number]
    scaled = (curvature[PAIRS - 1] / jnp.sum(changes[PAIRS - 1] * changes[PAIRS - 1])) * search
    for number in range(PAIRS):
        correction = inverse[number] * jnp.sum(changes[number] * scaled)
        scaled = scaled + (alphas[number] - correction) * displaced[number]
    direction = -scaled
    courant_next = courant + 0.05 * direction
    return (gradient, direction, courant_next)
```

```python
import functools

import jax
import jax.numpy as jnp
from jax import lax
from jax.experimental import pallas as pl
from jax.experimental.pallas import tpu as pltpu
from jax.sharding import PartitionSpec as P

STEPS = 4
PAIRS = 5
REACH = 4
PAD = 8
CHUNK = 16
coefficients = (-205.0 / 72.0, 8.0 / 5.0, -1.0 / 5.0, 8.0 / 315.0, -1.0 / 560.0)

F32 = jnp.float32
VM = pl.BlockSpec(memory_space=pltpu.VMEM)
SM = pl.BlockSpec(memory_space=pltpu.SMEM)
PARAMS = pltpu.CompilerParams(vmem_limit_bytes=16 << 20)


def shape(*dims):
    return jax.ShapeDtypeStruct(dims, F32)


def natural_row(row, rows, odd):
    return jnp.where(odd == 1, rows - 1 - row, row)


def odd_depth():
    return lax.rem(lax.axis_index("depth"), 2)


def lane_ids(width):
    return lax.broadcasted_iota(jnp.int32, (1, width), 1)


def laplace_chunk(ref, row, start, size):
    rows, width = ref.shape[0], ref.shape[2]
    core = ref[row, PAD + start : PAD + start + size, :]
    lane = lax.broadcasted_iota(jnp.int32, (size, width), 1)
    total = (3.0 * coefficients[0]) * core
    for reach in range(1, REACH + 1):
        near = (
            ref[row, PAD + start + reach : PAD + start + reach + size, :]
            + ref[row, PAD + start - reach : PAD + start - reach + size, :]
        )
        if row - reach >= 0:
            near = near + ref[row - reach, PAD + start : PAD + start + size, :]
        if row + reach < rows:
            near = near + ref[row + reach, PAD + start : PAD + start + size, :]
        near = near + jnp.where(lane >= reach, pltpu.roll(core, reach, 1), 0.0)
        near = near + jnp.where(lane < width - reach, pltpu.roll(core, width - reach, 1), 0.0)
        total = total + coefficients[reach] * near
    return total


def zero_pads(ref):
    rows, padded, width = ref.shape
    for row in range(rows):
        ref[row, :PAD, :] = jnp.zeros((PAD, width), F32)
        ref[row, padded - PAD :, :] = jnp.zeros((PAD, width), F32)


def first_send_kernel(wave, adjoint, courant, out_core, out_chip):
    rows = wave.shape[0]
    odd = odd_depth()
    for row in range(REACH):
        near = natural_row(rows - REACH + row, rows, odd)
        far = natural_row(row, rows, odd)
        out_core[row] = wave[near]
        out_core[REACH + row] = courant[near] * adjoint[near]
        out_chip[row] = wave[far]
        out_chip[REACH + row] = courant[far] * adjoint[far]


def prepare_kernel(wave, wave_old, adjoint, adjoint_old, courant, o_wave, o_wave_old, o_adj, o_adj_old, o_cour, o_prod):
    rows, across, width = wave.shape
    odd = odd_depth()
    zero_pads(o_wave)
    zero_pads(o_wave_old)
    zero_pads(o_prod)
    for row in range(rows):
        src = natural_row(row, rows, odd)
        o_wave[row, PAD : PAD + across, :] = wave[src]
        o_wave_old[row, PAD : PAD + across, :] = wave_old[src]
        o_adj[row] = adjoint[src]
        o_adj_old[row] = adjoint_old[src]
        o_cour[row] = courant[src]
        o_prod[row, PAD : PAD + across, :] = courant[src] * adjoint[src]


def split_cell(cell, rows, across, width):
    depth_row = cell // (across * width) - lax.axis_index("depth") * rows
    rest = cell % (across * width)
    inside = (depth_row >= 0) & (depth_row < rows)
    row = jnp.where(odd_depth() == 1, rows - 1 - depth_row, depth_row)
    return inside, row, rest // width, rest % width


def receiver_kernel(keys, places, residual, out):
    cells = out.shape[1]
    width = out.shape[2]
    count = keys.shape[1]
    hot = (lax.broadcasted_iota(jnp.int32, (cells, count), 0) == keys[...]).astype(jnp.bfloat16)
    lanes = lax.broadcasted_iota(jnp.int32, (width, count), 0) == places[...]
    for moment in range(STEPS):
        value = jnp.where(lanes, residual[moment : moment + 1, :], 0.0)
        high = value.astype(jnp.bfloat16)
        left = value - high.astype(F32)
        middle = left.astype(jnp.bfloat16)
        low = (left - middle.astype(F32)).astype(jnp.bfloat16)
        pieces = [
            lax.dot_general(hot, piece, (((1,), (1,)), ((), ())), preferred_element_type=F32)
            for piece in (low, middle, high)
        ]
        out[moment] = (pieces[0] + pieces[1]) + pieces[2]


def local_kernel(
    moment, cell, wavelet, wave, wave_old, prod, adj, adj_old, courant, injected, o_lap, o_wave, o_adj, o_prod
):
    rows, across, width = adj.shape
    zero_pads(o_wave)
    zero_pads(o_prod)
    for row in range(rows):
        for start in range(0, across, CHUNK):
            part = (row, pl.ds(start, CHUNK), slice(None))
            wide = (row, pl.ds(PAD + start, CHUNK), slice(None))
            lap = laplace_chunk(wave, row, start, CHUNK)
            o_lap[part] = lap
            o_wave[wide] = 2.0 * wave[wide] - wave_old[wide] + courant[part] * lap
            new = 2.0 * adj[part] - adj_old[part] + laplace_chunk(prod, row, start, CHUNK)
            new = new + injected[STEPS - 1 - moment, row * across + start : row * across + start + CHUNK, :]
            o_adj[part] = new
            o_prod[wide] = courant[part] * new
    inside, row, place, lane = split_cell(cell[0], rows, across, width)

    @pl.when(inside)
    def _():
        spot = (row, pl.ds(PAD + place, 1), slice(None))
        o_wave[spot] = o_wave[spot] + jnp.where(lane_ids(width) == lane, wavelet[0, moment], 0.0)


def halo_terms(core_ref, chip_ref, field, rows):
    base = field * REACH
    for place in range(REACH):
        chip_term = core_term = None
        for reach in range(place + 1, REACH + 1):
            one = coefficients[reach] * chip_ref[base + reach - place - 1]
            two = coefficients[reach] * core_ref[base + REACH - reach + place]
            chip_term = one if chip_term is None else chip_term + one
            core_term = two if core_term is None else core_term + two
        yield place, chip_term
        yield rows - 1 - place, core_term


def join_kernel(
    from_core, from_chip, courant, lap, wave, adj, prod, o_lap, o_wave, o_adj, o_prod, to_core, to_chip
):
    rows, across, width = adj.shape
    inner = slice(PAD, PAD + across)

    def send(row, field, value):
        if row < REACH:
            to_chip[field * REACH + row] = value
        else:
            to_core[field * REACH + row - (rows - REACH)] = value

    for row, term in halo_terms(from_core, from_chip, 0, rows):
        o_lap[row] = lap[row] + term
        new = wave[row, inner, :] + courant[row] * term
        o_wave[row, inner, :] = new
        send(row, 0, new)
    for row, term in halo_terms(from_core, from_chip, 1, rows):
        new = adj[row] + term
        o_adj[row] = new
        new = courant[row] * new
        o_prod[row, inner, :] = new
        send(row, 1, new)


def last_local_kernel(
    scale, wave, prod, adj, adj_old, injected, lap1, lap2, lap3, adj4, adj3, o_inner, o_part, o_lap, o_adj
):
    rows, across, width = adj.shape
    for row in range(rows):
        inner = REACH <= row < rows - REACH
        place = row - REACH if inner else (row if row < REACH else row - (rows - 2 * REACH))
        for start in range(0, across, CHUNK):
            part = (row, pl.ds(start, CHUNK), slice(None))
            put = (place, pl.ds(start, CHUNK), slice(None))
            lap = laplace_chunk(wave, row, start, CHUNK)
            new = 2.0 * adj[part] - adj_old[part] + laplace_chunk(prod, row, start, CHUNK)
            new = new + injected[0, row * across + start : row * across + start + CHUNK, :]
            known = adj[part] * lap2[part] + adj3[part] * lap3[part]
            if inner:
                o_inner[put] = scale * (known + adj4[part] * lap + new * lap1[part])
            else:
                o_part[put] = known
                o_lap[put] = lap
                o_adj[put] = new


def last_join_kernel(scale, from_core, from_chip, known, lap, adj, lap1, adj4, o_outer):
    rows = lap1.shape[0]

    def place(row):
        return row if row < REACH else row - (rows - 2 * REACH)

    waves = dict(halo_terms(from_core, from_chip, 0, rows))
    adjs = dict(halo_terms(from_core, from_chip, 1, rows))
    for row in waves:
        at = place(row)
        last_lap = lap[at] + waves[row]
        last_adj = adj[at] + adjs[row]
        o_outer[at] = scale * (known[at] + adj4[row] * last_lap + last_adj * lap1[row])


def fold(value):
    total = value[:8]
    for start in range(8, value.shape[0], 8):
        total = total + value[start : start + 8]
    return total


PRODUCTS = [(0, a, 1, b) for a in range(PAIRS) for b in range(a, PAIRS)] + [
    (1, a, 1, b) for a in range(PAIRS) for b in range(a, PAIRS)
]
SLOT = {key: PRODUCTS.index(key) for key in PRODUCTS}
FIRST_DOT = len(PRODUCTS)


def gram_kernel(history, out):
    pairs, rows, piece = history.shape[1], history.shape[2], history.shape[3]
    width = history.shape[4]
    for group in range(0, len(PRODUCTS), 10):
        members = PRODUCTS[group : group + 10]

        def body(row, sums, members=members):
            new = list(sums)
            for start in range(0, piece, 8):
                part = {}
                for a, i, b, j in members:
                    for key in ((a, i), (b, j)):
                        if key not in part:
                            part[key] = history[key[0], key[1], row, start : start + 8, :]
                for n, (a, i, b, j) in enumerate(members):
                    new[n] = new[n] + part[a, i] * part[b, j]
            return tuple(new)

        sums = lax.fori_loop(0, rows, body, tuple(jnp.zeros((8, width), F32) for _ in members))
        for n in range(len(members)):
            out[group + n] = sums[n]


def gradient_dots(rows_of, grad, pieces, sums):
    rows = pieces[0].shape[2]
    piece = pieces[0].shape[3]
    count = len(pieces)
    odd = odd_depth()
    for place, row in enumerate(rows_of):
        source = natural_row(row, rows, odd)
        for turn, ref in enumerate(pieces):
            offset = lax.rem(lax.axis_index("shot") + turn, count) * piece
            value = grad[place, pl.ds(pl.multiple_of(offset, piece), piece), :]
            for kind in range(2):
                for pair in range(PAIRS):
                    n = kind * PAIRS + pair
                    sums[n] = sums[n] + fold(ref[kind, pair, source] * value)
    return sums


def inner_rows(rows):
    return list(range(REACH, rows - REACH))


def outer_rows(rows):
    return list(range(REACH)) + list(range(rows - REACH, rows))


def inner_dots_kernel(count, grad, *refs):
    pieces, out = refs[:count], refs[count]
    sums = [jnp.zeros((8, grad.shape[2]), F32) for _ in range(2 * PAIRS)]
    sums = gradient_dots(inner_rows(pieces[0].shape[2]), grad, pieces, sums)
    for n in range(2 * PAIRS):
        out[n] = sums[n]


def outer_dots_kernel(count, grad, inner, gram, *refs):
    pieces, out = refs[:count], refs[count]
    sums = [inner[n] for n in range(2 * PAIRS)]
    sums = gradient_dots(outer_rows(pieces[0].shape[2]), grad, pieces, sums)
    lane = lane_ids(out.shape[1])
    line = jnp.zeros((1, out.shape[1]), F32)
    for n in range(FIRST_DOT + 2 * PAIRS):
        value = gram[n] if n < FIRST_DOT else sums[n - FIRST_DOT]
        line = line + jnp.where(lane == n, jnp.sum(value, axis=(0, 1), keepdims=True), 0.0)
    out[...] = jnp.broadcast_to(line, out.shape)


def weights(line):
    lane = lane_ids(line.shape[1])

    def number(n):
        return jnp.sum(jnp.where(lane == n, line, 0.0), axis=(0, 1), keepdims=True)

    values = [number(n) for n in range(FIRST_DOT + 2 * PAIRS)]

    def sy(a, b):
        return values[SLOT[0, a, 1, b]]

    def yy(a, b):
        return values[SLOT[1, min(a, b), 1, max(a, b)]]

    s_grad = values[FIRST_DOT : FIRST_DOT + PAIRS]
    y_grad = values[FIRST_DOT + PAIRS :]
    rho = [1.0 / sy(i, i) for i in range(PAIRS)]
    alpha = [None] * PAIRS
    for i in reversed(range(PAIRS)):
        dot = s_grad[i]
        for j in range(PAIRS - 1, i, -1):
            dot = dot - alpha[j] * sy(i, j)
        alpha[i] = rho[i] * dot
    scale = sy(PAIRS - 1, PAIRS - 1) / yy(PAIRS - 1, PAIRS - 1)
    s_weight = [None] * PAIRS
    for i in range(PAIRS):
        dot = y_grad[i]
        for j in range(PAIRS):
            dot = dot - alpha[j] * yy(i, j)
        dot = scale * dot
        for j in range(i):
            dot = dot + s_weight[j] * sy(j, i)
        s_weight[i] = alpha[i] - rho[i] * dot
    return scale, [-(scale * a) for a in alpha], s_weight


def finish_kernel(count, lines, courant, inner, outer, *refs):
    others = refs[: 2 * (count - 1)]
    pieces = refs[2 * (count - 1) : 2 * (count - 1) + count]
    o_grad, o_direction, o_next = refs[2 * (count - 1) + count :]
    rows, across, width = courant.shape
    piece = across // count
    odd = odd_depth()
    total = lines[0:8]
    for start in range(8, lines.shape[0], 8):
        total = total + lines[start : start + 8]
    scale, y_weight, s_weight = weights(jnp.sum(total, axis=0, keepdims=True))
    wide = [jnp.broadcast_to(v, (8, width)) for v in [scale] + s_weight + y_weight]
    inner_list, outer_list = inner_rows(rows), outer_rows(rows)
    for row in range(rows):
        source = natural_row(row, rows, odd)
        half = 0 if row in inner_list else 1
        place = (inner_list if half == 0 else outer_list).index(row)
        for turn, ref in enumerate(pieces):
            offset = lax.rem(lax.axis_index("shot") + turn, count) * piece
            for start in range(0, piece, 8):
                at = pl.ds(pl.multiple_of(offset + start, 8), 8)
                grad = (inner if half == 0 else outer)[place, at, :]
                for other in range(count - 1):
                    grad = grad + others[2 * other + half][place, at, :]
                move = wide[0] * grad
                for pair in range(PAIRS):
                    move = move + wide[1 + pair] * ref[0, pair, source, start : start + 8, :]
                    move = move + wide[1 + PAIRS + pair] * ref[1, pair, source, start : start + 8, :]
                move = -move
                if turn == 0:
                    o_grad[source, start : start + 8, :] = grad
                    o_direction[source, start : start + 8, :] = move
                o_next[source, at, :] = courant[source, at, :] + 0.05 * move


def call(kernel, name, outs, *args, specs=None, aliases=None, cost=1 << 20):
    return pl.pallas_call(
        kernel,
        name=name,
        out_shape=outs,
        in_specs=specs or [VM] * len(args),
        out_specs=jax.tree.map(lambda _: VM, outs),
        input_output_aliases=aliases or {},
        compiler_params=PARAMS,
        cost_estimate=pl.CostEstimate(flops=cost, bytes_accessed=cost, transcendentals=0),
    )(*args)


def per_device(
    courant,
    wave_before,
    wave_current,
    adjoint_after,
    adjoint_current,
    source_cell,
    wavelet,
    receiver_cell,
    residual,
    history,
):
    rows, across, width = courant.shape
    depths = lax.axis_size("depth")
    shots = lax.axis_size("shot")
    devices = depths * shots
    slab = shape(rows, across, width)
    padded = shape(rows, across + 2 * PAD, width)
    halo = shape(2 * REACH, across, width)
    on_chip = [(i, i ^ 1) for i in range(depths)]
    off_chip = [(i, i + 1 if i % 2 else i - 1) for i in range(1, depths - 1)]

    def exchange(to_core, to_chip):
        return lax.ppermute(to_core, "depth", on_chip), lax.ppermute(to_chip, "depth", off_chip)

    def to_shot(value, turn):
        return lax.ppermute(value, "shot", [((i + turn) % shots, i) for i in range(shots)])

    wave_old, wave = wave_before[0], wave_current[0]
    adj_old, adj = adjoint_after[0], adjoint_current[0]
    to_core, to_chip = call(first_send_kernel, "first_send", [halo, halo], wave, adj, courant)
    halos = exchange(to_core, to_chip)
    pieces = [history] + [to_shot(history, turn) for turn in range(1, shots)]
    wave, wave_old, adj, adj_old, cour, prod = call(
        prepare_kernel,
        "prepare",
        [padded, padded, slab, slab, slab, padded],
        wave,
        wave_old,
        adj,
        adj_old,
        courant,
    )
    inside, row, place, lane = split_cell(receiver_cell, rows, across, width)
    keys = jnp.where(inside, row * across + place, -1)
    injected = call(
        receiver_kernel, "receivers", shape(STEPS, rows * across, width), keys, lane, residual[0]
    )
    gram = call(gram_kernel, "gram", shape(len(PRODUCTS), 8, width), history)

    laps, adjs = [], []
    for moment in range(STEPS - 1):
        lap, new_wave, new_adj, new_prod = call(
            functools.partial(local_kernel, moment),
            f"local_{moment}",
            [slab, padded, slab, padded],
            source_cell,
            wavelet,
            wave,
            wave_old,
            prod,
            adj,
            adj_old,
            cour,
            injected,
            specs=[SM, SM] + [VM] * 7,
        )
        lap, new_wave, new_adj, new_prod, to_core, to_chip = call(
            join_kernel,
            f"join_{moment}",
            [slab, padded, slab, padded, halo, halo],
            *halos,
            cour,
            lap,
            new_wave,
            new_adj,
            new_prod,
            aliases={3: 0, 4: 1, 5: 2, 6: 3},
        )
        halos = exchange(to_core, to_chip)
        laps.append(lap)
        adjs.append(new_adj)
        wave_old, wave = wave, new_wave
        adj_old, adj = adj, new_adj
        prod = new_prod

    scale = 1.0 / (shots * STEPS)
    part = shape(rows - 2 * REACH, across, width)
    outer_part = shape(2 * REACH, across, width)
    inner, known, lap, last = call(
        functools.partial(last_local_kernel, scale),
        "last_local",
        [part, outer_part, outer_part, outer_part],
        wave,
        prod,
        adj,
        adj_old,
        injected,
        laps[0],
        laps[1],
        laps[2],
        adjs[0],
        adjs[1],
    )
    inner_others = [to_shot(inner, turn) for turn in range(1, shots)]
    inner_dots = call(
        functools.partial(inner_dots_kernel, shots),
        "inner_dots",
        shape(2 * PAIRS, 8, width),
        inner,
        *pieces,
    )
    outer = call(
        functools.partial(last_join_kernel, scale),
        "last_join",
        outer_part,
        *halos,
        known,
        lap,
        last,
        laps[0],
        adjs[0],
    )
    outer_others = [to_shot(outer, turn) for turn in range(1, shots)]
    line = call(
        functools.partial(outer_dots_kernel, shots),
        "outer_dots",
        shape(devices, 128),
        outer,
        inner_dots,
        gram,
        *pieces,
    )
    lines = lax.all_to_all(line, ("depth", "shot"), 0, 0, tiled=True)
    others = [value for pair in zip(inner_others, outer_others) for value in pair]
    own = shape(rows, across // shots, width)
    return tuple(
        call(
            functools.partial(finish_kernel, shots),
            "finish",
            [own, own, slab],
            lines,
            courant,
            inner,
            outer,
            *others,
            *pieces,
        )
    )


def solution(mesh):
    return jax.shard_map(
        per_device,
        mesh=mesh,
        in_specs=(
            P("depth", None, None),
            P("shot", "depth", None, None),
            P("shot", "depth", None, None),
            P("shot", "depth", None, None),
            P("shot", "depth", None, None),
            P("shot"),
            P("shot", None),
            P("shot", None),
            P("shot", None, None),
            P(None, None, "depth", "shot", None),
        ),
        out_specs=(P("depth", "shot", None), P("depth", "shot", None), P("depth", None, None)),
        check_vma=False,
    )
```

```python
import functools

import jax
import jax.numpy as jnp
from jax import lax
from jax.experimental import pallas as pl
from jax.experimental.pallas import tpu as pltpu
from jax.sharding import PartitionSpec as P

STEPS = 4
PAIRS = 5
REACH = 4
PAD = 8
CHUNK = 16
coefficients = (-205.0 / 72.0, 8.0 / 5.0, -1.0 / 5.0, 8.0 / 315.0, -1.0 / 560.0)

F32 = jnp.float32
VM = pl.BlockSpec(memory_space=pltpu.VMEM)
SM = pl.BlockSpec(memory_space=pltpu.SMEM)
HB = pl.BlockSpec(memory_space=pltpu.HBM)
PARAMS = pltpu.CompilerParams(vmem_limit_bytes=16 << 20)


def shape(*dims):
    return jax.ShapeDtypeStruct(dims, F32)


def natural_row(row, rows, odd):
    return jnp.where(odd == 1, rows - 1 - row, row)


def odd_depth():
    return lax.rem(lax.axis_index("depth"), 2)


def lane_ids(width):
    return lax.broadcasted_iota(jnp.int32, (1, width), 1)


def laplace_chunk(ref, row, start, size):
    rows, width = ref.shape[0], ref.shape[2]
    core = ref[row, PAD + start : PAD + start + size, :]
    lane = lax.broadcasted_iota(jnp.int32, (size, width), 1)
    total = (3.0 * coefficients[0]) * core
    for reach in range(1, REACH + 1):
        near = (
            ref[row, PAD + start + reach : PAD + start + reach + size, :]
            + ref[row, PAD + start - reach : PAD + start - reach + size, :]
        )
        if row - reach >= 0:
            near = near + ref[row - reach, PAD + start : PAD + start + size, :]
        if row + reach < rows:
            near = near + ref[row + reach, PAD + start : PAD + start + size, :]
        near = near + jnp.where(lane >= reach, pltpu.roll(core, reach, 1), 0.0)
        near = near + jnp.where(lane < width - reach, pltpu.roll(core, width - reach, 1), 0.0)
        total = total + coefficients[reach] * near
    return total


def zero_pads(ref):
    rows, padded, width = ref.shape
    for row in range(rows):
        ref[row, :PAD, :] = jnp.zeros((PAD, width), F32)
        ref[row, padded - PAD :, :] = jnp.zeros((PAD, width), F32)


def stage_kernel(
    wave,
    wave_old,
    adjoint,
    adjoint_old,
    courant,
    history,
    o_wave,
    o_wave_old,
    o_adj,
    o_adj_old,
    o_cour,
    o_prod,
    to_core,
    to_chip,
    o_history,
    b_wave,
    b_wave_old,
    b_adj,
    b_adj_old,
    b_cour,
    sems,
):
    rows, across, width = courant.shape
    fetched = [(wave, b_wave), (adjoint, b_adj), (courant, b_cour), (wave_old, b_wave_old), (adjoint_old, b_adj_old)]
    copies = [pltpu.make_async_copy(src, dst, sems.at[n]) for n, (src, dst) in enumerate(fetched)]
    for n, (start, at) in enumerate([(0, 0), (rows - REACH, REACH)]):
        src = history.at[:, :, pl.ds(start, REACH)]
        copies.append(pltpu.make_async_copy(src, o_history.at[:, :, pl.ds(at, REACH)], sems.at[len(fetched) + n]))
    for copy in copies:
        copy.start()
    zero_pads(o_wave)
    zero_pads(o_wave_old)
    zero_pads(o_prod)
    odd = odd_depth()
    for copy in copies[:3]:
        copy.wait()
    for row in range(rows):
        src = natural_row(row, rows, odd)
        now, adj, cour = b_wave[src], b_adj[src], b_cour[src]
        prod = cour * adj
        o_wave[row, PAD : PAD + across, :] = now
        o_adj[row] = adj
        o_cour[row] = cour
        o_prod[row, PAD : PAD + across, :] = prod
        if row < REACH:
            to_chip[row] = now
            to_chip[REACH + row] = prod
        if row >= rows - REACH:
            to_core[row - (rows - REACH)] = now
            to_core[row - (rows - REACH) + REACH] = prod
    for copy in copies[3:5]:
        copy.wait()
    for row in range(rows):
        src = natural_row(row, rows, odd)
        o_wave_old[row, PAD : PAD + across, :] = b_wave_old[src]
        o_adj_old[row] = b_adj_old[src]
    for copy in copies[5:]:
        copy.wait()


def split_cell(cell, rows, across, width):
    depth_row = cell // (across * width) - lax.axis_index("depth") * rows
    rest = cell % (across * width)
    inside = (depth_row >= 0) & (depth_row < rows)
    row = jnp.where(odd_depth() == 1, rows - 1 - depth_row, depth_row)
    return inside, row, rest // width, rest % width


def receiver_kernel(across, receivers, residual, out):
    cells = out.shape[1]
    width = out.shape[2]
    count = receivers.shape[1]
    inside, row, place, lane = split_cell(receivers[...], cells // across, across, width)
    keys = jnp.where(inside, row * across + place, -1)
    hot = (lax.broadcasted_iota(jnp.int32, (cells, count), 0) == keys).astype(jnp.bfloat16)
    lanes = lax.broadcasted_iota(jnp.int32, (width, count), 0) == lane
    for moment in range(STEPS):
        value = jnp.where(lanes, residual[moment : moment + 1, :], 0.0)
        high = value.astype(jnp.bfloat16)
        left = value - high.astype(F32)
        middle = left.astype(jnp.bfloat16)
        low = (left - middle.astype(F32)).astype(jnp.bfloat16)
        pieces = [
            lax.dot_general(hot, piece, (((1,), (1,)), ((), ())), preferred_element_type=F32)
            for piece in (low, middle, high)
        ]
        out[moment] = (pieces[0] + pieces[1]) + pieces[2]


def local_kernel(
    moment, cell, wavelet, wave, wave_old, prod, adj, adj_old, courant, injected, o_lap, o_wave, o_adj, o_prod
):
    rows, across, width = adj.shape
    zero_pads(o_wave)
    zero_pads(o_prod)
    for row in range(rows):
        for start in range(0, across, CHUNK):
            part = (row, pl.ds(start, CHUNK), slice(None))
            wide = (row, pl.ds(PAD + start, CHUNK), slice(None))
            lap = laplace_chunk(wave, row, start, CHUNK)
            o_lap[part] = lap
            o_wave[wide] = 2.0 * wave[wide] - wave_old[wide] + courant[part] * lap
            new = 2.0 * adj[part] - adj_old[part] + laplace_chunk(prod, row, start, CHUNK)
            new = new + injected[STEPS - 1 - moment, row * across + start : row * across + start + CHUNK, :]
            o_adj[part] = new
            o_prod[wide] = courant[part] * new
    inside, row, place, lane = split_cell(cell[0], rows, across, width)

    @pl.when(inside)
    def _():
        spot = (row, pl.ds(PAD + place, 1), slice(None))
        o_wave[spot] = o_wave[spot] + jnp.where(lane_ids(width) == lane, wavelet[0, moment], 0.0)


def chip_terms(ref, field):
    for place in range(REACH):
        term = None
        for reach in range(place + 1, REACH + 1):
            one = coefficients[reach] * ref[field * REACH + reach - place - 1]
            term = one if term is None else term + one
        yield place, term


def core_terms(ref, field, rows):
    for place in range(REACH):
        term = None
        for reach in range(place + 1, REACH + 1):
            one = coefficients[reach] * ref[field * REACH + REACH - reach + place]
            term = one if term is None else term + one
        yield rows - 1 - place, term


def join_kernel(chip, halo, courant, lap, wave, adj, prod, o_lap, o_wave, o_adj, o_prod, send):
    rows, across, width = adj.shape
    inner = slice(PAD, PAD + across)
    first = 0 if chip else rows - REACH
    for row, term in chip_terms(halo, 0) if chip else core_terms(halo, 0, rows):
        o_lap[row] = lap[row] + term
        new = wave[row, inner, :] + courant[row] * term
        o_wave[row, inner, :] = new
        send[row - first] = new
    for row, term in chip_terms(halo, 1) if chip else core_terms(halo, 1, rows):
        new = adj[row] + term
        o_adj[row] = new
        new = courant[row] * new
        o_prod[row, inner, :] = new
        send[REACH + row - first] = new


def last_rows(which, wave, prod, adj, adj_old, injected, extra_lap=None, extra_adj=None):
    across = adj.shape[1]
    for place, row in enumerate(which):
        for start in range(0, across, CHUNK):
            part = (row, pl.ds(start, CHUNK), slice(None))
            lap = laplace_chunk(wave, row, start, CHUNK)
            new = 2.0 * adj[part] - adj_old[part] + laplace_chunk(prod, row, start, CHUNK)
            new = new + injected[0, row * across + start : row * across + start + CHUNK, :]
            if extra_lap is not None and row in extra_lap:
                lap = lap + extra_lap[row][start : start + CHUNK]
                new = new + extra_adj[row][start : start + CHUNK]
            yield place, row, start, part, lap, new


def inner_kernel(
    scale, count, wave, prod, adj, adj_old, injected, lap1, lap2, lap3, adj4, adj3, *outs
):
    rows, across, width = adj.shape
    piece = across // count
    which = inner_rows(rows)
    full = outs[count]
    for place, row, start, part, lap, new in last_rows(which, wave, prod, adj, adj_old, injected):
        known = adj[part] * lap2[part] + adj3[part] * lap3[part]
        full[place, start : start + CHUNK, :] = scale * (known + adj4[part] * lap + new * lap1[part])
    for turn in range(count):
        offset = lax.rem(lax.axis_index("shot") + turn, count) * piece
        for place in range(len(which)):
            outs[turn][place] = full[place, pl.ds(pl.multiple_of(offset, 8), piece), :]


def outer_kernel(
    scale, from_core, wave, prod, adj, adj_old, injected, lap1, lap2, lap3, adj4, adj3, o_grad, o_lap, o_adj
):
    rows = adj.shape[0]
    waves = dict(core_terms(from_core, 0, rows))
    adjs = dict(core_terms(from_core, 1, rows))
    which = outer_rows(rows)
    for place, row, start, part, lap, new in last_rows(which, wave, prod, adj, adj_old, injected, waves, adjs):
        put = (place, pl.ds(start, CHUNK), slice(None))
        known = adj[part] * lap2[part] + adj3[part] * lap3[part]
        if row < REACH:
            o_grad[put] = known
            o_lap[put] = lap
            o_adj[put] = new
        else:
            o_grad[put] = scale * (known + adj4[part] * lap + new * lap1[part])


def last_join_kernel(scale, from_chip, grad, lap, adj, lap1, adj4, o_grad):
    waves = dict(chip_terms(from_chip, 0))
    adjs = dict(chip_terms(from_chip, 1))
    for row in range(REACH):
        last_lap = lap[row] + waves[row]
        last_adj = adj[row] + adjs[row]
        o_grad[row] = scale * (grad[row] + adj4[row] * last_lap + last_adj * lap1[row])


def fold(value):
    total = value[:8]
    for start in range(8, value.shape[0], 8):
        total = total + value[start : start + 8]
    return total


PRODUCTS = [(0, a, 1, b) for a in range(PAIRS) for b in range(a, PAIRS)] + [
    (1, a, 1, b) for a in range(PAIRS) for b in range(a, PAIRS)
]
SLOT = {key: PRODUCTS.index(key) for key in PRODUCTS}
FIRST_DOT = len(PRODUCTS)


def gram_kernel(history, out):
    pairs, rows, piece = history.shape[1], history.shape[2], history.shape[3]
    width = history.shape[4]
    for group in range(0, len(PRODUCTS), 10):
        members = PRODUCTS[group : group + 10]

        def body(row, sums, members=members):
            new = list(sums)
            for start in range(0, piece, 8):
                part = {}
                for a, i, b, j in members:
                    for key in ((a, i), (b, j)):
                        if key not in part:
                            part[key] = history[key[0], key[1], row, start : start + 8, :]
                for n, (a, i, b, j) in enumerate(members):
                    new[n] = new[n] + part[a, i] * part[b, j]
            return tuple(new)

        sums = lax.fori_loop(0, rows, body, tuple(jnp.zeros((8, width), F32) for _ in members))
        for n in range(len(members)):
            out[group + n] = sums[n]


def inner_rows(rows):
    return list(range(REACH, rows - REACH))


def outer_rows(rows):
    return list(range(REACH)) + list(range(rows - REACH, rows))


def add_dots(sums, values, history, row):
    for kind in range(2):
        for pair in range(PAIRS):
            n = kind * PAIRS + pair
            sums[n] = sums[n] + fold(history[kind, pair, row] * values)


def outer_dots_kernel(count, grad, *refs):
    pieces, out = refs[:count], refs[count]
    total, piece = grad.shape[0], pieces[0].shape[3]
    odd = odd_depth()
    sums = [jnp.zeros((8, grad.shape[2]), F32) for _ in range(2 * PAIRS)]
    for place in range(total):
        source = natural_row(place, total, odd)
        for turn, ref in enumerate(pieces):
            offset = lax.rem(lax.axis_index("shot") + turn, count) * piece
            values = grad[place, pl.ds(pl.multiple_of(offset, 8), piece), :]
            add_dots(sums, values, ref, source)
    for n in range(2 * PAIRS):
        out[n] = sums[n]


def line_kernel(outer, gram, history, *refs):
    parts, out, o_inner = refs[:-2], refs[-2], refs[-1]
    rows = history.shape[2]
    odd = odd_depth()
    sums = [outer[n] for n in range(2 * PAIRS)]
    for place, row in enumerate(inner_rows(rows)):
        values = parts[0][place]
        for other in parts[1:]:
            values = values + other[place]
        o_inner[place] = values
        add_dots(sums, values, history, natural_row(row, rows, odd))
    lane = lane_ids(out.shape[1])
    line = jnp.zeros((1, out.shape[1]), F32)
    for n in range(FIRST_DOT + 2 * PAIRS):
        value = gram[n] if n < FIRST_DOT else sums[n - FIRST_DOT]
        line = line + jnp.where(lane == n, jnp.sum(value, axis=(0, 1), keepdims=True), 0.0)
    out[...] = jnp.broadcast_to(line, out.shape)


def weights(line):
    lane = lane_ids(line.shape[1])

    def number(n):
        return jnp.sum(jnp.where(lane == n, line, 0.0), axis=(0, 1), keepdims=True)

    values = [number(n) for n in range(FIRST_DOT + 2 * PAIRS)]

    def sy(a, b):
        return values[SLOT[0, a, 1, b]]

    def yy(a, b):
        return values[SLOT[1, min(a, b), 1, max(a, b)]]

    s_grad = values[FIRST_DOT : FIRST_DOT + PAIRS]
    y_grad = values[FIRST_DOT + PAIRS :]
    rho = [1.0 / sy(i, i) for i in range(PAIRS)]
    alpha = [None] * PAIRS
    for i in reversed(range(PAIRS)):
        dot = s_grad[i]
        for j in range(PAIRS - 1, i, -1):
            dot = dot - alpha[j] * sy(i, j)
        alpha[i] = rho[i] * dot
    scale = sy(PAIRS - 1, PAIRS - 1) / yy(PAIRS - 1, PAIRS - 1)
    s_weight = [None] * PAIRS
    for i in range(PAIRS):
        dot = y_grad[i]
        for j in range(PAIRS):
            dot = dot - alpha[j] * yy(i, j)
        dot = scale * dot
        for j in range(i):
            dot = dot + s_weight[j] * sy(j, i)
        s_weight[i] = alpha[i] - rho[i] * dot
    return scale, [-(scale * a) for a in alpha], s_weight


def weights_kernel(lines, inner, history, o_weights, o_move):
    rows = history.shape[2]
    piece, width = inner.shape[1], inner.shape[2]
    odd = odd_depth()
    total = lines[0:8]
    for start in range(8, lines.shape[0], 8):
        total = total + lines[start : start + 8]
    scale, y_weight, s_weight = weights(jnp.sum(total, axis=0, keepdims=True))
    wide = [jnp.broadcast_to(v, (8, width)) for v in [scale] + s_weight + y_weight]
    for n, value in enumerate(wide):
        o_weights[n] = value
    for place, row in enumerate(inner_rows(rows)):
        source = natural_row(row, rows, odd)
        for start in range(0, piece, 8):
            at = slice(start, start + 8)
            o_move[place, at, :] = move_of(wide, inner[place, at, :], history, source, at)


def move_of(wide, grad, history, row, at):
    move = wide[0] * grad
    for pair in range(PAIRS):
        move = move + wide[1 + pair] * history[0, pair, row, at, :]
        move = move + wide[1 + PAIRS + pair] * history[1, pair, row, at, :]
    return -move


def finish_kernel(count, weight, courant, inner, inner_move, outer, *refs):
    others, pieces = refs[: count - 1], refs[count - 1 : 2 * count - 1]
    o_grad, o_direction, o_next = refs[2 * count - 1 :]
    rows, across, width = courant.shape
    piece = across // count
    odd = odd_depth()
    wide = [weight[n] for n in range(1 + 2 * PAIRS)]
    mine = lax.axis_index("shot") * piece
    for place, row in enumerate(inner_rows(rows)):
        source = natural_row(row, rows, odd)
        at = pl.ds(pl.multiple_of(mine, 8), piece)
        o_grad[source] = inner[place]
        o_direction[source] = inner_move[place]
        o_next[source, at, :] = courant[source, at, :] + 0.05 * inner_move[place]
    outer_list = outer_rows(rows)
    for place, row in enumerate(outer_list):
        source = natural_row(row, rows, odd)
        kept = natural_row(place, len(outer_list), odd)
        for turn, ref in enumerate(pieces):
            offset = lax.rem(lax.axis_index("shot") + turn, count) * piece
            for start in range(0, piece, 8):
                at = pl.ds(pl.multiple_of(offset + start, 8), 8)
                grad = outer[place, at, :]
                for other in others:
                    grad = grad + other[place, at, :]
                move = move_of(wide, grad, ref, kept, slice(start, start + 8))
                if turn == 0:
                    o_grad[source, start : start + 8, :] = grad
                    o_direction[source, start : start + 8, :] = move
                o_next[source, at, :] = courant[source, at, :] + 0.05 * move


def last_piece_kernel(count, courant, done, *refs):
    moves, o_next, buffer, sem = refs[: count - 1], refs[-3], refs[-2], refs[-1]
    rows, across, width = courant.shape
    piece = across // count
    odd = odd_depth()
    first = REACH
    copies = []
    for turn in range(1, count):
        offset = pl.multiple_of(lax.rem(lax.axis_index("shot") + turn, count) * piece, 8)
        for place, row in enumerate(inner_rows(rows)):
            source = natural_row(row, rows, odd)
            value = courant[source, pl.ds(offset, piece), :] + 0.05 * moves[turn - 1][place]
            buffer[turn - 1, source - first] = value
        copies.append(
            pltpu.make_async_copy(
                buffer.at[turn - 1],
                o_next.at[pl.ds(first, rows - 2 * REACH), pl.ds(offset, piece)],
                sem.at[turn - 1],
            )
        )
        copies[-1].start()
    for copy in copies:
        copy.wait()


def call(
    kernel, name, outs, *args, specs=None, out_specs=None, aliases=None, scratch=(), cost=1 << 20
):
    return pl.pallas_call(
        kernel,
        name=name,
        out_shape=outs,
        in_specs=specs or [VM] * len(args),
        out_specs=out_specs or jax.tree.map(lambda _: VM, outs),
        input_output_aliases=aliases or {},
        scratch_shapes=list(scratch),
        compiler_params=PARAMS,
        cost_estimate=pl.CostEstimate(flops=cost, bytes_accessed=cost, transcendentals=0),
    )(*args)


def per_device(
    courant,
    wave_before,
    wave_current,
    adjoint_after,
    adjoint_current,
    source_cell,
    wavelet,
    receiver_cell,
    residual,
    history,
):
    rows, across, width = courant.shape
    depths = lax.axis_size("depth")
    shots = lax.axis_size("shot")
    devices = depths * shots
    piece = across // shots
    slab = shape(rows, across, width)
    padded = shape(rows, across + 2 * PAD, width)
    halo = shape(2 * REACH, across, width)
    on_chip = [(i, i ^ 1) for i in range(depths)]
    off_chip = [(i, i + 1 if i % 2 else i - 1) for i in range(1, depths - 1)]

    def swap_core(value):
        return lax.ppermute(value, "depth", on_chip)

    def swap_chip(value):
        return lax.ppermute(value, "depth", off_chip)

    def from_shot(value, turn):
        return lax.ppermute(value, "shot", [((i + turn) % shots, i) for i in range(shots)])

    block = pltpu.VMEM((rows, across, width), F32)
    wave, wave_old, adj, adj_old, cour, prod, to_core, to_chip, kept = call(
        stage_kernel,
        "stage",
        [padded, padded, slab, slab, slab, padded, halo, halo, shape(2, PAIRS, 2 * REACH, piece, width)],
        wave_current[0],
        wave_before[0],
        adjoint_current[0],
        adjoint_after[0],
        courant,
        history,
        specs=[HB] * 6,
        scratch=[block] * 5 + [pltpu.SemaphoreType.DMA((7,))],
    )
    from_chip = swap_chip(to_chip)
    from_core = swap_core(to_core)
    kept = [kept] + [from_shot(kept, turn) for turn in range(1, shots)]
    injected = call(
        functools.partial(receiver_kernel, across),
        "receivers",
        shape(STEPS, rows * across, width),
        receiver_cell,
        residual[0],
    )

    laps, adjs = [], []
    for moment in range(STEPS - 1):
        lap, new_wave, new_adj, new_prod = call(
            functools.partial(local_kernel, moment),
            f"local_{moment}",
            [slab, padded, slab, padded],
            source_cell,
            wavelet,
            wave,
            wave_old,
            prod,
            adj,
            adj_old,
            cour,
            injected,
            specs=[SM, SM] + [VM] * 7,
        )
        sends = []
        for chip, came in ((False, from_core), (True, from_chip)):
            lap, new_wave, new_adj, new_prod, send = call(
                functools.partial(join_kernel, chip),
                f"join_{'chip' if chip else 'core'}_{moment}",
                [slab, padded, slab, padded, halo],
                came,
                cour,
                lap,
                new_wave,
                new_adj,
                new_prod,
                aliases={2: 0, 3: 1, 4: 2, 5: 3},
            )
            sends.append(send)
        from_core = swap_core(sends[0])
        from_chip = swap_chip(sends[1])
        laps.append(lap)
        adjs.append(new_adj)
        wave_old, wave = wave, new_wave
        adj_old, adj = adj, new_adj
        prod = new_prod

    scale = 1.0 / (shots * STEPS)
    inner_count = rows - 2 * REACH
    last = (wave, prod, adj, adj_old, injected, laps[0], laps[1], laps[2], adjs[0], adjs[1])
    mine = shape(inner_count, piece, width)
    inner = call(
        functools.partial(inner_kernel, scale, shots),
        "inner",
        [mine] * shots,
        *last,
        scratch=[pltpu.VMEM((inner_count, across, width), F32)],
    )
    parts = [inner[0]] + [from_shot(inner[shots - turn], turn) for turn in range(1, shots)]
    gram = call(gram_kernel, "gram", shape(len(PRODUCTS), 8, width), history)
    outer_part = shape(2 * REACH, across, width)
    chip_part = shape(REACH, across, width)
    outer, lap, new_adj = call(
        functools.partial(outer_kernel, scale),
        "outer",
        [outer_part, chip_part, chip_part],
        from_core,
        *last,
    )
    outer = call(
        functools.partial(last_join_kernel, scale),
        "last_join",
        outer_part,
        from_chip,
        outer,
        lap,
        new_adj,
        laps[0],
        adjs[0],
        aliases={1: 0},
    )
    others = [from_shot(outer, turn) for turn in range(1, shots)]
    outer_dots = call(
        functools.partial(outer_dots_kernel, shots),
        "outer_dots",
        shape(2 * PAIRS, 8, width),
        outer,
        *kept,
    )
    line, inner_grad = call(
        line_kernel,
        "line",
        [shape(devices, 128), mine],
        outer_dots,
        gram,
        history,
        *parts,
    )
    lines = lax.all_to_all(line, ("depth", "shot"), 0, 0, tiled=True)
    weight, move = call(
        weights_kernel,
        "weights",
        [shape(1 + 2 * PAIRS, 8, width), mine],
        lines,
        inner_grad,
        history,
    )
    moves = [from_shot(move, turn) for turn in range(1, shots)]
    own = shape(rows, piece, width)
    gradient, direction, courant_next = call(
        functools.partial(finish_kernel, shots),
        "finish",
        [own, own, slab],
        weight,
        courant,
        inner_grad,
        move,
        outer,
        *others,
        *kept,
    )
    courant_next = call(
        functools.partial(last_piece_kernel, shots),
        "last_piece",
        slab,
        courant,
        courant_next,
        *moves,
        specs=[VM, HB] + [VM] * (shots - 1),
        out_specs=HB,
        aliases={1: 0},
        scratch=[
            pltpu.VMEM((shots - 1, inner_count, piece, width), F32),
            pltpu.SemaphoreType.DMA((shots - 1,)),
        ],
    )
    return gradient, direction, courant_next


def solution(mesh):
    return jax.shard_map(
        per_device,
        mesh=mesh,
        in_specs=(
            P("depth", None, None),
            P("shot", "depth", None, None),
            P("shot", "depth", None, None),
            P("shot", "depth", None, None),
            P("shot", "depth", None, None),
            P("shot"),
            P("shot", None),
            P("shot", None),
            P("shot", None, None),
            P(None, None, "depth", "shot", None),
        ),
        out_specs=(P("depth", "shot", None), P("depth", "shot", None), P("depth", None, None)),
        check_vma=False,
    )
```

```python
import functools

import jax
import jax.numpy as jnp
from jax import lax
from jax.experimental import pallas as pl
from jax.experimental.pallas import tpu as pltpu
from jax.sharding import PartitionSpec as P

STEPS = 4
PAIRS = 5
REACH = 4
PAD = 8
CHUNK = 16
coefficients = (-205.0 / 72.0, 8.0 / 5.0, -1.0 / 5.0, 8.0 / 315.0, -1.0 / 560.0)

F32 = jnp.float32
VM = pl.BlockSpec(memory_space=pltpu.VMEM)
SM = pl.BlockSpec(memory_space=pltpu.SMEM)
HB = pl.BlockSpec(memory_space=pltpu.HBM)
PARAMS = pltpu.CompilerParams(vmem_limit_bytes=16 << 20)


def in_hbm(value):
    return pltpu.with_memory_space_constraint(value, pltpu.HBM)


def shape(*dims):
    return jax.ShapeDtypeStruct(dims, F32)


def natural_row(row, rows, odd):
    return jnp.where(odd == 1, rows - 1 - row, row)


def odd_depth():
    return lax.rem(lax.axis_index("depth"), 2)


def lane_ids(width):
    return lax.broadcasted_iota(jnp.int32, (1, width), 1)


def laplace_chunk(ref, row, start, size):
    rows, width = ref.shape[0], ref.shape[2]
    core = ref[row, PAD + start : PAD + start + size, :]
    lane = lax.broadcasted_iota(jnp.int32, (size, width), 1)
    total = (3.0 * coefficients[0]) * core
    for reach in range(1, REACH + 1):
        near = (
            ref[row, PAD + start + reach : PAD + start + reach + size, :]
            + ref[row, PAD + start - reach : PAD + start - reach + size, :]
        )
        if row - reach >= 0:
            near = near + ref[row - reach, PAD + start : PAD + start + size, :]
        if row + reach < rows:
            near = near + ref[row + reach, PAD + start : PAD + start + size, :]
        near = near + jnp.where(lane >= reach, pltpu.roll(core, reach, 1), 0.0)
        near = near + jnp.where(lane < width - reach, pltpu.roll(core, width - reach, 1), 0.0)
        total = total + coefficients[reach] * near
    return total


def zero_pads(ref):
    rows, padded, width = ref.shape
    for row in range(rows):
        ref[row, :PAD, :] = jnp.zeros((PAD, width), F32)
        ref[row, padded - PAD :, :] = jnp.zeros((PAD, width), F32)


def stage_kernel(
    wave,
    wave_old,
    adjoint,
    adjoint_old,
    courant,
    o_wave,
    o_wave_old,
    o_adj,
    o_adj_old,
    o_cour,
    o_prod,
    to_core,
    to_chip,
    b_wave,
    b_wave_old,
    b_adj,
    b_adj_old,
    b_cour,
    sems,
):
    rows, across, width = courant.shape
    fetched = [(wave, b_wave), (adjoint, b_adj), (courant, b_cour), (wave_old, b_wave_old), (adjoint_old, b_adj_old)]
    copies = [pltpu.make_async_copy(src, dst, sems.at[n]) for n, (src, dst) in enumerate(fetched)]
    for copy in copies:
        copy.start()
    zero_pads(o_wave)
    zero_pads(o_wave_old)
    zero_pads(o_prod)
    odd = odd_depth()
    for copy in copies[:3]:
        copy.wait()
    for row in range(rows):
        src = natural_row(row, rows, odd)
        now, adj, cour = b_wave[src], b_adj[src], b_cour[src]
        prod = cour * adj
        o_wave[row, PAD : PAD + across, :] = now
        o_adj[row] = adj
        o_cour[row] = cour
        o_prod[row, PAD : PAD + across, :] = prod
        if row < REACH:
            to_chip[row] = now
            to_chip[REACH + row] = prod
        if row >= rows - REACH:
            to_core[row - (rows - REACH)] = now
            to_core[row - (rows - REACH) + REACH] = prod
    for copy in copies[3:]:
        copy.wait()
    for row in range(rows):
        src = natural_row(row, rows, odd)
        o_wave_old[row, PAD : PAD + across, :] = b_wave_old[src]
        o_adj_old[row] = b_adj_old[src]


def keep_kernel(history, _, out, sem):
    start = odd_depth() * (history.shape[2] - REACH)
    copy = pltpu.make_async_copy(history.at[:, :, pl.ds(start, REACH)], out, sem)
    copy.start()
    copy.wait()


def split_cell(cell, rows, across, width):
    depth_row = cell // (across * width) - lax.axis_index("depth") * rows
    rest = cell % (across * width)
    inside = (depth_row >= 0) & (depth_row < rows)
    row = jnp.where(odd_depth() == 1, rows - 1 - depth_row, depth_row)
    return inside, row, rest // width, rest % width


def receiver_kernel(across, receivers, residual, out):
    cells = out.shape[1]
    width = out.shape[2]
    count = receivers.shape[1]
    inside, row, place, lane = split_cell(receivers[...], cells // across, across, width)
    keys = jnp.where(inside, row * across + place, -1)
    hot = (lax.broadcasted_iota(jnp.int32, (cells, count), 0) == keys).astype(jnp.bfloat16)
    lanes = lax.broadcasted_iota(jnp.int32, (width, count), 0) == lane
    for moment in range(STEPS):
        value = jnp.where(lanes, residual[moment : moment + 1, :], 0.0)
        high = value.astype(jnp.bfloat16)
        left = value - high.astype(F32)
        middle = left.astype(jnp.bfloat16)
        low = (left - middle.astype(F32)).astype(jnp.bfloat16)
        pieces = [
            lax.dot_general(hot, piece, (((1,), (1,)), ((), ())), preferred_element_type=F32)
            for piece in (low, middle, high)
        ]
        out[moment] = (pieces[0] + pieces[1]) + pieces[2]


def local_kernel(
    moment, cell, wavelet, wave, wave_old, prod, adj, adj_old, courant, injected, *outs
):
    o_lap, o_wave, o_adj, o_prod = outs[-4:]
    rows, across, width = adj.shape
    zero_pads(o_wave)
    zero_pads(o_prod)
    for row in range(rows):
        for start in range(0, across, CHUNK):
            part = (row, pl.ds(start, CHUNK), slice(None))
            wide = (row, pl.ds(PAD + start, CHUNK), slice(None))
            lap = laplace_chunk(wave, row, start, CHUNK)
            o_lap[part] = lap
            o_wave[wide] = 2.0 * wave[wide] - wave_old[wide] + courant[part] * lap
            new = 2.0 * adj[part] - adj_old[part] + laplace_chunk(prod, row, start, CHUNK)
            new = new + injected[STEPS - 1 - moment, row * across + start : row * across + start + CHUNK, :]
            o_adj[part] = new
            o_prod[wide] = courant[part] * new
    inside, row, place, lane = split_cell(cell[0], rows, across, width)

    @pl.when(inside)
    def _():
        spot = (row, pl.ds(PAD + place, 1), slice(None))
        o_wave[spot] = o_wave[spot] + jnp.where(lane_ids(width) == lane, wavelet[0, moment], 0.0)


def chip_terms(ref, field):
    for place in range(REACH):
        term = None
        for reach in range(place + 1, REACH + 1):
            one = coefficients[reach] * ref[field * REACH + reach - place - 1]
            term = one if term is None else term + one
        yield place, term


def core_terms(ref, field, rows):
    for place in range(REACH):
        term = None
        for reach in range(place + 1, REACH + 1):
            one = coefficients[reach] * ref[field * REACH + REACH - reach + place]
            term = one if term is None else term + one
        yield rows - 1 - place, term


def join_kernel(chip, halo, courant, lap, wave, adj, prod, o_lap, o_wave, o_adj, o_prod, send):
    rows, across, width = adj.shape
    inner = slice(PAD, PAD + across)
    first = 0 if chip else rows - REACH
    for row, term in chip_terms(halo, 0) if chip else core_terms(halo, 0, rows):
        o_lap[row] = lap[row] + term
        new = wave[row, inner, :] + courant[row] * term
        o_wave[row, inner, :] = new
        send[row - first] = new
    for row, term in chip_terms(halo, 1) if chip else core_terms(halo, 1, rows):
        new = adj[row] + term
        o_adj[row] = new
        new = courant[row] * new
        o_prod[row, inner, :] = new
        send[REACH + row - first] = new


def last_rows(which, wave, prod, adj, adj_old, injected, extra_lap=None, extra_adj=None):
    across = adj.shape[1]
    for place, row in enumerate(which):
        for start in range(0, across, CHUNK):
            part = (row, pl.ds(start, CHUNK), slice(None))
            lap = laplace_chunk(wave, row, start, CHUNK)
            new = 2.0 * adj[part] - adj_old[part] + laplace_chunk(prod, row, start, CHUNK)
            new = new + injected[0, row * across + start : row * across + start + CHUNK, :]
            if extra_lap is not None and row in extra_lap:
                lap = lap + extra_lap[row][start : start + CHUNK]
                new = new + extra_adj[row][start : start + CHUNK]
            yield place, row, start, part, lap, new


def lay_pieces(full, outs):
    count = len(outs)
    piece = full.shape[1] // count
    for turn, out in enumerate(outs):
        offset = lax.rem(lax.axis_index("shot") + turn, count) * piece
        for place in range(full.shape[0]):
            out[place] = full[place, pl.ds(pl.multiple_of(offset, 8), piece), :]


def inner_kernel(scale, wave, prod, adj, adj_old, injected, lap1, lap2, lap3, adj4, adj3, *outs):
    full = outs[-1]
    which = inner_rows(adj.shape[0])
    for place, row, start, part, lap, new in last_rows(which, wave, prod, adj, adj_old, injected):
        known = adj[part] * lap2[part] + adj3[part] * lap3[part]
        full[place, start : start + CHUNK, :] = scale * (known + adj4[part] * lap + new * lap1[part])
    lay_pieces(full, outs[:-1])


def outer_kernel(
    scale, from_core, wave, prod, adj, adj_old, injected, lap1, lap2, lap3, adj4, adj3, o_known, o_lap, o_adj, *outs
):
    rows = adj.shape[0]
    full = outs[-1]
    waves = dict(core_terms(from_core, 0, rows))
    adjs = dict(core_terms(from_core, 1, rows))
    which = list(range(rows - REACH, rows)) + list(range(REACH))
    for place, row, start, part, lap, new in last_rows(which, wave, prod, adj, adj_old, injected, waves, adjs):
        known = adj[part] * lap2[part] + adj3[part] * lap3[part]
        if row < REACH:
            o_known[part] = known
            o_lap[part] = lap
            o_adj[part] = new
        else:
            full[place, start : start + CHUNK, :] = scale * (known + adj4[part] * lap + new * lap1[part])
    lay_pieces(full, outs[:-1])


def last_join_kernel(scale, from_chip, known, lap, adj, lap1, adj4, o_grad):
    waves = dict(chip_terms(from_chip, 0))
    adjs = dict(chip_terms(from_chip, 1))
    for row in range(REACH):
        last_lap = lap[row] + waves[row]
        last_adj = adj[row] + adjs[row]
        o_grad[row] = scale * (known[row] + adj4[row] * last_lap + last_adj * lap1[row])


def fold(value):
    total = value[:8]
    for start in range(8, value.shape[0], 8):
        total = total + value[start : start + 8]
    return total


PRODUCTS = [(0, a, 1, b) for a in range(PAIRS) for b in range(a, PAIRS)] + [
    (1, a, 1, b) for a in range(PAIRS) for b in range(a, PAIRS)
]
SLOT = {key: PRODUCTS.index(key) for key in PRODUCTS}
FIRST_DOT = len(PRODUCTS)


def gram_kernel(history, out):
    pairs, rows, piece = history.shape[1], history.shape[2], history.shape[3]
    width = history.shape[4]
    for group in range(0, len(PRODUCTS), 10):
        members = PRODUCTS[group : group + 10]

        def body(row, sums, members=members):
            new = list(sums)
            for start in range(0, piece, 8):
                part = {}
                for a, i, b, j in members:
                    for key in ((a, i), (b, j)):
                        if key not in part:
                            part[key] = history[key[0], key[1], row, start : start + 8, :]
                for n, (a, i, b, j) in enumerate(members):
                    new[n] = new[n] + part[a, i] * part[b, j]
            return tuple(new)

        sums = lax.fori_loop(0, rows, body, tuple(jnp.zeros((8, width), F32) for _ in members))
        for n in range(len(members)):
            out[group + n] = sums[n]


def inner_rows(rows):
    return list(range(REACH, rows - REACH))


def near_rows(rows):
    return list(range(REACH, rows))


def add_dots(sums, values, history, row):
    for kind in range(2):
        for pair in range(PAIRS):
            n = kind * PAIRS + pair
            sums[n] = sums[n] + fold(history[kind, pair, row] * values)


def chip_dots_kernel(count, grad, *refs):
    pieces, out = refs[:count], refs[count]
    total, piece = grad.shape[0], pieces[0].shape[3]
    odd = odd_depth()
    sums = [jnp.zeros((8, grad.shape[2]), F32) for _ in range(2 * PAIRS)]
    for place in range(total):
        source = natural_row(place, total, odd)
        for turn, ref in enumerate(pieces):
            offset = lax.rem(lax.axis_index("shot") + turn, count) * piece
            values = grad[place, pl.ds(pl.multiple_of(offset, 8), piece), :]
            add_dots(sums, values, ref, source)
    for n in range(2 * PAIRS):
        out[n] = sums[n]


def line_kernel(count, chip, gram, history, *refs):
    inner, core, out, o_near = refs[:count], refs[count : 2 * count], refs[-2], refs[-1]
    rows = history.shape[2]
    odd = odd_depth()
    sums = [chip[n] for n in range(2 * PAIRS)]
    for place, row in enumerate(near_rows(rows)):
        parts, at = (inner, place) if place < inner[0].shape[0] else (core, place - inner[0].shape[0])
        values = parts[0][at]
        for other in parts[1:]:
            values = values + other[at]
        o_near[place] = values
        add_dots(sums, values, history, natural_row(row, rows, odd))
    lane = lane_ids(out.shape[1])
    line = jnp.zeros((1, out.shape[1]), F32)
    for n in range(FIRST_DOT + 2 * PAIRS):
        value = gram[n] if n < FIRST_DOT else sums[n - FIRST_DOT]
        line = line + jnp.where(lane == n, jnp.sum(value, axis=(0, 1), keepdims=True), 0.0)
    out[...] = jnp.broadcast_to(line, out.shape)


def weights(line):
    lane = lane_ids(line.shape[1])

    def number(n):
        return jnp.sum(jnp.where(lane == n, line, 0.0), axis=(0, 1), keepdims=True)

    values = [number(n) for n in range(FIRST_DOT + 2 * PAIRS)]

    def sy(a, b):
        return values[SLOT[0, a, 1, b]]

    def yy(a, b):
        return values[SLOT[1, min(a, b), 1, max(a, b)]]

    s_grad = values[FIRST_DOT : FIRST_DOT + PAIRS]
    y_grad = values[FIRST_DOT + PAIRS :]
    rho = [1.0 / sy(i, i) for i in range(PAIRS)]
    alpha = [None] * PAIRS
    for i in reversed(range(PAIRS)):
        dot = s_grad[i]
        for j in range(PAIRS - 1, i, -1):
            dot = dot - alpha[j] * sy(i, j)
        alpha[i] = rho[i] * dot
    scale = sy(PAIRS - 1, PAIRS - 1) / yy(PAIRS - 1, PAIRS - 1)
    s_weight = [None] * PAIRS
    for i in range(PAIRS):
        dot = y_grad[i]
        for j in range(PAIRS):
            dot = dot - alpha[j] * yy(i, j)
        dot = scale * dot
        for j in range(i):
            dot = dot + s_weight[j] * sy(j, i)
        s_weight[i] = alpha[i] - rho[i] * dot
    return scale, [-(scale * a) for a in alpha], s_weight


def weights_kernel(lines, near, history, o_weights, o_move):
    rows = history.shape[2]
    piece, width = near.shape[1], near.shape[2]
    odd = odd_depth()
    total = lines[0:8]
    for start in range(8, lines.shape[0], 8):
        total = total + lines[start : start + 8]
    scale, y_weight, s_weight = weights(jnp.sum(total, axis=0, keepdims=True))
    wide = [jnp.broadcast_to(v, (8, width)) for v in [scale] + s_weight + y_weight]
    for n, value in enumerate(wide):
        o_weights[n] = value
    for place, row in enumerate(near_rows(rows)):
        source = natural_row(row, rows, odd)
        for start in range(0, piece, 8):
            at = slice(start, start + 8)
            o_move[place, at, :] = move_of(wide, near[place, at, :], history, source, at)


def move_of(wide, grad, history, row, at):
    move = wide[0] * grad
    for pair in range(PAIRS):
        move = move + wide[1 + pair] * history[0, pair, row, at, :]
        move = move + wide[1 + PAIRS + pair] * history[1, pair, row, at, :]
    return -move


def finish_kernel(count, weight, courant, near, near_move, chip, *refs):
    others, pieces = refs[: count - 1], refs[count - 1 : 2 * count - 1]
    o_grad, o_direction, o_next = refs[2 * count - 1 :]
    rows, across, width = courant.shape
    piece = across // count
    odd = odd_depth()
    wide = [weight[n] for n in range(1 + 2 * PAIRS)]
    mine = pl.ds(pl.multiple_of(lax.axis_index("shot") * piece, 8), piece)
    for place, row in enumerate(near_rows(rows)):
        source = natural_row(row, rows, odd)
        o_grad[source] = near[place]
        o_direction[source] = near_move[place]
        o_next[source, mine, :] = courant[source, mine, :] + 0.05 * near_move[place]
    for row in range(REACH):
        source = natural_row(row, rows, odd)
        kept = natural_row(row, REACH, odd)
        for turn, ref in enumerate(pieces):
            offset = lax.rem(lax.axis_index("shot") + turn, count) * piece
            for start in range(0, piece, 8):
                at = pl.ds(pl.multiple_of(offset + start, 8), 8)
                grad = chip[row, at, :]
                for other in others:
                    grad = grad + other[row, at, :]
                move = move_of(wide, grad, ref, kept, slice(start, start + 8))
                if turn == 0:
                    o_grad[source, start : start + 8, :] = grad
                    o_direction[source, start : start + 8, :] = move
                o_next[source, at, :] = courant[source, at, :] + 0.05 * move


def last_piece_kernel(count, courant, done, *refs):
    moves, o_next, buffer, sem = refs[: count - 1], refs[-3], refs[-2], refs[-1]
    rows, across, width = courant.shape
    piece = across // count
    odd = odd_depth()
    first = (1 - odd) * REACH
    copies = []
    for turn in range(1, count):
        offset = pl.multiple_of(lax.rem(lax.axis_index("shot") + turn, count) * piece, 8)
        for place, row in enumerate(near_rows(rows)):
            source = natural_row(row, rows, odd)
            value = courant[source, pl.ds(offset, piece), :] + 0.05 * moves[turn - 1][place]
            buffer[turn - 1, source - first] = value
        copies.append(
            pltpu.make_async_copy(
                buffer.at[turn - 1],
                o_next.at[pl.ds(first, rows - REACH), pl.ds(offset, piece)],
                sem.at[turn - 1],
            )
        )
        copies[-1].start()
    for copy in copies:
        copy.wait()


def call(
    kernel, name, outs, *args, specs=None, out_specs=None, aliases=None, scratch=(), cost=1 << 20
):
    return pl.pallas_call(
        kernel,
        name=name,
        out_shape=outs,
        in_specs=specs or [VM] * len(args),
        out_specs=out_specs or jax.tree.map(lambda _: VM, outs),
        input_output_aliases=aliases or {},
        scratch_shapes=list(scratch),
        compiler_params=PARAMS,
        cost_estimate=pl.CostEstimate(flops=cost, bytes_accessed=cost, transcendentals=0),
    )(*args)


def per_device(
    courant,
    wave_before,
    wave_current,
    adjoint_after,
    adjoint_current,
    source_cell,
    wavelet,
    receiver_cell,
    residual,
    history,
):
    rows, across, width = courant.shape
    depths = lax.axis_size("depth")
    shots = lax.axis_size("shot")
    devices = depths * shots
    piece = across // shots
    slab = shape(rows, across, width)
    padded = shape(rows, across + 2 * PAD, width)
    halo = shape(2 * REACH, across, width)
    on_chip = [(i, i ^ 1) for i in range(depths)]
    off_chip = [(i, i + 1 if i % 2 else i - 1) for i in range(1, depths - 1)]

    def swap_core(value):
        return lax.ppermute(value, "depth", on_chip)

    def swap_chip(value):
        return lax.ppermute(value, "depth", off_chip)

    def from_shot(value, turn):
        return lax.ppermute(value, "shot", [((i + turn) % shots, i) for i in range(shots)])

    block = pltpu.VMEM((rows, across, width), F32)
    held = [
        in_hbm(value)
        for value in (wave_current[0], wave_before[0], adjoint_current[0], adjoint_after[0], courant, history)
    ]
    wave, wave_old, adj, adj_old, cour, prod, to_core, to_chip = call(
        stage_kernel,
        "stage",
        [padded, padded, slab, slab, slab, padded, halo, halo],
        *held[:5],
        specs=[HB] * 5,
        scratch=[block] * 5 + [pltpu.SemaphoreType.DMA((5,))],
    )
    from_chip = swap_chip(to_chip)
    from_core = swap_core(to_core)
    kept = call(
        keep_kernel,
        "keep",
        shape(2, PAIRS, REACH, piece, width),
        held[5],
        from_core,
        specs=[HB, VM],
        scratch=[pltpu.SemaphoreType.DMA],
    )
    kept = [kept] + [from_shot(kept, turn) for turn in range(1, shots)]
    injected = call(
        functools.partial(receiver_kernel, across),
        "receivers",
        shape(STEPS, rows * across, width),
        receiver_cell,
        residual[0],
    )

    gram = call(gram_kernel, "gram", shape(len(PRODUCTS), 8, width), history)

    laps, adjs = [], []
    for moment in range(STEPS - 1):
        lap, new_wave, new_adj, new_prod = call(
            functools.partial(local_kernel, moment),
            f"local_{moment}",
            [slab, padded, slab, padded],
            source_cell,
            wavelet,
            wave,
            wave_old,
            prod,
            adj,
            adj_old,
            cour,
            injected,
            *([gram] if moment == STEPS - 2 else []),
            specs=[SM, SM] + [VM] * (8 if moment == STEPS - 2 else 7),
        )
        sends = []
        for chip, came in ((False, from_core), (True, from_chip)):
            lap, new_wave, new_adj, new_prod, send = call(
                functools.partial(join_kernel, chip),
                f"join_{'chip' if chip else 'core'}_{moment}",
                [slab, padded, slab, padded, halo],
                came,
                cour,
                lap,
                new_wave,
                new_adj,
                new_prod,
                aliases={2: 0, 3: 1, 4: 2, 5: 3},
            )
            sends.append(send)
        from_core = swap_core(sends[0])
        from_chip = swap_chip(sends[1])
        laps.append(lap)
        adjs.append(new_adj)
        wave_old, wave = wave, new_wave
        adj_old, adj = adj, new_adj
        prod = new_prod

    scale = 1.0 / (shots * STEPS)
    inner_count, near_count = rows - 2 * REACH, rows - REACH
    last = (wave, prod, adj, adj_old, injected, laps[0], laps[1], laps[2], adjs[0], adjs[1])

    def sum_parts(values):
        return [values[0]] + [from_shot(values[shots - turn], turn) for turn in range(1, shots)]

    inner = call(
        functools.partial(inner_kernel, scale),
        "inner",
        [shape(inner_count, piece, width)] * shots,
        *last,
        scratch=[pltpu.VMEM((inner_count, across, width), F32)],
    )
    inner = sum_parts(inner)
    chip_part = shape(REACH, across, width)
    known, lap, new_adj, *core = call(
        functools.partial(outer_kernel, scale),
        "outer",
        [chip_part] * 3 + [shape(REACH, piece, width)] * shots,
        from_core,
        *last,
        scratch=[pltpu.VMEM((REACH, across, width), F32)],
    )
    core = sum_parts(core)
    chip = call(
        functools.partial(last_join_kernel, scale),
        "last_join",
        chip_part,
        from_chip,
        known,
        lap,
        new_adj,
        laps[0],
        adjs[0],
    )
    others = [from_shot(chip, turn) for turn in range(1, shots)]
    chip_dots = call(
        functools.partial(chip_dots_kernel, shots),
        "chip_dots",
        shape(2 * PAIRS, 8, width),
        chip,
        *kept,
    )
    near = shape(near_count, piece, width)
    line, near_grad = call(
        functools.partial(line_kernel, shots),
        "line",
        [shape(devices, 128), near],
        chip_dots,
        gram,
        history,
        *inner,
        *core,
    )
    lines = lax.all_to_all(line, ("depth", "shot"), 0, 0, tiled=True)
    weight, move = call(
        weights_kernel,
        "weights",
        [shape(1 + 2 * PAIRS, 8, width), near],
        lines,
        near_grad,
        history,
    )
    moves = [from_shot(move, turn) for turn in range(1, shots)]
    own = shape(rows, piece, width)
    gradient, direction, courant_next = call(
        functools.partial(finish_kernel, shots),
        "finish",
        [own, own, slab],
        weight,
        courant,
        near_grad,
        move,
        chip,
        *others,
        *kept,
    )
    courant_next = call(
        functools.partial(last_piece_kernel, shots),
        "last_piece",
        slab,
        courant,
        courant_next,
        *moves,
        specs=[VM, HB] + [VM] * (shots - 1),
        out_specs=HB,
        aliases={1: 0},
        scratch=[
            pltpu.VMEM((shots - 1, near_count, piece, width), F32),
            pltpu.SemaphoreType.DMA((shots - 1,)),
        ],
    )
    return gradient, direction, courant_next


def solution(mesh):
    return jax.shard_map(
        per_device,
        mesh=mesh,
        in_specs=(
            P("depth", None, None),
            P("shot", "depth", None, None),
            P("shot", "depth", None, None),
            P("shot", "depth", None, None),
            P("shot", "depth", None, None),
            P("shot"),
            P("shot", None),
            P("shot", None),
            P("shot", None, None),
            P(None, None, "depth", "shot", None),
        ),
        out_specs=(P("depth", "shot", None), P("depth", "shot", None), P("depth", None, None)),
        check_vma=False,
    )
```

```python
import functools

import jax
import jax.numpy as jnp
from jax import lax
from jax.experimental import pallas as pl
from jax.experimental.pallas import tpu as pltpu
from jax.sharding import PartitionSpec as P

STEPS = 4
PAIRS = 5
REACH = 4
PAD = 8
GROUP = 8
CHUNK = 16
coefficients = (-205.0 / 72.0, 8.0 / 5.0, -1.0 / 5.0, 8.0 / 315.0, -1.0 / 560.0)

F32 = jnp.float32
VM = pl.BlockSpec(memory_space=pltpu.VMEM)
SM = pl.BlockSpec(memory_space=pltpu.SMEM)
HB = pl.BlockSpec(memory_space=pltpu.HBM)
PARAMS = pltpu.CompilerParams(vmem_limit_bytes=16 << 20)


def in_hbm(value):
    return pltpu.with_memory_space_constraint(value, pltpu.HBM)


def shape(*dims):
    return jax.ShapeDtypeStruct(dims, F32)


def natural_row(row, rows, odd):
    return jnp.where(odd == 1, rows - 1 - row, row)


def odd_depth():
    return lax.rem(lax.axis_index("depth"), 2)


def lane_ids(width):
    return lax.broadcasted_iota(jnp.int32, (1, width), 1)


def split3(value):
    high = value.astype(jnp.bfloat16)
    left = value - high.astype(F32)
    middle = left.astype(jnp.bfloat16)
    return high, middle, (left - middle.astype(F32)).astype(jnp.bfloat16)


def band_parts(width):
    apart = jnp.abs(
        lax.broadcasted_iota(jnp.int32, (width, width), 0) - lax.broadcasted_iota(jnp.int32, (width, width), 1)
    )
    band = jnp.zeros((width, width), F32)
    for reach in range(1, REACH + 1):
        band = band + jnp.where(apart == reach, coefficients[reach], 0.0)
    high, middle, low = split3(band)
    pair = jnp.concatenate([high, middle], axis=1)
    return jnp.concatenate([pair, pair], axis=0), jnp.concatenate([high, low], axis=0)


def along_last(ref, which, wide_band, tall_band, out):
    width = ref.shape[2]
    across = ref.shape[1] - 2 * PAD
    for first in range(0, len(which), GROUP):
        group = which[first : first + GROUP]
        cells = jnp.concatenate([ref[row, PAD : PAD + across, :] for row in group], axis=0)
        high, middle, low = split3(cells)
        large = jnp.dot(jnp.concatenate([high, middle], axis=1), wide_band, preferred_element_type=F32)
        small = jnp.dot(jnp.concatenate([low, high], axis=1), tall_band, preferred_element_type=F32)
        total = large[:, :width] + (large[:, width:] + small)
        for n in range(len(group)):
            out[first + n] = total[n * across : (n + 1) * across]


def laplace_chunk(ref, row, start, size, along):
    rows = ref.shape[0]
    total = along + (3.0 * coefficients[0]) * ref[row, PAD + start : PAD + start + size, :]
    for reach in range(1, REACH + 1):
        near = (
            ref[row, PAD + start + reach : PAD + start + reach + size, :]
            + ref[row, PAD + start - reach : PAD + start - reach + size, :]
        )
        if row - reach >= 0:
            near = near + ref[row - reach, PAD + start : PAD + start + size, :]
        if row + reach < rows:
            near = near + ref[row + reach, PAD + start : PAD + start + size, :]
        total = total + coefficients[reach] * near
    return total


def zero_pads(ref):
    rows, padded, width = ref.shape
    for row in range(rows):
        ref[row, :PAD, :] = jnp.zeros((PAD, width), F32)
        ref[row, padded - PAD :, :] = jnp.zeros((PAD, width), F32)


def stage_kernel(
    wave,
    wave_old,
    adjoint,
    adjoint_old,
    courant,
    o_wave,
    o_wave_old,
    o_adj,
    o_adj_old,
    o_cour,
    o_prod,
    to_core,
    to_chip,
    o_wide,
    o_tall,
    b_wave,
    b_wave_old,
    b_adj,
    b_adj_old,
    b_cour,
    sems,
):
    rows, across, width = courant.shape
    fetched = [(wave, b_wave), (adjoint, b_adj), (courant, b_cour), (wave_old, b_wave_old), (adjoint_old, b_adj_old)]
    copies = [pltpu.make_async_copy(src, dst, sems.at[n]) for n, (src, dst) in enumerate(fetched)]
    for copy in copies:
        copy.start()
    zero_pads(o_wave)
    zero_pads(o_wave_old)
    zero_pads(o_prod)
    o_wide[...], o_tall[...] = band_parts(width)
    odd = odd_depth()
    for copy in copies[:3]:
        copy.wait()
    for row in range(rows):
        src = natural_row(row, rows, odd)
        now, adj, cour = b_wave[src], b_adj[src], b_cour[src]
        prod = cour * adj
        o_wave[row, PAD : PAD + across, :] = now
        o_adj[row] = adj
        o_cour[row] = cour
        o_prod[row, PAD : PAD + across, :] = prod
        if row < REACH:
            to_chip[row] = now
            to_chip[REACH + row] = prod
        if row >= rows - REACH:
            to_core[row - (rows - REACH)] = now
            to_core[row - (rows - REACH) + REACH] = prod
    for copy in copies[3:]:
        copy.wait()
    for row in range(rows):
        src = natural_row(row, rows, odd)
        o_wave_old[row, PAD : PAD + across, :] = b_wave_old[src]
        o_adj_old[row] = b_adj_old[src]


def keep_kernel(history, _, out, sem):
    start = odd_depth() * (history.shape[2] - REACH)
    copy = pltpu.make_async_copy(history.at[:, :, pl.ds(start, REACH)], out, sem)
    copy.start()
    copy.wait()


def split_cell(cell, rows, across, width):
    depth_row = cell // (across * width) - lax.axis_index("depth") * rows
    rest = cell % (across * width)
    inside = (depth_row >= 0) & (depth_row < rows)
    row = jnp.where(odd_depth() == 1, rows - 1 - depth_row, depth_row)
    return inside, row, rest // width, rest % width


def receiver_kernel(across, receivers, residual, out):
    cells = out.shape[1]
    width = out.shape[2]
    count = receivers.shape[1]
    inside, row, place, lane = split_cell(receivers[...], cells // across, across, width)
    keys = jnp.where(inside, row * across + place, -1)
    hot = (lax.broadcasted_iota(jnp.int32, (cells, count), 0) == keys).astype(jnp.bfloat16)
    lanes = lax.broadcasted_iota(jnp.int32, (width, count), 0) == lane
    for moment in range(STEPS):
        value = jnp.where(lanes, residual[moment : moment + 1, :], 0.0)
        high = value.astype(jnp.bfloat16)
        left = value - high.astype(F32)
        middle = left.astype(jnp.bfloat16)
        low = (left - middle.astype(F32)).astype(jnp.bfloat16)
        pieces = [
            lax.dot_general(hot, piece, (((1,), (1,)), ((), ())), preferred_element_type=F32)
            for piece in (low, middle, high)
        ]
        out[moment] = (pieces[0] + pieces[1]) + pieces[2]


def local_kernel(
    moment, cell, wavelet, wave, wave_old, prod, adj, adj_old, courant, injected, wide_band, tall_band, *outs
):
    o_lap, o_wave, o_adj, o_prod, along_wave, along_prod = outs[-6:]
    rows, across, width = adj.shape
    along_last(wave, list(range(rows)), wide_band[...], tall_band[...], along_wave)
    along_last(prod, list(range(rows)), wide_band[...], tall_band[...], along_prod)
    zero_pads(o_wave)
    zero_pads(o_prod)
    for row in range(rows):
        for start in range(0, across, CHUNK):
            part = (row, pl.ds(start, CHUNK), slice(None))
            wide = (row, pl.ds(PAD + start, CHUNK), slice(None))
            lap = laplace_chunk(wave, row, start, CHUNK, along_wave[part])
            o_lap[part] = lap
            o_wave[wide] = 2.0 * wave[wide] - wave_old[wide] + courant[part] * lap
            new = 2.0 * adj[part] - adj_old[part] + laplace_chunk(prod, row, start, CHUNK, along_prod[part])
            new = new + injected[STEPS - 1 - moment, row * across + start : row * across + start + CHUNK, :]
            o_adj[part] = new
            o_prod[wide] = courant[part] * new
    inside, row, place, lane = split_cell(cell[0], rows, across, width)

    @pl.when(inside)
    def _():
        spot = (row, pl.ds(PAD + place, 1), slice(None))
        o_wave[spot] = o_wave[spot] + jnp.where(lane_ids(width) == lane, wavelet[0, moment], 0.0)


def chip_terms(ref, field):
    for place in range(REACH):
        term = None
        for reach in range(place + 1, REACH + 1):
            one = coefficients[reach] * ref[field * REACH + reach - place - 1]
            term = one if term is None else term + one
        yield place, term


def core_terms(ref, field, rows):
    for place in range(REACH):
        term = None
        for reach in range(place + 1, REACH + 1):
            one = coefficients[reach] * ref[field * REACH + REACH - reach + place]
            term = one if term is None else term + one
        yield rows - 1 - place, term


def join_kernel(chip, halo, courant, lap, wave, adj, prod, o_lap, o_wave, o_adj, o_prod, send):
    rows, across, width = adj.shape
    inner = slice(PAD, PAD + across)
    first = 0 if chip else rows - REACH
    for row, term in chip_terms(halo, 0) if chip else core_terms(halo, 0, rows):
        o_lap[row] = lap[row] + term
        new = wave[row, inner, :] + courant[row] * term
        o_wave[row, inner, :] = new
        send[row - first] = new
    for row, term in chip_terms(halo, 1) if chip else core_terms(halo, 1, rows):
        new = adj[row] + term
        o_adj[row] = new
        new = courant[row] * new
        o_prod[row, inner, :] = new
        send[REACH + row - first] = new


def last_rows(which, wave, prod, adj, adj_old, injected, wide_band, tall_band, along_wave, along_prod):
    across = adj.shape[1]
    along_last(wave, which, wide_band[...], tall_band[...], along_wave)
    along_last(prod, which, wide_band[...], tall_band[...], along_prod)
    for place, row in enumerate(which):
        for start in range(0, across, CHUNK):
            part = (row, pl.ds(start, CHUNK), slice(None))
            put = (place, pl.ds(start, CHUNK), slice(None))
            lap = laplace_chunk(wave, row, start, CHUNK, along_wave[put])
            new = 2.0 * adj[part] - adj_old[part] + laplace_chunk(prod, row, start, CHUNK, along_prod[put])
            new = new + injected[0, row * across + start : row * across + start + CHUNK, :]
            yield place, row, start, part, lap, new


def lay_pieces(full, outs):
    count = len(outs)
    piece = full.shape[1] // count
    for turn, out in enumerate(outs):
        offset = lax.rem(lax.axis_index("shot") + turn, count) * piece
        for place in range(full.shape[0]):
            out[place] = full[place, pl.ds(pl.multiple_of(offset, 8), piece), :]


def known_terms(part, adj, lap2, lap3, adj3):
    return adj[part] * lap2[part] + adj3[part] * lap3[part]


def inner_kernel(scale, _, wave, prod, adj, adj_old, injected, wide, tall, lap1, lap2, lap3, adj4, adj3, *outs):
    full, along = outs[-3], outs[-2:]
    which = inner_rows(adj.shape[0])
    for place, row, start, part, lap, new in last_rows(which, wave, prod, adj, adj_old, injected, wide, tall, *along):
        known = known_terms(part, adj, lap2, lap3, adj3)
        full[place, start : start + CHUNK, :] = scale * (known + adj4[part] * lap + new * lap1[part])
    lay_pieces(full, outs[:-3])


def core_kernel(
    scale, from_core, wave, prod, adj, adj_old, injected, wide, tall, lap1, lap2, lap3, adj4, adj3, *outs
):
    full, along = outs[-3], outs[-2:]
    rows = adj.shape[0]
    waves = dict(core_terms(from_core, 0, rows))
    adjs = dict(core_terms(from_core, 1, rows))
    which = list(range(rows - REACH, rows))
    for place, row, start, part, lap, new in last_rows(which, wave, prod, adj, adj_old, injected, wide, tall, *along):
        known = known_terms(part, adj, lap2, lap3, adj3)
        lap = lap + waves[row][start : start + CHUNK]
        new = new + adjs[row][start : start + CHUNK]
        full[place, start : start + CHUNK, :] = scale * (known + adj4[part] * lap + new * lap1[part])
    lay_pieces(full, outs[:-3])


def chip_kernel(
    wave, prod, adj, adj_old, injected, wide, tall, lap1, lap2, lap3, adj4, adj3, o_known, o_lap, o_adj, *along
):
    which = list(range(REACH))
    for place, row, start, part, lap, new in last_rows(which, wave, prod, adj, adj_old, injected, wide, tall, *along):
        o_known[part] = known_terms(part, adj, lap2, lap3, adj3)
        o_lap[part] = lap
        o_adj[part] = new


def last_join_kernel(scale, from_chip, known, lap, adj, lap1, adj4, *refs):
    o_grad = refs[-1]
    waves = dict(chip_terms(from_chip, 0))
    adjs = dict(chip_terms(from_chip, 1))
    for row in range(REACH):
        last_lap = lap[row] + waves[row]
        last_adj = adj[row] + adjs[row]
        o_grad[row] = scale * (known[row] + adj4[row] * last_lap + last_adj * lap1[row])


def fold(value):
    total = value[:8]
    for start in range(8, value.shape[0], 8):
        total = total + value[start : start + 8]
    return total


PRODUCTS = [(0, a, 1, b) for a in range(PAIRS) for b in range(a, PAIRS)] + [
    (1, a, 1, b) for a in range(PAIRS) for b in range(a, PAIRS)
]
SLOT = {key: PRODUCTS.index(key) for key in PRODUCTS}
FIRST_DOT = len(PRODUCTS)


def gram_kernel(history, out):
    pairs, rows, piece = history.shape[1], history.shape[2], history.shape[3]
    width = history.shape[4]
    for group in range(0, len(PRODUCTS), 10):
        members = PRODUCTS[group : group + 10]

        def body(row, sums, members=members):
            new = list(sums)
            for start in range(0, piece, 8):
                part = {}
                for a, i, b, j in members:
                    for key in ((a, i), (b, j)):
                        if key not in part:
                            part[key] = history[key[0], key[1], row, start : start + 8, :]
                for n, (a, i, b, j) in enumerate(members):
                    new[n] = new[n] + part[a, i] * part[b, j]
            return tuple(new)

        sums = lax.fori_loop(0, rows, body, tuple(jnp.zeros((8, width), F32) for _ in members))
        for n in range(len(members)):
            out[group + n] = sums[n]


def inner_rows(rows):
    return list(range(REACH, rows - REACH))


def near_rows(rows):
    return list(range(REACH, rows))


def add_dots(sums, values, history, row):
    for kind in range(2):
        for pair in range(PAIRS):
            n = kind * PAIRS + pair
            sums[n] = sums[n] + fold(history[kind, pair, row] * values)


def chip_dots_kernel(count, grad, *refs):
    pieces, out = refs[:count], refs[count]
    total, piece = grad.shape[0], pieces[0].shape[3]
    odd = odd_depth()
    sums = [jnp.zeros((8, grad.shape[2]), F32) for _ in range(2 * PAIRS)]
    for place in range(total):
        source = natural_row(place, total, odd)
        for turn, ref in enumerate(pieces):
            offset = lax.rem(lax.axis_index("shot") + turn, count) * piece
            values = grad[place, pl.ds(pl.multiple_of(offset, 8), piece), :]
            add_dots(sums, values, ref, source)
    for n in range(2 * PAIRS):
        out[n] = sums[n]


def line_kernel(count, chip, gram, history, *refs):
    inner, core, out, o_near = refs[:count], refs[count : 2 * count], refs[-2], refs[-1]
    rows = history.shape[2]
    odd = odd_depth()
    sums = [chip[n] for n in range(2 * PAIRS)]
    for place, row in enumerate(near_rows(rows)):
        parts, at = (inner, place) if place < inner[0].shape[0] else (core, place - inner[0].shape[0])
        values = parts[0][at]
        for other in parts[1:]:
            values = values + other[at]
        o_near[place] = values
        add_dots(sums, values, history, natural_row(row, rows, odd))
    lane = lane_ids(out.shape[1])
    line = jnp.zeros((1, out.shape[1]), F32)
    for n in range(FIRST_DOT + 2 * PAIRS):
        value = gram[n] if n < FIRST_DOT else sums[n - FIRST_DOT]
        line = line + jnp.where(lane == n, jnp.sum(value, axis=(0, 1), keepdims=True), 0.0)
    out[...] = jnp.broadcast_to(line, out.shape)


def weights(line):
    lane = lane_ids(line.shape[1])

    def number(n):
        return jnp.sum(jnp.where(lane == n, line, 0.0), axis=(0, 1), keepdims=True)

    values = [number(n) for n in range(FIRST_DOT + 2 * PAIRS)]

    def sy(a, b):
        return values[SLOT[0, a, 1, b]]

    def yy(a, b):
        return values[SLOT[1, min(a, b), 1, max(a, b)]]

    s_grad = values[FIRST_DOT : FIRST_DOT + PAIRS]
    y_grad = values[FIRST_DOT + PAIRS :]
    rho = [1.0 / sy(i, i) for i in range(PAIRS)]
    alpha = [None] * PAIRS
    for i in reversed(range(PAIRS)):
        dot = s_grad[i]
        for j in range(PAIRS - 1, i, -1):
            dot = dot - alpha[j] * sy(i, j)
        alpha[i] = rho[i] * dot
    scale = sy(PAIRS - 1, PAIRS - 1) / yy(PAIRS - 1, PAIRS - 1)
    s_weight = [None] * PAIRS
    for i in range(PAIRS):
        dot = y_grad[i]
        for j in range(PAIRS):
            dot = dot - alpha[j] * yy(i, j)
        dot = scale * dot
        for j in range(i):
            dot = dot + s_weight[j] * sy(j, i)
        s_weight[i] = alpha[i] - rho[i] * dot
    return scale, [-(scale * a) for a in alpha], s_weight


def weights_kernel(lines, near, history, *refs):
    o_weights, o_move = refs[-2:]
    rows = history.shape[2]
    piece, width = near.shape[1], near.shape[2]
    odd = odd_depth()
    total = lines[0:8]
    for start in range(8, lines.shape[0], 8):
        total = total + lines[start : start + 8]
    scale, y_weight, s_weight = weights(jnp.sum(total, axis=0, keepdims=True))
    wide = [jnp.broadcast_to(v, (8, width)) for v in [scale] + s_weight + y_weight]
    for n, value in enumerate(wide):
        o_weights[n] = value
    for place, row in enumerate(near_rows(rows)):
        source = natural_row(row, rows, odd)
        for start in range(0, piece, 8):
            at = slice(start, start + 8)
            o_move[place, at, :] = move_of(wide, near[place, at, :], history, source, at)


def move_of(wide, grad, history, row, at):
    move = wide[0] * grad
    for pair in range(PAIRS):
        move = move + wide[1 + pair] * history[0, pair, row, at, :]
        move = move + wide[1 + PAIRS + pair] * history[1, pair, row, at, :]
    return -move


def finish_kernel(count, weight, courant, near, near_move, chip, *refs):
    others, pieces = refs[: count - 1], refs[count - 1 : 2 * count - 1]
    o_grad, o_direction, o_next = refs[2 * count - 1 :]
    rows, across, width = courant.shape
    piece = across // count
    odd = odd_depth()
    wide = [weight[n] for n in range(1 + 2 * PAIRS)]
    mine = pl.ds(pl.multiple_of(lax.axis_index("shot") * piece, 8), piece)
    for place, row in enumerate(near_rows(rows)):
        source = natural_row(row, rows, odd)
        o_grad[source] = near[place]
        o_direction[source] = near_move[place]
        o_next[source, mine, :] = courant[source, mine, :] + 0.05 * near_move[place]
    for row in range(REACH):
        source = natural_row(row, rows, odd)
        kept = natural_row(row, REACH, odd)
        for turn, ref in enumerate(pieces):
            offset = lax.rem(lax.axis_index("shot") + turn, count) * piece
            for start in range(0, piece, 8):
                at = pl.ds(pl.multiple_of(offset + start, 8), 8)
                grad = chip[row, at, :]
                for other in others:
                    grad = grad + other[row, at, :]
                move = move_of(wide, grad, ref, kept, slice(start, start + 8))
                if turn == 0:
                    o_grad[source, start : start + 8, :] = grad
                    o_direction[source, start : start + 8, :] = move
                o_next[source, at, :] = courant[source, at, :] + 0.05 * move


def last_piece_kernel(count, courant, done, *refs):
    moves, o_next, buffer, sem = refs[: count - 1], refs[-3], refs[-2], refs[-1]
    rows, across, width = courant.shape
    piece = across // count
    odd = odd_depth()
    first = (1 - odd) * REACH
    copies = []
    for turn in range(1, count):
        offset = pl.multiple_of(lax.rem(lax.axis_index("shot") + turn, count) * piece, 8)
        for place, row in enumerate(near_rows(rows)):
            source = natural_row(row, rows, odd)
            value = courant[source, pl.ds(offset, piece), :] + 0.05 * moves[turn - 1][place]
            buffer[turn - 1, source - first] = value
        copies.append(
            pltpu.make_async_copy(
                buffer.at[turn - 1],
                o_next.at[pl.ds(first, rows - REACH), pl.ds(offset, piece)],
                sem.at[turn - 1],
            )
        )
        copies[-1].start()
    for copy in copies:
        copy.wait()


def call(
    kernel, name, outs, *args, specs=None, out_specs=None, aliases=None, scratch=(), cost=1 << 20
):
    return pl.pallas_call(
        kernel,
        name=name,
        out_shape=outs,
        in_specs=specs or [VM] * len(args),
        out_specs=out_specs or jax.tree.map(lambda _: VM, outs),
        input_output_aliases=aliases or {},
        scratch_shapes=list(scratch),
        compiler_params=PARAMS,
        cost_estimate=pl.CostEstimate(flops=cost, bytes_accessed=cost, transcendentals=0),
    )(*args)


def per_device(
    courant,
    wave_before,
    wave_current,
    adjoint_after,
    adjoint_current,
    source_cell,
    wavelet,
    receiver_cell,
    residual,
    history,
):
    rows, across, width = courant.shape
    depths = lax.axis_size("depth")
    shots = lax.axis_size("shot")
    devices = depths * shots
    piece = across // shots
    slab = shape(rows, across, width)
    padded = shape(rows, across + 2 * PAD, width)
    halo = shape(2 * REACH, across, width)
    on_chip = [(i, i ^ 1) for i in range(depths)]
    off_chip = [(i, i + 1 if i % 2 else i - 1) for i in range(1, depths - 1)]

    def swap_core(value):
        return lax.ppermute(value, "depth", on_chip)

    def swap_chip(value):
        return lax.ppermute(value, "depth", off_chip)

    def from_shot(value, turn):
        return lax.ppermute(value, "shot", [((i + turn) % shots, i) for i in range(shots)])

    block = pltpu.VMEM((rows, across, width), F32)
    held = [
        in_hbm(value)
        for value in (wave_current[0], wave_before[0], adjoint_current[0], adjoint_after[0], courant, history)
    ]
    bands = [jax.ShapeDtypeStruct((2 * width, n * width), jnp.bfloat16) for n in (2, 1)]
    wave, wave_old, adj, adj_old, cour, prod, to_core, to_chip, *bands = call(
        stage_kernel,
        "stage",
        [padded, padded, slab, slab, slab, padded, halo, halo] + bands,
        *held[:5],
        specs=[HB] * 5,
        scratch=[block] * 5 + [pltpu.SemaphoreType.DMA((5,))],
    )
    from_chip = swap_chip(to_chip)
    from_core = swap_core(to_core)
    kept = call(
        keep_kernel,
        "keep",
        shape(2, PAIRS, REACH, piece, width),
        held[5],
        from_core,
        specs=[HB, VM],
        scratch=[pltpu.SemaphoreType.DMA],
    )
    kept = [kept] + [from_shot(kept, turn) for turn in range(1, shots)]
    injected = call(
        functools.partial(receiver_kernel, across),
        "receivers",
        shape(STEPS, rows * across, width),
        receiver_cell,
        residual[0],
    )

    gram = call(gram_kernel, "gram", shape(len(PRODUCTS), 8, width), history)

    laps, adjs = [], []
    for moment in range(STEPS - 1):
        lap, new_wave, new_adj, new_prod = call(
            functools.partial(local_kernel, moment),
            f"local_{moment}",
            [slab, padded, slab, padded],
            source_cell,
            wavelet,
            wave,
            wave_old,
            prod,
            adj,
            adj_old,
            cour,
            injected,
            *bands,
            *([gram] if moment == STEPS - 2 else []),
            specs=[SM, SM] + [VM] * (10 if moment == STEPS - 2 else 9),
            scratch=[block] * 2,
        )
        sends = []
        for chip, came in ((False, from_core), (True, from_chip)):
            lap, new_wave, new_adj, new_prod, send = call(
                functools.partial(join_kernel, chip),
                f"join_{'chip' if chip else 'core'}_{moment}",
                [slab, padded, slab, padded, halo],
                came,
                cour,
                lap,
                new_wave,
                new_adj,
                new_prod,
                aliases={2: 0, 3: 1, 4: 2, 5: 3},
            )
            sends.append(send)
        from_core = swap_core(sends[0])
        from_chip = swap_chip(sends[1])
        laps.append(lap)
        adjs.append(new_adj)
        wave_old, wave = wave, new_wave
        adj_old, adj = adj, new_adj
        prod = new_prod

    scale = 1.0 / (shots * STEPS)
    inner_count, near_count = rows - 2 * REACH, rows - REACH
    last = (wave, prod, adj, adj_old, injected, *bands, laps[0], laps[1], laps[2], adjs[0], adjs[1])

    def sum_parts(values):
        return [values[0]] + [from_shot(values[shots - turn], turn) for turn in range(1, shots)]

    def some_rows(count, copies):
        return [pltpu.VMEM((count, across, width), F32)] * copies

    core = call(
        functools.partial(core_kernel, scale),
        "core",
        [shape(REACH, piece, width)] * shots,
        from_core,
        *last,
        scratch=some_rows(REACH, 3),
    )
    inner = call(
        functools.partial(inner_kernel, scale),
        "inner",
        [shape(inner_count, piece, width)] * shots,
        core[0],
        *last,
        scratch=some_rows(inner_count, 3),
    )
    core, inner = sum_parts(core), sum_parts(inner)
    chip_part = shape(REACH, across, width)
    known, lap, new_adj = call(chip_kernel, "chip", [chip_part] * 3, *last, scratch=some_rows(REACH, 2))
    chip = call(
        functools.partial(last_join_kernel, scale),
        "last_join",
        chip_part,
        from_chip,
        known,
        lap,
        new_adj,
        laps[0],
        adjs[0],
        *core[1:],
        *inner[1:],
    )
    others = [from_shot(chip, turn) for turn in range(1, shots)]
    chip_dots = call(
        functools.partial(chip_dots_kernel, shots),
        "chip_dots",
        shape(2 * PAIRS, 8, width),
        chip,
        *kept,
    )
    near = shape(near_count, piece, width)
    line, near_grad = call(
        functools.partial(line_kernel, shots),
        "line",
        [shape(devices, 128), near],
        chip_dots,
        gram,
        history,
        *inner,
        *core,
    )
    lines = lax.all_to_all(line, ("depth", "shot"), 0, 0, tiled=True)
    weight, move = call(
        weights_kernel,
        "weights",
        [shape(1 + 2 * PAIRS, 8, width), near],
        lines,
        near_grad,
        history,
        *others,
    )
    moves = [from_shot(move, turn) for turn in range(1, shots)]
    own = shape(rows, piece, width)
    gradient, direction, courant_next = call(
        functools.partial(finish_kernel, shots),
        "finish",
        [own, own, slab],
        weight,
        courant,
        near_grad,
        move,
        chip,
        *others,
        *kept,
    )
    courant_next = call(
        functools.partial(last_piece_kernel, shots),
        "last_piece",
        slab,
        courant,
        courant_next,
        *moves,
        specs=[VM, HB] + [VM] * (shots - 1),
        out_specs=HB,
        aliases={1: 0},
        scratch=[
            pltpu.VMEM((shots - 1, near_count, piece, width), F32),
            pltpu.SemaphoreType.DMA((shots - 1,)),
        ],
    )
    return gradient, direction, courant_next


def solution(mesh):
    return jax.shard_map(
        per_device,
        mesh=mesh,
        in_specs=(
            P("depth", None, None),
            P("shot", "depth", None, None),
            P("shot", "depth", None, None),
            P("shot", "depth", None, None),
            P("shot", "depth", None, None),
            P("shot"),
            P("shot", None),
            P("shot", None),
            P("shot", None, None),
            P(None, None, "depth", "shot", None),
        ),
        out_specs=(P("depth", "shot", None), P("depth", "shot", None), P("depth", None, None)),
        check_vma=False,
    )
```

```python
import functools

import jax
import jax.numpy as jnp
from jax import lax
from jax.experimental import pallas as pl
from jax.experimental.pallas import tpu as pltpu
from jax.sharding import PartitionSpec as P

STEPS = 4
PAIRS = 5
REACH = 4
PAD = 8
GROUP = 8
CHUNK = 16
coefficients = (-205.0 / 72.0, 8.0 / 5.0, -1.0 / 5.0, 8.0 / 315.0, -1.0 / 560.0)

F32 = jnp.float32
VM = pl.BlockSpec(memory_space=pltpu.VMEM)
SM = pl.BlockSpec(memory_space=pltpu.SMEM)
HB = pl.BlockSpec(memory_space=pltpu.HBM)
PARAMS = pltpu.CompilerParams(vmem_limit_bytes=16 << 20)


def in_hbm(value):
    return pltpu.with_memory_space_constraint(value, pltpu.HBM)


def shape(*dims):
    return jax.ShapeDtypeStruct(dims, F32)


def natural_row(row, rows, odd):
    return jnp.where(odd == 1, rows - 1 - row, row)


def odd_depth():
    return lax.rem(lax.axis_index("depth"), 2)


def lane_ids(width):
    return lax.broadcasted_iota(jnp.int32, (1, width), 1)


def split3(value):
    high = value.astype(jnp.bfloat16)
    left = value - high.astype(F32)
    middle = left.astype(jnp.bfloat16)
    return high, middle, (left - middle.astype(F32)).astype(jnp.bfloat16)


def band_parts(width):
    apart = jnp.abs(
        lax.broadcasted_iota(jnp.int32, (width, width), 0) - lax.broadcasted_iota(jnp.int32, (width, width), 1)
    )
    band = jnp.zeros((width, width), F32)
    for reach in range(1, REACH + 1):
        band = band + jnp.where(apart == reach, coefficients[reach], 0.0)
    high, middle, low = split3(band)
    pair = jnp.concatenate([high, middle], axis=1)
    return jnp.concatenate([pair, pair], axis=0), jnp.concatenate([high, low], axis=0)


def along_last(ref, which, wide_band, tall_band, out):
    width = ref.shape[2]
    across = ref.shape[1] - 2 * PAD
    for first in range(0, len(which), GROUP):
        group = which[first : first + GROUP]
        cells = jnp.concatenate([ref[row, PAD : PAD + across, :] for row in group], axis=0)
        high, middle, low = split3(cells)
        large = jnp.dot(jnp.concatenate([high, middle], axis=1), wide_band, preferred_element_type=F32)
        small = jnp.dot(jnp.concatenate([low, high], axis=1), tall_band, preferred_element_type=F32)
        total = large[:, :width] + (large[:, width:] + small)
        for n in range(len(group)):
            out[first + n] = total[n * across : (n + 1) * across]


def laplace_chunk(ref, row, start, size, along):
    rows = ref.shape[0]
    total = along + (3.0 * coefficients[0]) * ref[row, PAD + start : PAD + start + size, :]
    for reach in range(1, REACH + 1):
        near = (
            ref[row, PAD + start + reach : PAD + start + reach + size, :]
            + ref[row, PAD + start - reach : PAD + start - reach + size, :]
        )
        if row - reach >= 0:
            near = near + ref[row - reach, PAD + start : PAD + start + size, :]
        if row + reach < rows:
            near = near + ref[row + reach, PAD + start : PAD + start + size, :]
        total = total + coefficients[reach] * near
    return total


def zero_pads(ref):
    rows, padded, width = ref.shape
    for row in range(rows):
        ref[row, :PAD, :] = jnp.zeros((PAD, width), F32)
        ref[row, padded - PAD :, :] = jnp.zeros((PAD, width), F32)


def first_send_kernel(wave, adjoint, courant, to_chip, to_core, b_wave, b_adj, b_cour, sems):
    rows = courant.shape[0]
    odd = odd_depth()
    copies = []
    for which, start in enumerate((odd * (rows - REACH), (1 - odd) * (rows - REACH))):
        for n, (src, dst) in enumerate([(wave, b_wave), (adjoint, b_adj), (courant, b_cour)]):
            copies.append(pltpu.make_async_copy(src.at[pl.ds(start, REACH)], dst.at[which], sems.at[3 * which + n]))
    for copy in copies:
        copy.start()
    for copy in copies:
        copy.wait()
    for which, send in enumerate((to_chip, to_core)):
        for row in range(REACH):
            src = natural_row(row, REACH, odd)
            send[row] = b_wave[which, src]
            send[REACH + row] = b_cour[which, src] * b_adj[which, src]


def stage_kernel(
    wave,
    wave_old,
    adjoint,
    adjoint_old,
    courant,
    o_wave,
    o_wave_old,
    o_adj,
    o_adj_old,
    o_cour,
    o_prod,
    o_wide,
    o_tall,
    b_wave,
    b_wave_old,
    b_adj,
    b_adj_old,
    b_cour,
    sems,
):
    rows, across, width = courant.shape
    fetched = [(wave, b_wave), (adjoint, b_adj), (courant, b_cour), (wave_old, b_wave_old), (adjoint_old, b_adj_old)]
    copies = [pltpu.make_async_copy(src, dst, sems.at[n]) for n, (src, dst) in enumerate(fetched)]
    for copy in copies:
        copy.start()
    zero_pads(o_wave)
    zero_pads(o_wave_old)
    zero_pads(o_prod)
    o_wide[...], o_tall[...] = band_parts(width)
    odd = odd_depth()
    for copy in copies[:3]:
        copy.wait()
    for row in range(rows):
        src = natural_row(row, rows, odd)
        now, adj, cour = b_wave[src], b_adj[src], b_cour[src]
        prod = cour * adj
        o_wave[row, PAD : PAD + across, :] = now
        o_adj[row] = adj
        o_cour[row] = cour
        o_prod[row, PAD : PAD + across, :] = prod
    for copy in copies[3:]:
        copy.wait()
    for row in range(rows):
        src = natural_row(row, rows, odd)
        o_wave_old[row, PAD : PAD + across, :] = b_wave_old[src]
        o_adj_old[row] = b_adj_old[src]


def keep_kernel(history, _, out, sem):
    start = odd_depth() * (history.shape[2] - REACH)
    copy = pltpu.make_async_copy(history.at[:, :, pl.ds(start, REACH)], out, sem)
    copy.start()
    copy.wait()


def split_cell(cell, rows, across, width):
    depth_row = cell // (across * width) - lax.axis_index("depth") * rows
    rest = cell % (across * width)
    inside = (depth_row >= 0) & (depth_row < rows)
    row = jnp.where(odd_depth() == 1, rows - 1 - depth_row, depth_row)
    return inside, row, rest // width, rest % width


def receiver_kernel(across, receivers, residual, out):
    cells = out.shape[1]
    width = out.shape[2]
    count = receivers.shape[1]
    inside, row, place, lane = split_cell(receivers[...], cells // across, across, width)
    keys = jnp.where(inside, row * across + place, -1)
    hot = (lax.broadcasted_iota(jnp.int32, (cells, count), 0) == keys).astype(jnp.bfloat16)
    lanes = lax.broadcasted_iota(jnp.int32, (width, count), 0) == lane
    for moment in range(STEPS):
        value = jnp.where(lanes, residual[moment : moment + 1, :], 0.0)
        high = value.astype(jnp.bfloat16)
        left = value - high.astype(F32)
        middle = left.astype(jnp.bfloat16)
        low = (left - middle.astype(F32)).astype(jnp.bfloat16)
        pieces = [
            lax.dot_general(hot, piece, (((1,), (1,)), ((), ())), preferred_element_type=F32)
            for piece in (low, middle, high)
        ]
        out[moment] = (pieces[0] + pieces[1]) + pieces[2]


def local_kernel(
    moment, cell, wavelet, wave, wave_old, prod, adj, adj_old, courant, injected, wide_band, tall_band, *outs
):
    o_lap, o_wave, o_adj, o_prod, along_wave, along_prod = outs[-6:]
    rows, across, width = adj.shape
    along_last(wave, list(range(rows)), wide_band[...], tall_band[...], along_wave)
    along_last(prod, list(range(rows)), wide_band[...], tall_band[...], along_prod)
    zero_pads(o_wave)
    zero_pads(o_prod)
    for row in range(rows):
        for start in range(0, across, CHUNK):
            part = (row, pl.ds(start, CHUNK), slice(None))
            wide = (row, pl.ds(PAD + start, CHUNK), slice(None))
            lap = laplace_chunk(wave, row, start, CHUNK, along_wave[part])
            o_lap[part] = lap
            o_wave[wide] = 2.0 * wave[wide] - wave_old[wide] + courant[part] * lap
            new = 2.0 * adj[part] - adj_old[part] + laplace_chunk(prod, row, start, CHUNK, along_prod[part])
            new = new + injected[STEPS - 1 - moment, row * across + start : row * across + start + CHUNK, :]
            o_adj[part] = new
            o_prod[wide] = courant[part] * new
    inside, row, place, lane = split_cell(cell[0], rows, across, width)

    @pl.when(inside)
    def _():
        spot = (row, pl.ds(PAD + place, 1), slice(None))
        o_wave[spot] = o_wave[spot] + jnp.where(lane_ids(width) == lane, wavelet[0, moment], 0.0)


def chip_terms(ref, field):
    for place in range(REACH):
        term = None
        for reach in range(place + 1, REACH + 1):
            one = coefficients[reach] * ref[field * REACH + reach - place - 1]
            term = one if term is None else term + one
        yield place, term


def core_terms(ref, field, rows):
    for place in range(REACH):
        term = None
        for reach in range(place + 1, REACH + 1):
            one = coefficients[reach] * ref[field * REACH + REACH - reach + place]
            term = one if term is None else term + one
        yield rows - 1 - place, term


def join_kernel(chip, halo, courant, lap, wave, adj, prod, o_lap, o_wave, o_adj, o_prod, send):
    rows, across, width = adj.shape
    inner = slice(PAD, PAD + across)
    first = 0 if chip else rows - REACH
    for row, term in chip_terms(halo, 0) if chip else core_terms(halo, 0, rows):
        o_lap[row] = lap[row] + term
        new = wave[row, inner, :] + courant[row] * term
        o_wave[row, inner, :] = new
        send[row - first] = new
    for row, term in chip_terms(halo, 1) if chip else core_terms(halo, 1, rows):
        new = adj[row] + term
        o_adj[row] = new
        new = courant[row] * new
        o_prod[row, inner, :] = new
        send[REACH + row - first] = new


def last_rows(which, wave, prod, adj, adj_old, injected, wide_band, tall_band, along_wave, along_prod):
    across = adj.shape[1]
    along_last(wave, which, wide_band[...], tall_band[...], along_wave)
    along_last(prod, which, wide_band[...], tall_band[...], along_prod)
    for place, row in enumerate(which):
        for start in range(0, across, CHUNK):
            part = (row, pl.ds(start, CHUNK), slice(None))
            put = (place, pl.ds(start, CHUNK), slice(None))
            lap = laplace_chunk(wave, row, start, CHUNK, along_wave[put])
            new = 2.0 * adj[part] - adj_old[part] + laplace_chunk(prod, row, start, CHUNK, along_prod[put])
            new = new + injected[0, row * across + start : row * across + start + CHUNK, :]
            yield place, row, start, part, lap, new


def lay_pieces(full, outs):
    count = len(outs)
    piece = full.shape[1] // count
    for turn, out in enumerate(outs):
        offset = lax.rem(lax.axis_index("shot") + turn, count) * piece
        for place in range(full.shape[0]):
            out[place] = full[place, pl.ds(pl.multiple_of(offset, 8), piece), :]


def known_terms(part, adj, lap2, lap3, adj3):
    return adj[part] * lap2[part] + adj3[part] * lap3[part]


def inner_kernel(scale, _, wave, prod, adj, adj_old, injected, wide, tall, lap1, lap2, lap3, adj4, adj3, *outs):
    full, along = outs[-3], outs[-2:]
    which = inner_rows(adj.shape[0])
    for place, row, start, part, lap, new in last_rows(which, wave, prod, adj, adj_old, injected, wide, tall, *along):
        known = known_terms(part, adj, lap2, lap3, adj3)
        full[place, start : start + CHUNK, :] = scale * (known + adj4[part] * lap + new * lap1[part])
    lay_pieces(full, outs[:-3])


def core_kernel(
    scale, from_core, wave, prod, adj, adj_old, injected, wide, tall, lap1, lap2, lap3, adj4, adj3, *outs
):
    full, along = outs[-3], outs[-2:]
    rows = adj.shape[0]
    waves = dict(core_terms(from_core, 0, rows))
    adjs = dict(core_terms(from_core, 1, rows))
    which = list(range(rows - REACH, rows))
    for place, row, start, part, lap, new in last_rows(which, wave, prod, adj, adj_old, injected, wide, tall, *along):
        known = known_terms(part, adj, lap2, lap3, adj3)
        lap = lap + waves[row][start : start + CHUNK]
        new = new + adjs[row][start : start + CHUNK]
        full[place, start : start + CHUNK, :] = scale * (known + adj4[part] * lap + new * lap1[part])
    lay_pieces(full, outs[:-3])


def chip_kernel(wave, prod, adj, adj_old, injected, wide, tall, lap1, lap2, lap3, adj4, adj3, *refs):
    o_known, o_lap, o_adj, *along = refs[-5:]
    which = list(range(REACH))
    for place, row, start, part, lap, new in last_rows(which, wave, prod, adj, adj_old, injected, wide, tall, *along):
        o_known[part] = known_terms(part, adj, lap2, lap3, adj3)
        o_lap[part] = lap
        o_adj[part] = new


def last_join_kernel(scale, from_chip, known, lap, adj, lap1, adj4, *refs):
    o_grad = refs[-1]
    waves = dict(chip_terms(from_chip, 0))
    adjs = dict(chip_terms(from_chip, 1))
    for row in range(REACH):
        last_lap = lap[row] + waves[row]
        last_adj = adj[row] + adjs[row]
        o_grad[row] = scale * (known[row] + adj4[row] * last_lap + last_adj * lap1[row])


def fold(value):
    total = value[:8]
    for start in range(8, value.shape[0], 8):
        total = total + value[start : start + 8]
    return total


PRODUCTS = [(0, a, 1, b) for a in range(PAIRS) for b in range(a, PAIRS)] + [
    (1, a, 1, b) for a in range(PAIRS) for b in range(a, PAIRS)
]
SLOT = {key: PRODUCTS.index(key) for key in PRODUCTS}
FIRST_DOT = len(PRODUCTS)


def gram_kernel(history, out):
    pairs, rows, piece = history.shape[1], history.shape[2], history.shape[3]
    width = history.shape[4]
    for group in range(0, len(PRODUCTS), 10):
        members = PRODUCTS[group : group + 10]

        def body(row, sums, members=members):
            new = list(sums)
            for start in range(0, piece, 8):
                part = {}
                for a, i, b, j in members:
                    for key in ((a, i), (b, j)):
                        if key not in part:
                            part[key] = history[key[0], key[1], row, start : start + 8, :]
                for n, (a, i, b, j) in enumerate(members):
                    new[n] = new[n] + part[a, i] * part[b, j]
            return tuple(new)

        sums = lax.fori_loop(0, rows, body, tuple(jnp.zeros((8, width), F32) for _ in members))
        for n in range(len(members)):
            out[group + n] = sums[n]


def inner_rows(rows):
    return list(range(REACH, rows - REACH))


def near_rows(rows):
    return list(range(REACH, rows))


def add_dots(sums, values, history, row):
    for kind in range(2):
        for pair in range(PAIRS):
            n = kind * PAIRS + pair
            sums[n] = sums[n] + fold(history[kind, pair, row] * values)


def chip_dots_kernel(count, grad, *refs):
    pieces, out = refs[:count], refs[-1]
    total, piece = grad.shape[0], pieces[0].shape[3]
    odd = odd_depth()
    sums = [jnp.zeros((8, grad.shape[2]), F32) for _ in range(2 * PAIRS)]
    for place in range(total):
        source = natural_row(place, total, odd)
        for turn, ref in enumerate(pieces):
            offset = lax.rem(lax.axis_index("shot") + turn, count) * piece
            values = grad[place, pl.ds(pl.multiple_of(offset, 8), piece), :]
            add_dots(sums, values, ref, source)
    for n in range(2 * PAIRS):
        out[n] = sums[n]


def line_kernel(count, chip, gram, history, *refs):
    inner, core, out, o_near = refs[:count], refs[count : 2 * count], refs[-2], refs[-1]
    rows = history.shape[2]
    odd = odd_depth()
    sums = [chip[n] for n in range(2 * PAIRS)]
    for place, row in enumerate(near_rows(rows)):
        parts, at = (inner, place) if place < inner[0].shape[0] else (core, place - inner[0].shape[0])
        values = parts[0][at]
        for other in parts[1:]:
            values = values + other[at]
        o_near[place] = values
        add_dots(sums, values, history, natural_row(row, rows, odd))
    lane = lane_ids(out.shape[1])
    line = jnp.zeros((1, out.shape[1]), F32)
    for n in range(FIRST_DOT + 2 * PAIRS):
        value = gram[n] if n < FIRST_DOT else sums[n - FIRST_DOT]
        line = line + jnp.where(lane == n, jnp.sum(value, axis=(0, 1), keepdims=True), 0.0)
    out[...] = jnp.broadcast_to(line, out.shape)


def weights(line):
    lane = lane_ids(line.shape[1])

    def number(n):
        return jnp.sum(jnp.where(lane == n, line, 0.0), axis=(0, 1), keepdims=True)

    values = [number(n) for n in range(FIRST_DOT + 2 * PAIRS)]

    def sy(a, b):
        return values[SLOT[0, a, 1, b]]

    def yy(a, b):
        return values[SLOT[1, min(a, b), 1, max(a, b)]]

    s_grad = values[FIRST_DOT : FIRST_DOT + PAIRS]
    y_grad = values[FIRST_DOT + PAIRS :]
    rho = [1.0 / sy(i, i) for i in range(PAIRS)]
    alpha = [None] * PAIRS
    for i in reversed(range(PAIRS)):
        dot = s_grad[i]
        for j in range(PAIRS - 1, i, -1):
            dot = dot - alpha[j] * sy(i, j)
        alpha[i] = rho[i] * dot
    scale = sy(PAIRS - 1, PAIRS - 1) / yy(PAIRS - 1, PAIRS - 1)
    s_weight = [None] * PAIRS
    for i in range(PAIRS):
        dot = y_grad[i]
        for j in range(PAIRS):
            dot = dot - alpha[j] * yy(i, j)
        dot = scale * dot
        for j in range(i):
            dot = dot + s_weight[j] * sy(j, i)
        s_weight[i] = alpha[i] - rho[i] * dot
    return scale, [-(scale * a) for a in alpha], s_weight


def weights_kernel(lines, near, history, *refs):
    o_weights, o_move = refs[-2:]
    rows = history.shape[2]
    piece, width = near.shape[1], near.shape[2]
    odd = odd_depth()
    total = lines[0:8]
    for start in range(8, lines.shape[0], 8):
        total = total + lines[start : start + 8]
    scale, y_weight, s_weight = weights(jnp.sum(total, axis=0, keepdims=True))
    wide = [jnp.broadcast_to(v, (8, width)) for v in [scale] + s_weight + y_weight]
    for n, value in enumerate(wide):
        o_weights[n] = value
    for place, row in enumerate(near_rows(rows)):
        source = natural_row(row, rows, odd)
        for start in range(0, piece, 8):
            at = slice(start, start + 8)
            o_move[place, at, :] = move_of(wide, near[place, at, :], history, source, at)


def move_of(wide, grad, history, row, at):
    move = wide[0] * grad
    for pair in range(PAIRS):
        move = move + wide[1 + pair] * history[0, pair, row, at, :]
        move = move + wide[1 + PAIRS + pair] * history[1, pair, row, at, :]
    return -move


def finish_kernel(count, weight, courant, near, near_move, chip, *refs):
    others, pieces = refs[: count - 1], refs[count - 1 : 2 * count - 1]
    o_grad, o_direction, o_next = refs[2 * count - 1 :]
    rows, across, width = courant.shape
    piece = across // count
    odd = odd_depth()
    wide = [weight[n] for n in range(1 + 2 * PAIRS)]
    mine = pl.ds(pl.multiple_of(lax.axis_index("shot") * piece, 8), piece)
    for place, row in enumerate(near_rows(rows)):
        source = natural_row(row, rows, odd)
        o_grad[source] = near[place]
        o_direction[source] = near_move[place]
        o_next[source, mine, :] = courant[source, mine, :] + 0.05 * near_move[place]
    for row in range(REACH):
        source = natural_row(row, rows, odd)
        kept = natural_row(row, REACH, odd)
        for turn, ref in enumerate(pieces):
            offset = lax.rem(lax.axis_index("shot") + turn, count) * piece
            for start in range(0, piece, 8):
                at = pl.ds(pl.multiple_of(offset + start, 8), 8)
                grad = chip[row, at, :]
                for other in others:
                    grad = grad + other[row, at, :]
                move = move_of(wide, grad, ref, kept, slice(start, start + 8))
                if turn == 0:
                    o_grad[source, start : start + 8, :] = grad
                    o_direction[source, start : start + 8, :] = move
                o_next[source, at, :] = courant[source, at, :] + 0.05 * move


def last_piece_kernel(count, courant, done, *refs):
    moves, o_next, buffer, sem = refs[: count - 1], refs[-3], refs[-2], refs[-1]
    rows, across, width = courant.shape
    piece = across // count
    odd = odd_depth()
    first = (1 - odd) * REACH
    copies = []
    for turn in range(1, count):
        offset = pl.multiple_of(lax.rem(lax.axis_index("shot") + turn, count) * piece, 8)
        for place, row in enumerate(near_rows(rows)):
            source = natural_row(row, rows, odd)
            value = courant[source, pl.ds(offset, piece), :] + 0.05 * moves[turn - 1][place]
            buffer[turn - 1, source - first] = value
        copies.append(
            pltpu.make_async_copy(
                buffer.at[turn - 1],
                o_next.at[pl.ds(first, rows - REACH), pl.ds(offset, piece)],
                sem.at[turn - 1],
            )
        )
        copies[-1].start()
    for copy in copies:
        copy.wait()


def call(
    kernel, name, outs, *args, specs=None, out_specs=None, aliases=None, scratch=(), cost=1 << 20
):
    return pl.pallas_call(
        kernel,
        name=name,
        out_shape=outs,
        in_specs=specs or [VM] * len(args),
        out_specs=out_specs or jax.tree.map(lambda _: VM, outs),
        input_output_aliases=aliases or {},
        scratch_shapes=list(scratch),
        compiler_params=PARAMS,
        cost_estimate=pl.CostEstimate(flops=cost, bytes_accessed=cost, transcendentals=0),
    )(*args)


def per_device(
    courant,
    wave_before,
    wave_current,
    adjoint_after,
    adjoint_current,
    source_cell,
    wavelet,
    receiver_cell,
    residual,
    history,
):
    rows, across, width = courant.shape
    depths = lax.axis_size("depth")
    shots = lax.axis_size("shot")
    devices = depths * shots
    piece = across // shots
    slab = shape(rows, across, width)
    padded = shape(rows, across + 2 * PAD, width)
    halo = shape(2 * REACH, across, width)
    on_chip = [(i, i ^ 1) for i in range(depths)]
    off_chip = [(i, i + 1 if i % 2 else i - 1) for i in range(1, depths - 1)]

    def swap_core(value):
        return lax.ppermute(value, "depth", on_chip)

    def swap_chip(value):
        return lax.ppermute(value, "depth", off_chip)

    def from_shot(value, turn):
        return lax.ppermute(value, "shot", [((i + turn) % shots, i) for i in range(shots)])

    block = pltpu.VMEM((rows, across, width), F32)
    held = [
        in_hbm(value)
        for value in (wave_current[0], wave_before[0], adjoint_current[0], adjoint_after[0], courant, history)
    ]
    bands = [jax.ShapeDtypeStruct((2 * width, n * width), jnp.bfloat16) for n in (2, 1)]
    outer_rows = pltpu.VMEM((2, REACH, across, width), F32)
    to_chip, to_core = call(
        first_send_kernel,
        "first_send",
        [halo, halo],
        held[0],
        held[2],
        held[4],
        specs=[HB] * 3,
        scratch=[outer_rows] * 3 + [pltpu.SemaphoreType.DMA((6,))],
    )
    from_chip = swap_chip(to_chip)
    from_core = swap_core(to_core)
    wave, wave_old, adj, adj_old, cour, prod, *bands = call(
        stage_kernel,
        "stage",
        [padded, padded, slab, slab, slab, padded] + bands,
        *held[:5],
        specs=[HB] * 5,
        scratch=[block] * 5 + [pltpu.SemaphoreType.DMA((5,))],
    )
    kept = call(
        keep_kernel,
        "keep",
        shape(2, PAIRS, REACH, piece, width),
        held[5],
        from_core,
        specs=[HB, VM],
        scratch=[pltpu.SemaphoreType.DMA],
    )
    kept = [kept] + [from_shot(kept, turn) for turn in range(1, shots)]
    injected = call(
        functools.partial(receiver_kernel, across),
        "receivers",
        shape(STEPS, rows * across, width),
        receiver_cell,
        residual[0],
    )

    gram = call(gram_kernel, "gram", shape(len(PRODUCTS), 8, width), history)

    laps, adjs = [], []
    for moment in range(STEPS - 1):
        lap, new_wave, new_adj, new_prod = call(
            functools.partial(local_kernel, moment),
            f"local_{moment}",
            [slab, padded, slab, padded],
            source_cell,
            wavelet,
            wave,
            wave_old,
            prod,
            adj,
            adj_old,
            cour,
            injected,
            *bands,
            *([gram] if moment == STEPS - 2 else []),
            specs=[SM, SM] + [VM] * (10 if moment == STEPS - 2 else 9),
            scratch=[block] * 2,
        )
        sends = []
        for chip, came in ((False, from_core), (True, from_chip)):
            lap, new_wave, new_adj, new_prod, send = call(
                functools.partial(join_kernel, chip),
                f"join_{'chip' if chip else 'core'}_{moment}",
                [slab, padded, slab, padded, halo],
                came,
                cour,
                lap,
                new_wave,
                new_adj,
                new_prod,
                aliases={2: 0, 3: 1, 4: 2, 5: 3},
            )
            sends.append(send)
        from_core = swap_core(sends[0])
        from_chip = swap_chip(sends[1])
        laps.append(lap)
        adjs.append(new_adj)
        wave_old, wave = wave, new_wave
        adj_old, adj = adj, new_adj
        prod = new_prod

    scale = 1.0 / (shots * STEPS)
    inner_count, near_count = rows - 2 * REACH, rows - REACH
    last = (wave, prod, adj, adj_old, injected, *bands, laps[0], laps[1], laps[2], adjs[0], adjs[1])

    def sum_parts(values):
        return [values[0]] + [from_shot(values[shots - turn], turn) for turn in range(1, shots)]

    def some_rows(count, copies):
        return [pltpu.VMEM((count, across, width), F32)] * copies

    core = call(
        functools.partial(core_kernel, scale),
        "core",
        [shape(REACH, piece, width)] * shots,
        from_core,
        *last,
        scratch=some_rows(REACH, 3),
    )
    inner = call(
        functools.partial(inner_kernel, scale),
        "inner",
        [shape(inner_count, piece, width)] * shots,
        core[0],
        *last,
        scratch=some_rows(inner_count, 3),
    )
    core, inner = sum_parts(core), sum_parts(inner)
    chip_part = shape(REACH, across, width)
    known, lap, new_adj = call(chip_kernel, "chip", [chip_part] * 3, *last, *kept[1:], scratch=some_rows(REACH, 2))
    chip = call(
        functools.partial(last_join_kernel, scale),
        "last_join",
        chip_part,
        from_chip,
        known,
        lap,
        new_adj,
        laps[0],
        adjs[0],
        *core[1:],
    )
    others = [from_shot(chip, turn) for turn in range(1, shots)]
    chip_dots = call(
        functools.partial(chip_dots_kernel, shots),
        "chip_dots",
        shape(2 * PAIRS, 8, width),
        chip,
        *kept,
        *inner[1:],
    )
    near = shape(near_count, piece, width)
    line, near_grad = call(
        functools.partial(line_kernel, shots),
        "line",
        [shape(devices, 128), near],
        chip_dots,
        gram,
        history,
        *inner,
        *core,
    )
    lines = lax.all_to_all(line, ("depth", "shot"), 0, 0, tiled=True)
    weight, move = call(
        weights_kernel,
        "weights",
        [shape(1 + 2 * PAIRS, 8, width), near],
        lines,
        near_grad,
        history,
        *others,
    )
    moves = [from_shot(move, turn) for turn in range(1, shots)]
    own = shape(rows, piece, width)
    gradient, direction, courant_next = call(
        functools.partial(finish_kernel, shots),
        "finish",
        [own, own, slab],
        weight,
        courant,
        near_grad,
        move,
        chip,
        *others,
        *kept,
    )
    courant_next = call(
        functools.partial(last_piece_kernel, shots),
        "last_piece",
        slab,
        courant,
        courant_next,
        *moves,
        specs=[VM, HB] + [VM] * (shots - 1),
        out_specs=HB,
        aliases={1: 0},
        scratch=[
            pltpu.VMEM((shots - 1, near_count, piece, width), F32),
            pltpu.SemaphoreType.DMA((shots - 1,)),
        ],
    )
    return gradient, direction, courant_next


def solution(mesh):
    return jax.shard_map(
        per_device,
        mesh=mesh,
        in_specs=(
            P("depth", None, None),
            P("shot", "depth", None, None),
            P("shot", "depth", None, None),
            P("shot", "depth", None, None),
            P("shot", "depth", None, None),
            P("shot"),
            P("shot", None),
            P("shot", None),
            P("shot", None, None),
            P(None, None, "depth", "shot", None),
        ),
        out_specs=(P("depth", "shot", None), P("depth", "shot", None), P("depth", None, None)),
        check_vma=False,
    )
```

```python
import functools

import jax
import jax.numpy as jnp
from jax import lax
from jax.experimental import pallas as pl
from jax.experimental.pallas import tpu as pltpu
from jax.sharding import PartitionSpec as P

STEPS = 4
PAIRS = 5
REACH = 4
PAD = 8
GROUP = 8
CHUNK = 16
coefficients = (-205.0 / 72.0, 8.0 / 5.0, -1.0 / 5.0, 8.0 / 315.0, -1.0 / 560.0)

F32 = jnp.float32
VM = pl.BlockSpec(memory_space=pltpu.VMEM)
SM = pl.BlockSpec(memory_space=pltpu.SMEM)
HB = pl.BlockSpec(memory_space=pltpu.HBM)
PARAMS = pltpu.CompilerParams(vmem_limit_bytes=16 << 20)


def in_hbm(value):
    return pltpu.with_memory_space_constraint(value, pltpu.HBM)


def shape(*dims):
    return jax.ShapeDtypeStruct(dims, F32)


def natural_row(row, rows, odd):
    return jnp.where(odd == 1, rows - 1 - row, row)


def odd_depth():
    return lax.rem(lax.axis_index("depth"), 2)


def lane_ids(width):
    return lax.broadcasted_iota(jnp.int32, (1, width), 1)


def split3(value):
    high = value.astype(jnp.bfloat16)
    left = value - high.astype(F32)
    middle = left.astype(jnp.bfloat16)
    return high, middle, (left - middle.astype(F32)).astype(jnp.bfloat16)


def band_parts(width):
    apart = jnp.abs(
        lax.broadcasted_iota(jnp.int32, (width, width), 0) - lax.broadcasted_iota(jnp.int32, (width, width), 1)
    )
    band = jnp.zeros((width, width), F32)
    for reach in range(1, REACH + 1):
        band = band + jnp.where(apart == reach, coefficients[reach], 0.0)
    high, middle, low = split3(band)
    pair = jnp.concatenate([high, middle], axis=1)
    return jnp.concatenate([pair, pair], axis=0), jnp.concatenate([high, low], axis=0)


def along_last(ref, which, wide_band, tall_band, out):
    width = ref.shape[2]
    across = ref.shape[1] - 2 * PAD
    for first in range(0, len(which), GROUP):
        group = which[first : first + GROUP]
        cells = jnp.concatenate([ref[row, PAD : PAD + across, :] for row in group], axis=0)
        high, middle, low = split3(cells)
        large = jnp.dot(jnp.concatenate([high, middle], axis=1), wide_band, preferred_element_type=F32)
        small = jnp.dot(jnp.concatenate([low, high], axis=1), tall_band, preferred_element_type=F32)
        total = large[:, :width] + (large[:, width:] + small)
        for n in range(len(group)):
            out[first + n] = total[n * across : (n + 1) * across]


def laplace_chunk(ref, row, start, size, along):
    rows = ref.shape[0]
    total = along + (3.0 * coefficients[0]) * ref[row, PAD + start : PAD + start + size, :]
    for reach in range(1, REACH + 1):
        near = (
            ref[row, PAD + start + reach : PAD + start + reach + size, :]
            + ref[row, PAD + start - reach : PAD + start - reach + size, :]
        )
        if row - reach >= 0:
            near = near + ref[row - reach, PAD + start : PAD + start + size, :]
        if row + reach < rows:
            near = near + ref[row + reach, PAD + start : PAD + start + size, :]
        total = total + coefficients[reach] * near
    return total


def zero_pads(ref):
    rows, padded, width = ref.shape
    for row in range(rows):
        ref[row, :PAD, :] = jnp.zeros((PAD, width), F32)
        ref[row, padded - PAD :, :] = jnp.zeros((PAD, width), F32)


def first_send_kernel(wave, adjoint, courant, to_chip, to_core, b_wave, b_adj, b_cour, sems):
    rows = courant.shape[0]
    odd = odd_depth()
    copies = []
    for which, start in enumerate((odd * (rows - REACH), (1 - odd) * (rows - REACH))):
        for n, (src, dst) in enumerate([(wave, b_wave), (adjoint, b_adj), (courant, b_cour)]):
            copies.append(pltpu.make_async_copy(src.at[pl.ds(start, REACH)], dst.at[which], sems.at[3 * which + n]))
    for copy in copies:
        copy.start()
    for copy in copies:
        copy.wait()
    for which, send in enumerate((to_chip, to_core)):
        for row in range(REACH):
            src = natural_row(row, REACH, odd)
            send[row] = b_wave[which, src]
            send[REACH + row] = b_cour[which, src] * b_adj[which, src]


def stage_kernel(
    wave,
    wave_old,
    adjoint,
    adjoint_old,
    courant,
    o_wave,
    o_wave_old,
    o_adj,
    o_adj_old,
    o_cour,
    o_prod,
    o_wide,
    o_tall,
    b_wave,
    b_wave_old,
    b_adj,
    b_adj_old,
    b_cour,
    sems,
):
    rows, across, width = courant.shape
    fetched = [(wave, b_wave), (adjoint, b_adj), (courant, b_cour), (wave_old, b_wave_old), (adjoint_old, b_adj_old)]
    copies = [pltpu.make_async_copy(src, dst, sems.at[n]) for n, (src, dst) in enumerate(fetched)]
    for copy in copies:
        copy.start()
    zero_pads(o_wave)
    zero_pads(o_wave_old)
    zero_pads(o_prod)
    o_wide[...], o_tall[...] = band_parts(width)
    odd = odd_depth()
    for copy in copies[:3]:
        copy.wait()
    for row in range(rows):
        src = natural_row(row, rows, odd)
        now, adj, cour = b_wave[src], b_adj[src], b_cour[src]
        prod = cour * adj
        o_wave[row, PAD : PAD + across, :] = now
        o_adj[row] = adj
        o_cour[row] = cour
        o_prod[row, PAD : PAD + across, :] = prod
    for copy in copies[3:]:
        copy.wait()
    for row in range(rows):
        src = natural_row(row, rows, odd)
        o_wave_old[row, PAD : PAD + across, :] = b_wave_old[src]
        o_adj_old[row] = b_adj_old[src]


def keep_kernel(history, _, out, sem):
    start = odd_depth() * (history.shape[2] - REACH)
    copy = pltpu.make_async_copy(history.at[:, :, pl.ds(start, REACH)], out, sem)
    copy.start()
    copy.wait()


def split_cell(cell, rows, across, width):
    depth_row = cell // (across * width) - lax.axis_index("depth") * rows
    rest = cell % (across * width)
    inside = (depth_row >= 0) & (depth_row < rows)
    row = jnp.where(odd_depth() == 1, rows - 1 - depth_row, depth_row)
    return inside, row, rest // width, rest % width


def receiver_kernel(across, receivers, residual, out):
    cells = out.shape[1]
    width = out.shape[2]
    count = receivers.shape[1]
    inside, row, place, lane = split_cell(receivers[...], cells // across, across, width)
    keys = jnp.where(inside, row * across + place, -1)
    hot = (lax.broadcasted_iota(jnp.int32, (cells, count), 0) == keys).astype(jnp.bfloat16)
    lanes = lax.broadcasted_iota(jnp.int32, (width, count), 0) == lane
    for moment in range(STEPS):
        value = jnp.where(lanes, residual[moment : moment + 1, :], 0.0)
        high = value.astype(jnp.bfloat16)
        left = value - high.astype(F32)
        middle = left.astype(jnp.bfloat16)
        low = (left - middle.astype(F32)).astype(jnp.bfloat16)
        pieces = [
            lax.dot_general(hot, piece, (((1,), (1,)), ((), ())), preferred_element_type=F32)
            for piece in (low, middle, high)
        ]
        out[moment] = (pieces[0] + pieces[1]) + pieces[2]


def local_kernel(
    moment, cell, wavelet, wave, wave_old, prod, adj, adj_old, courant, injected, wide_band, tall_band, *outs
):
    o_lap, o_wave, o_adj, o_prod, along_wave, along_prod = outs[-6:]
    rows, across, width = adj.shape
    along_last(wave, list(range(rows)), wide_band[...], tall_band[...], along_wave)
    along_last(prod, list(range(rows)), wide_band[...], tall_band[...], along_prod)
    zero_pads(o_wave)
    zero_pads(o_prod)
    for row in range(rows):
        for start in range(0, across, CHUNK):
            part = (row, pl.ds(start, CHUNK), slice(None))
            wide = (row, pl.ds(PAD + start, CHUNK), slice(None))
            lap = laplace_chunk(wave, row, start, CHUNK, along_wave[part])
            o_lap[part] = lap
            o_wave[wide] = 2.0 * wave[wide] - wave_old[wide] + courant[part] * lap
            new = 2.0 * adj[part] - adj_old[part] + laplace_chunk(prod, row, start, CHUNK, along_prod[part])
            new = new + injected[STEPS - 1 - moment, row * across + start : row * across + start + CHUNK, :]
            o_adj[part] = new
            o_prod[wide] = courant[part] * new
    inside, row, place, lane = split_cell(cell[0], rows, across, width)

    @pl.when(inside)
    def _():
        spot = (row, pl.ds(PAD + place, 1), slice(None))
        o_wave[spot] = o_wave[spot] + jnp.where(lane_ids(width) == lane, wavelet[0, moment], 0.0)


def chip_terms(ref, field):
    for place in range(REACH):
        term = None
        for reach in range(place + 1, REACH + 1):
            one = coefficients[reach] * ref[field * REACH + reach - place - 1]
            term = one if term is None else term + one
        yield place, term


def core_terms(ref, field, rows):
    for place in range(REACH):
        term = None
        for reach in range(place + 1, REACH + 1):
            one = coefficients[reach] * ref[field * REACH + REACH - reach + place]
            term = one if term is None else term + one
        yield rows - 1 - place, term


def join_kernel(chip, halo, courant, lap, wave, adj, prod, o_lap, o_wave, o_adj, o_prod, send):
    rows, across, width = adj.shape
    inner = slice(PAD, PAD + across)
    first = 0 if chip else rows - REACH
    for row, term in chip_terms(halo, 0) if chip else core_terms(halo, 0, rows):
        o_lap[row] = lap[row] + term
        new = wave[row, inner, :] + courant[row] * term
        o_wave[row, inner, :] = new
        send[row - first] = new
    for row, term in chip_terms(halo, 1) if chip else core_terms(halo, 1, rows):
        new = adj[row] + term
        o_adj[row] = new
        new = courant[row] * new
        o_prod[row, inner, :] = new
        send[REACH + row - first] = new


def last_rows(which, wave, prod, adj, adj_old, injected, wide_band, tall_band, along_wave, along_prod):
    across = adj.shape[1]
    along_last(wave, which, wide_band[...], tall_band[...], along_wave)
    along_last(prod, which, wide_band[...], tall_band[...], along_prod)
    for place, row in enumerate(which):
        for start in range(0, across, CHUNK):
            part = (row, pl.ds(start, CHUNK), slice(None))
            put = (place, pl.ds(start, CHUNK), slice(None))
            lap = laplace_chunk(wave, row, start, CHUNK, along_wave[put])
            new = 2.0 * adj[part] - adj_old[part] + laplace_chunk(prod, row, start, CHUNK, along_prod[put])
            new = new + injected[0, row * across + start : row * across + start + CHUNK, :]
            yield place, row, start, part, lap, new


def lay_pieces(full, outs):
    count = len(outs)
    piece = full.shape[1] // count
    for turn, out in enumerate(outs):
        offset = lax.rem(lax.axis_index("shot") + turn, count) * piece
        for place in range(full.shape[0]):
            out[place] = full[place, pl.ds(pl.multiple_of(offset, 8), piece), :]


def known_terms(part, adj, lap2, lap3, adj3):
    return adj[part] * lap2[part] + adj3[part] * lap3[part]


def gradient_rows(scale, which, first, full, wave, prod, adj, adj_old, injected, wide, tall, lap1, lap2, lap3, adj4, adj3, along):
    for place, row, start, part, lap, new in last_rows(which, wave, prod, adj, adj_old, injected, wide, tall, *along):
        known = known_terms(part, adj, lap2, lap3, adj3)
        full[first + place, start : start + CHUNK, :] = scale * (known + adj4[part] * lap + new * lap1[part])


def join_far_kernel(
    scale, halo, courant, lap, wave, adj, prod, adj_old, injected, wide, tall, lap1, lap2, adj4, *refs
):
    joined, full, along = refs[:5], refs[5], refs[6:]
    join_kernel(False, halo, courant, lap, wave, adj, prod, *joined)
    o_lap, o_wave, o_adj, o_prod = joined[:4]
    which = list(range(2 * REACH, courant.shape[0] - REACH))
    gradient_rows(
        scale, which, 0, full, o_wave, o_prod, o_adj, adj_old, injected, wide, tall, lap1, lap2, o_lap, adj4, adj_old, along
    )


def inner_kernel(scale, _, far, wave, prod, adj, adj_old, injected, wide, tall, lap1, lap2, lap3, adj4, adj3, *outs):
    full, along = outs[-3], outs[-2:]
    which = list(range(REACH, 2 * REACH))
    for place in range(far.shape[0]):
        full[REACH + place] = far[place]
    gradient_rows(
        scale, which, 0, full, wave, prod, adj, adj_old, injected, wide, tall, lap1, lap2, lap3, adj4, adj3, along
    )
    lay_pieces(full, outs[:-3])


def core_kernel(
    scale, from_core, wave, prod, adj, adj_old, injected, wide, tall, lap1, lap2, lap3, adj4, adj3, *outs
):
    full, along = outs[-3], outs[-2:]
    rows = adj.shape[0]
    waves = dict(core_terms(from_core, 0, rows))
    adjs = dict(core_terms(from_core, 1, rows))
    which = list(range(rows - REACH, rows))
    for place, row, start, part, lap, new in last_rows(which, wave, prod, adj, adj_old, injected, wide, tall, *along):
        known = known_terms(part, adj, lap2, lap3, adj3)
        lap = lap + waves[row][start : start + CHUNK]
        new = new + adjs[row][start : start + CHUNK]
        full[place, start : start + CHUNK, :] = scale * (known + adj4[part] * lap + new * lap1[part])
    lay_pieces(full, outs[:-3])


def chip_kernel(wave, prod, adj, adj_old, injected, wide, tall, lap1, lap2, lap3, adj4, adj3, *refs):
    o_known, o_lap, o_adj, *along = refs[-5:]
    which = list(range(REACH))
    for place, row, start, part, lap, new in last_rows(which, wave, prod, adj, adj_old, injected, wide, tall, *along):
        o_known[part] = known_terms(part, adj, lap2, lap3, adj3)
        o_lap[part] = lap
        o_adj[part] = new


def last_join_kernel(scale, from_chip, known, lap, adj, lap1, adj4, *refs):
    o_grad = refs[-1]
    waves = dict(chip_terms(from_chip, 0))
    adjs = dict(chip_terms(from_chip, 1))
    for row in range(REACH):
        last_lap = lap[row] + waves[row]
        last_adj = adj[row] + adjs[row]
        o_grad[row] = scale * (known[row] + adj4[row] * last_lap + last_adj * lap1[row])


def fold(value):
    total = value[:8]
    for start in range(8, value.shape[0], 8):
        total = total + value[start : start + 8]
    return total


PRODUCTS = [(0, a, 1, b) for a in range(PAIRS) for b in range(a, PAIRS)] + [
    (1, a, 1, b) for a in range(PAIRS) for b in range(a, PAIRS)
]
SLOT = {key: PRODUCTS.index(key) for key in PRODUCTS}
FIRST_DOT = len(PRODUCTS)


def gram_kernel(history, out):
    pairs, rows, piece = history.shape[1], history.shape[2], history.shape[3]
    width = history.shape[4]
    for group in range(0, len(PRODUCTS), 10):
        members = PRODUCTS[group : group + 10]

        def body(row, sums, members=members):
            new = list(sums)
            for start in range(0, piece, 8):
                part = {}
                for a, i, b, j in members:
                    for key in ((a, i), (b, j)):
                        if key not in part:
                            part[key] = history[key[0], key[1], row, start : start + 8, :]
                for n, (a, i, b, j) in enumerate(members):
                    new[n] = new[n] + part[a, i] * part[b, j]
            return tuple(new)

        sums = lax.fori_loop(0, rows, body, tuple(jnp.zeros((8, width), F32) for _ in members))
        for n in range(len(members)):
            out[group + n] = sums[n]


def inner_rows(rows):
    return list(range(REACH, rows - REACH))


def near_rows(rows):
    return list(range(REACH, rows))


def add_dots(sums, values, history, row):
    for kind in range(2):
        for pair in range(PAIRS):
            n = kind * PAIRS + pair
            sums[n] = sums[n] + fold(history[kind, pair, row] * values)


def chip_dots_kernel(count, grad, *refs):
    pieces, out = refs[:count], refs[-1]
    total, piece = grad.shape[0], pieces[0].shape[3]
    odd = odd_depth()
    sums = [jnp.zeros((8, grad.shape[2]), F32) for _ in range(2 * PAIRS)]
    for place in range(total):
        source = natural_row(place, total, odd)
        for turn, ref in enumerate(pieces):
            offset = lax.rem(lax.axis_index("shot") + turn, count) * piece
            values = grad[place, pl.ds(pl.multiple_of(offset, 8), piece), :]
            add_dots(sums, values, ref, source)
    for n in range(2 * PAIRS):
        out[n] = sums[n]


def line_kernel(count, chip, gram, history, *refs):
    inner, core, out, o_near = refs[:count], refs[count : 2 * count], refs[-2], refs[-1]
    rows = history.shape[2]
    odd = odd_depth()
    sums = [chip[n] for n in range(2 * PAIRS)]
    for place, row in enumerate(near_rows(rows)):
        parts, at = (inner, place) if place < inner[0].shape[0] else (core, place - inner[0].shape[0])
        values = parts[0][at]
        for other in parts[1:]:
            values = values + other[at]
        o_near[place] = values
        add_dots(sums, values, history, natural_row(row, rows, odd))
    lane = lane_ids(out.shape[1])
    line = jnp.zeros((1, out.shape[1]), F32)
    for n in range(FIRST_DOT + 2 * PAIRS):
        value = gram[n] if n < FIRST_DOT else sums[n - FIRST_DOT]
        line = line + jnp.where(lane == n, jnp.sum(value, axis=(0, 1), keepdims=True), 0.0)
    out[...] = jnp.broadcast_to(line, out.shape)


def weights(line):
    lane = lane_ids(line.shape[1])

    def number(n):
        return jnp.sum(jnp.where(lane == n, line, 0.0), axis=(0, 1), keepdims=True)

    values = [number(n) for n in range(FIRST_DOT + 2 * PAIRS)]

    def sy(a, b):
        return values[SLOT[0, a, 1, b]]

    def yy(a, b):
        return values[SLOT[1, min(a, b), 1, max(a, b)]]

    s_grad = values[FIRST_DOT : FIRST_DOT + PAIRS]
    y_grad = values[FIRST_DOT + PAIRS :]
    rho = [1.0 / sy(i, i) for i in range(PAIRS)]
    alpha = [None] * PAIRS
    for i in reversed(range(PAIRS)):
        dot = s_grad[i]
        for j in range(PAIRS - 1, i, -1):
            dot = dot - alpha[j] * sy(i, j)
        alpha[i] = rho[i] * dot
    scale = sy(PAIRS - 1, PAIRS - 1) / yy(PAIRS - 1, PAIRS - 1)
    s_weight = [None] * PAIRS
    for i in range(PAIRS):
        dot = y_grad[i]
        for j in range(PAIRS):
            dot = dot - alpha[j] * yy(i, j)
        dot = scale * dot
        for j in range(i):
            dot = dot + s_weight[j] * sy(j, i)
        s_weight[i] = alpha[i] - rho[i] * dot
    return scale, [-(scale * a) for a in alpha], s_weight


def weights_kernel(lines, near, history, *refs):
    o_weights, o_move = refs[-2:]
    rows = history.shape[2]
    piece, width = near.shape[1], near.shape[2]
    odd = odd_depth()
    total = lines[0:8]
    for start in range(8, lines.shape[0], 8):
        total = total + lines[start : start + 8]
    scale, y_weight, s_weight = weights(jnp.sum(total, axis=0, keepdims=True))
    wide = [jnp.broadcast_to(v, (8, width)) for v in [scale] + s_weight + y_weight]
    for n, value in enumerate(wide):
        o_weights[n] = value
    for place, row in enumerate(near_rows(rows)):
        source = natural_row(row, rows, odd)
        for start in range(0, piece, 8):
            at = slice(start, start + 8)
            o_move[place, at, :] = move_of(wide, near[place, at, :], history, source, at)


def move_of(wide, grad, history, row, at):
    move = wide[0] * grad
    for pair in range(PAIRS):
        move = move + wide[1 + pair] * history[0, pair, row, at, :]
        move = move + wide[1 + PAIRS + pair] * history[1, pair, row, at, :]
    return -move


def finish_kernel(count, weight, courant, near, near_move, chip, *refs):
    others, pieces = refs[: count - 1], refs[count - 1 : 2 * count - 1]
    o_grad, o_direction, o_next = refs[2 * count - 1 :]
    rows, across, width = courant.shape
    piece = across // count
    odd = odd_depth()
    wide = [weight[n] for n in range(1 + 2 * PAIRS)]
    mine = pl.ds(pl.multiple_of(lax.axis_index("shot") * piece, 8), piece)
    for place, row in enumerate(near_rows(rows)):
        source = natural_row(row, rows, odd)
        o_grad[source] = near[place]
        o_direction[source] = near_move[place]
        o_next[source, mine, :] = courant[source, mine, :] + 0.05 * near_move[place]
    for row in range(REACH):
        source = natural_row(row, rows, odd)
        kept = natural_row(row, REACH, odd)
        for turn, ref in enumerate(pieces):
            offset = lax.rem(lax.axis_index("shot") + turn, count) * piece
            for start in range(0, piece, 8):
                at = pl.ds(pl.multiple_of(offset + start, 8), 8)
                grad = chip[row, at, :]
                for other in others:
                    grad = grad + other[row, at, :]
                move = move_of(wide, grad, ref, kept, slice(start, start + 8))
                if turn == 0:
                    o_grad[source, start : start + 8, :] = grad
                    o_direction[source, start : start + 8, :] = move
                o_next[source, at, :] = courant[source, at, :] + 0.05 * move


def last_piece_kernel(count, courant, done, *refs):
    moves, o_next, buffer, sem = refs[: count - 1], refs[-3], refs[-2], refs[-1]
    rows, across, width = courant.shape
    piece = across // count
    odd = odd_depth()
    first = (1 - odd) * REACH
    copies = []
    for turn in range(1, count):
        offset = pl.multiple_of(lax.rem(lax.axis_index("shot") + turn, count) * piece, 8)
        for place, row in enumerate(near_rows(rows)):
            source = natural_row(row, rows, odd)
            value = courant[source, pl.ds(offset, piece), :] + 0.05 * moves[turn - 1][place]
            buffer[turn - 1, source - first] = value
        copies.append(
            pltpu.make_async_copy(
                buffer.at[turn - 1],
                o_next.at[pl.ds(first, rows - REACH), pl.ds(offset, piece)],
                sem.at[turn - 1],
            )
        )
        copies[-1].start()
    for copy in copies:
        copy.wait()


def call(
    kernel, name, outs, *args, specs=None, out_specs=None, aliases=None, scratch=(), cost=1 << 20
):
    return pl.pallas_call(
        kernel,
        name=name,
        out_shape=outs,
        in_specs=specs or [VM] * len(args),
        out_specs=out_specs or jax.tree.map(lambda _: VM, outs),
        input_output_aliases=aliases or {},
        scratch_shapes=list(scratch),
        compiler_params=PARAMS,
        cost_estimate=pl.CostEstimate(flops=cost, bytes_accessed=cost, transcendentals=0),
    )(*args)


def per_device(
    courant,
    wave_before,
    wave_current,
    adjoint_after,
    adjoint_current,
    source_cell,
    wavelet,
    receiver_cell,
    residual,
    history,
):
    rows, across, width = courant.shape
    depths = lax.axis_size("depth")
    shots = lax.axis_size("shot")
    devices = depths * shots
    piece = across // shots
    slab = shape(rows, across, width)
    padded = shape(rows, across + 2 * PAD, width)
    halo = shape(2 * REACH, across, width)
    on_chip = [(i, i ^ 1) for i in range(depths)]
    off_chip = [(i, i + 1 if i % 2 else i - 1) for i in range(1, depths - 1)]

    def swap_core(value):
        return lax.ppermute(value, "depth", on_chip)

    def swap_chip(value):
        return lax.ppermute(value, "depth", off_chip)

    def from_shot(value, turn):
        return lax.ppermute(value, "shot", [((i + turn) % shots, i) for i in range(shots)])

    block = pltpu.VMEM((rows, across, width), F32)
    held = [
        in_hbm(value)
        for value in (wave_current[0], wave_before[0], adjoint_current[0], adjoint_after[0], courant, history)
    ]
    bands = [jax.ShapeDtypeStruct((2 * width, n * width), jnp.bfloat16) for n in (2, 1)]
    outer_rows = pltpu.VMEM((2, REACH, across, width), F32)
    to_chip, to_core = call(
        first_send_kernel,
        "first_send",
        [halo, halo],
        held[0],
        held[2],
        held[4],
        specs=[HB] * 3,
        scratch=[outer_rows] * 3 + [pltpu.SemaphoreType.DMA((6,))],
    )
    from_chip = swap_chip(to_chip)
    from_core = swap_core(to_core)
    wave, wave_old, adj, adj_old, cour, prod, *bands = call(
        stage_kernel,
        "stage",
        [padded, padded, slab, slab, slab, padded] + bands,
        *held[:5],
        specs=[HB] * 5,
        scratch=[block] * 5 + [pltpu.SemaphoreType.DMA((5,))],
    )
    kept = call(
        keep_kernel,
        "keep",
        shape(2, PAIRS, REACH, piece, width),
        held[5],
        from_core,
        specs=[HB, VM],
        scratch=[pltpu.SemaphoreType.DMA],
    )
    kept = [kept] + [from_shot(kept, turn) for turn in range(1, shots)]
    injected = call(
        functools.partial(receiver_kernel, across),
        "receivers",
        shape(STEPS, rows * across, width),
        receiver_cell,
        residual[0],
    )

    gram = call(gram_kernel, "gram", shape(len(PRODUCTS), 8, width), history)

    scale = 1.0 / (shots * STEPS)

    def some_rows(count, copies):
        return [pltpu.VMEM((count, across, width), F32)] * copies

    laps, adjs = [], []
    for moment in range(STEPS - 1):
        lap, new_wave, new_adj, new_prod = call(
            functools.partial(local_kernel, moment),
            f"local_{moment}",
            [slab, padded, slab, padded],
            source_cell,
            wavelet,
            wave,
            wave_old,
            prod,
            adj,
            adj_old,
            cour,
            injected,
            *bands,
            *([gram] if moment == STEPS - 2 else []),
            specs=[SM, SM] + [VM] * (10 if moment == STEPS - 2 else 9),
            scratch=[block] * 2,
        )
        sends = []
        for chip, came in ((False, from_core), (True, from_chip)):
            arrays = (came, cour, lap, new_wave, new_adj, new_prod)
            if moment == STEPS - 2 and not chip:
                lap, new_wave, new_adj, new_prod, send, far = call(
                    functools.partial(join_far_kernel, scale),
                    "join_far",
                    [slab, padded, slab, padded, halo, shape(rows - 3 * REACH, across, width)],
                    *arrays,
                    adj,
                    injected,
                    *bands,
                    *laps,
                    adjs[0],
                    aliases={2: 0, 3: 1, 4: 2, 5: 3},
                    scratch=some_rows(rows - 3 * REACH, 2),
                )
            else:
                lap, new_wave, new_adj, new_prod, send = call(
                    functools.partial(join_kernel, chip),
                    f"join_{'chip' if chip else 'core'}_{moment}",
                    [slab, padded, slab, padded, halo],
                    *arrays,
                    aliases={2: 0, 3: 1, 4: 2, 5: 3},
                )
            sends.append(send)
        from_core = swap_core(sends[0])
        from_chip = swap_chip(sends[1])
        laps.append(lap)
        adjs.append(new_adj)
        wave_old, wave = wave, new_wave
        adj_old, adj = adj, new_adj
        prod = new_prod

    inner_count, near_count = rows - 2 * REACH, rows - REACH
    last = (wave, prod, adj, adj_old, injected, *bands, laps[0], laps[1], laps[2], adjs[0], adjs[1])

    def sum_parts(values):
        return [values[0]] + [from_shot(values[shots - turn], turn) for turn in range(1, shots)]

    core = call(
        functools.partial(core_kernel, scale),
        "core",
        [shape(REACH, piece, width)] * shots,
        from_core,
        *last,
        scratch=some_rows(REACH, 3),
    )
    inner = call(
        functools.partial(inner_kernel, scale),
        "inner",
        [shape(inner_count, piece, width)] * shots,
        core[0],
        far,
        *last,
        scratch=some_rows(inner_count, 1) + some_rows(REACH, 2),
    )
    core, inner = sum_parts(core), sum_parts(inner)
    chip_part = shape(REACH, across, width)
    known, lap, new_adj = call(chip_kernel, "chip", [chip_part] * 3, *last, *kept[1:], scratch=some_rows(REACH, 2))
    chip = call(
        functools.partial(last_join_kernel, scale),
        "last_join",
        chip_part,
        from_chip,
        known,
        lap,
        new_adj,
        laps[0],
        adjs[0],
        *core[1:],
    )
    others = [from_shot(chip, turn) for turn in range(1, shots)]
    chip_dots = call(
        functools.partial(chip_dots_kernel, shots),
        "chip_dots",
        shape(2 * PAIRS, 8, width),
        chip,
        *kept,
        *inner[1:],
    )
    near = shape(near_count, piece, width)
    line, near_grad = call(
        functools.partial(line_kernel, shots),
        "line",
        [shape(devices, 128), near],
        chip_dots,
        gram,
        history,
        *inner,
        *core,
    )
    lines = lax.all_to_all(line, ("depth", "shot"), 0, 0, tiled=True)
    weight, move = call(
        weights_kernel,
        "weights",
        [shape(1 + 2 * PAIRS, 8, width), near],
        lines,
        near_grad,
        history,
        *others,
    )
    moves = [from_shot(move, turn) for turn in range(1, shots)]
    own = shape(rows, piece, width)
    gradient, direction, courant_next = call(
        functools.partial(finish_kernel, shots),
        "finish",
        [own, own, slab],
        weight,
        courant,
        near_grad,
        move,
        chip,
        *others,
        *kept,
    )
    courant_next = call(
        functools.partial(last_piece_kernel, shots),
        "last_piece",
        slab,
        courant,
        courant_next,
        *moves,
        specs=[VM, HB] + [VM] * (shots - 1),
        out_specs=HB,
        aliases={1: 0},
        scratch=[
            pltpu.VMEM((shots - 1, near_count, piece, width), F32),
            pltpu.SemaphoreType.DMA((shots - 1,)),
        ],
    )
    return gradient, direction, courant_next


def solution(mesh):
    return jax.shard_map(
        per_device,
        mesh=mesh,
        in_specs=(
            P("depth", None, None),
            P("shot", "depth", None, None),
            P("shot", "depth", None, None),
            P("shot", "depth", None, None),
            P("shot", "depth", None, None),
            P("shot"),
            P("shot", None),
            P("shot", None),
            P("shot", None, None),
            P(None, None, "depth", "shot", None),
        ),
        out_specs=(P("depth", "shot", None), P("depth", "shot", None), P("depth", None, None)),
        check_vma=False,
    )
```

```python
import functools

import jax
import jax.numpy as jnp
from jax import lax
from jax.experimental import pallas as pl
from jax.experimental.pallas import tpu as pltpu
from jax.sharding import PartitionSpec as P

STEPS = 4
PAIRS = 5
REACH = 4
PAD = 8
GROUP = 8
CHUNK = 16
coefficients = (-205.0 / 72.0, 8.0 / 5.0, -1.0 / 5.0, 8.0 / 315.0, -1.0 / 560.0)

F32 = jnp.float32
VM = pl.BlockSpec(memory_space=pltpu.VMEM)
SM = pl.BlockSpec(memory_space=pltpu.SMEM)
HB = pl.BlockSpec(memory_space=pltpu.HBM)
PARAMS = pltpu.CompilerParams(vmem_limit_bytes=16 << 20)


def in_hbm(value):
    return pltpu.with_memory_space_constraint(value, pltpu.HBM)


def in_vmem(value):
    return pltpu.with_memory_space_constraint(value, pltpu.VMEM)


def shape(*dims):
    return jax.ShapeDtypeStruct(dims, F32)


def natural_row(row, rows, odd):
    return jnp.where(odd == 1, rows - 1 - row, row)


def odd_depth():
    return lax.rem(lax.axis_index("depth"), 2)


def lane_ids(width):
    return lax.broadcasted_iota(jnp.int32, (1, width), 1)


def split3(value):
    high = value.astype(jnp.bfloat16)
    left = value - high.astype(F32)
    middle = left.astype(jnp.bfloat16)
    return high, middle, (left - middle.astype(F32)).astype(jnp.bfloat16)


def band_parts(width):
    apart = jnp.abs(
        lax.broadcasted_iota(jnp.int32, (width, width), 0) - lax.broadcasted_iota(jnp.int32, (width, width), 1)
    )
    band = jnp.zeros((width, width), F32)
    for reach in range(1, REACH + 1):
        band = band + jnp.where(apart == reach, coefficients[reach], 0.0)
    high, middle, low = split3(band)
    pair = jnp.concatenate([high, middle], axis=1)
    return jnp.concatenate([pair, pair], axis=0), jnp.concatenate([high, low], axis=0)


def along_last(ref, which, wide_band, tall_band, out):
    width = ref.shape[2]
    across = ref.shape[1] - 2 * PAD
    for first in range(0, len(which), GROUP):
        group = which[first : first + GROUP]
        cells = jnp.concatenate([ref[row, PAD : PAD + across, :] for row in group], axis=0)
        high, middle, low = split3(cells)
        large = jnp.dot(jnp.concatenate([high, middle], axis=1), wide_band, preferred_element_type=F32)
        small = jnp.dot(jnp.concatenate([low, high], axis=1), tall_band, preferred_element_type=F32)
        total = large[:, :width] + (large[:, width:] + small)
        for n in range(len(group)):
            out[first + n] = total[n * across : (n + 1) * across]


def laplace_chunk(ref, row, start, size, along):
    rows = ref.shape[0]
    total = along + (3.0 * coefficients[0]) * ref[row, PAD + start : PAD + start + size, :]
    for reach in range(1, REACH + 1):
        near = (
            ref[row, PAD + start + reach : PAD + start + reach + size, :]
            + ref[row, PAD + start - reach : PAD + start - reach + size, :]
        )
        if row - reach >= 0:
            near = near + ref[row - reach, PAD + start : PAD + start + size, :]
        if row + reach < rows:
            near = near + ref[row + reach, PAD + start : PAD + start + size, :]
        total = total + coefficients[reach] * near
    return total


def zero_pads(ref):
    rows, padded, width = ref.shape
    for row in range(rows):
        ref[row, :PAD, :] = jnp.zeros((PAD, width), F32)
        ref[row, padded - PAD :, :] = jnp.zeros((PAD, width), F32)


def first_send_kernel(wave, adjoint, courant, to_chip, to_core, b_wave, b_adj, b_cour, sems):
    rows = courant.shape[0]
    odd = odd_depth()
    copies = []
    for which, start in enumerate((odd * (rows - REACH), (1 - odd) * (rows - REACH))):
        for n, (src, dst) in enumerate([(wave, b_wave), (adjoint, b_adj), (courant, b_cour)]):
            copies.append(pltpu.make_async_copy(src.at[pl.ds(start, REACH)], dst.at[which], sems.at[3 * which + n]))
    for copy in copies:
        copy.start()
    for copy in copies:
        copy.wait()
    for which, send in enumerate((to_chip, to_core)):
        for row in range(REACH):
            src = natural_row(row, REACH, odd)
            send[row] = b_wave[which, src]
            send[REACH + row] = b_cour[which, src] * b_adj[which, src]


def stage_kernel(
    wave,
    wave_old,
    adjoint,
    adjoint_old,
    courant,
    o_wave,
    o_wave_old,
    o_adj,
    o_adj_old,
    o_cour,
    o_prod,
    o_wide,
    o_tall,
    b_wave,
    b_wave_old,
    b_adj,
    b_adj_old,
    b_cour,
    sems,
):
    rows, across, width = courant.shape
    fetched = [(wave, b_wave), (adjoint, b_adj), (courant, b_cour), (wave_old, b_wave_old), (adjoint_old, b_adj_old)]
    copies = [pltpu.make_async_copy(src, dst, sems.at[n]) for n, (src, dst) in enumerate(fetched)]
    for copy in copies:
        copy.start()
    zero_pads(o_wave)
    zero_pads(o_wave_old)
    zero_pads(o_prod)
    o_wide[...], o_tall[...] = band_parts(width)
    odd = odd_depth()
    for copy in copies[:3]:
        copy.wait()
    for row in range(rows):
        src = natural_row(row, rows, odd)
        now, adj, cour = b_wave[src], b_adj[src], b_cour[src]
        prod = cour * adj
        o_wave[row, PAD : PAD + across, :] = now
        o_adj[row] = adj
        o_cour[row] = cour
        o_prod[row, PAD : PAD + across, :] = prod
    for copy in copies[3:]:
        copy.wait()
    for row in range(rows):
        src = natural_row(row, rows, odd)
        o_wave_old[row, PAD : PAD + across, :] = b_wave_old[src]
        o_adj_old[row] = b_adj_old[src]


def keep_kernel(history, _, out, sem):
    start = odd_depth() * (history.shape[2] - REACH)
    copy = pltpu.make_async_copy(history.at[:, :, pl.ds(start, REACH)], out, sem)
    copy.start()
    copy.wait()


def split_cell(cell, rows, across, width):
    depth_row = cell // (across * width) - lax.axis_index("depth") * rows
    rest = cell % (across * width)
    inside = (depth_row >= 0) & (depth_row < rows)
    row = jnp.where(odd_depth() == 1, rows - 1 - depth_row, depth_row)
    return inside, row, rest // width, rest % width


def receiver_kernel(across, receivers, residual, out):
    cells = out.shape[1]
    width = out.shape[2]
    count = receivers.shape[1]
    inside, row, place, lane = split_cell(receivers[...], cells // across, across, width)
    keys = jnp.where(inside, row * across + place, -1)
    hot = (lax.broadcasted_iota(jnp.int32, (cells, count), 0) == keys).astype(jnp.bfloat16)
    lanes = lax.broadcasted_iota(jnp.int32, (width, count), 0) == lane
    for moment in range(STEPS):
        value = jnp.where(lanes, residual[moment : moment + 1, :], 0.0)
        high = value.astype(jnp.bfloat16)
        left = value - high.astype(F32)
        middle = left.astype(jnp.bfloat16)
        low = (left - middle.astype(F32)).astype(jnp.bfloat16)
        pieces = [
            lax.dot_general(hot, piece, (((1,), (1,)), ((), ())), preferred_element_type=F32)
            for piece in (low, middle, high)
        ]
        out[moment] = (pieces[0] + pieces[1]) + pieces[2]


def local_kernel(
    moment, cell, wavelet, wave, wave_old, prod, adj, adj_old, courant, injected, wide_band, tall_band, *outs
):
    o_lap, o_wave, o_adj, o_prod, along_wave, along_prod = outs[-6:]
    rows, across, width = adj.shape
    along_last(wave, list(range(rows)), wide_band[...], tall_band[...], along_wave)
    along_last(prod, list(range(rows)), wide_band[...], tall_band[...], along_prod)
    zero_pads(o_wave)
    zero_pads(o_prod)
    for row in range(rows):
        for start in range(0, across, CHUNK):
            part = (row, pl.ds(start, CHUNK), slice(None))
            wide = (row, pl.ds(PAD + start, CHUNK), slice(None))
            lap = laplace_chunk(wave, row, start, CHUNK, along_wave[part])
            o_lap[part] = lap
            o_wave[wide] = 2.0 * wave[wide] - wave_old[wide] + courant[part] * lap
            new = 2.0 * adj[part] - adj_old[part] + laplace_chunk(prod, row, start, CHUNK, along_prod[part])
            new = new + injected[STEPS - 1 - moment, row * across + start : row * across + start + CHUNK, :]
            o_adj[part] = new
            o_prod[wide] = courant[part] * new
    inside, row, place, lane = split_cell(cell[0], rows, across, width)

    @pl.when(inside)
    def _():
        spot = (row, pl.ds(PAD + place, 1), slice(None))
        o_wave[spot] = o_wave[spot] + jnp.where(lane_ids(width) == lane, wavelet[0, moment], 0.0)


def chip_terms(ref, field):
    for place in range(REACH):
        term = None
        for reach in range(place + 1, REACH + 1):
            one = coefficients[reach] * ref[field * REACH + reach - place - 1]
            term = one if term is None else term + one
        yield place, term


def core_terms(ref, field, rows):
    for place in range(REACH):
        term = None
        for reach in range(place + 1, REACH + 1):
            one = coefficients[reach] * ref[field * REACH + REACH - reach + place]
            term = one if term is None else term + one
        yield rows - 1 - place, term


def join_kernel(chip, halo, courant, lap, wave, adj, prod, o_lap, o_wave, o_adj, o_prod, send):
    rows, across, width = adj.shape
    inner = slice(PAD, PAD + across)
    first = 0 if chip else rows - REACH
    for row, term in chip_terms(halo, 0) if chip else core_terms(halo, 0, rows):
        o_lap[row] = lap[row] + term
        new = wave[row, inner, :] + courant[row] * term
        o_wave[row, inner, :] = new
        send[row - first] = new
    for row, term in chip_terms(halo, 1) if chip else core_terms(halo, 1, rows):
        new = adj[row] + term
        o_adj[row] = new
        new = courant[row] * new
        o_prod[row, inner, :] = new
        send[REACH + row - first] = new


def last_rows(which, wave, prod, adj, adj_old, injected, wide_band, tall_band, along_wave, along_prod):
    across = adj.shape[1]
    along_last(wave, which, wide_band[...], tall_band[...], along_wave)
    along_last(prod, which, wide_band[...], tall_band[...], along_prod)
    for place, row in enumerate(which):
        for start in range(0, across, CHUNK):
            part = (row, pl.ds(start, CHUNK), slice(None))
            put = (place, pl.ds(start, CHUNK), slice(None))
            lap = laplace_chunk(wave, row, start, CHUNK, along_wave[put])
            new = 2.0 * adj[part] - adj_old[part] + laplace_chunk(prod, row, start, CHUNK, along_prod[put])
            new = new + injected[0, row * across + start : row * across + start + CHUNK, :]
            yield place, row, start, part, lap, new


def lay_pieces(full, outs):
    count = len(outs)
    piece = full.shape[1] // count
    for turn, out in enumerate(outs):
        offset = lax.rem(lax.axis_index("shot") + turn, count) * piece
        for place in range(full.shape[0]):
            out[place] = full[place, pl.ds(pl.multiple_of(offset, 8), piece), :]


def known_terms(part, adj, lap2, lap3, adj3):
    return adj[part] * lap2[part] + adj3[part] * lap3[part]


def gradient_rows(scale, which, first, full, wave, prod, adj, adj_old, injected, wide, tall, lap1, lap2, lap3, adj4, adj3, along):
    for place, row, start, part, lap, new in last_rows(which, wave, prod, adj, adj_old, injected, wide, tall, *along):
        known = known_terms(part, adj, lap2, lap3, adj3)
        full[first + place, start : start + CHUNK, :] = scale * (known + adj4[part] * lap + new * lap1[part])


def join_far_kernel(
    scale, halo, courant, lap, wave, adj, prod, adj_old, injected, wide, tall, lap1, lap2, adj4, *refs
):
    joined, full, along = refs[:5], refs[5], refs[6:]
    join_kernel(False, halo, courant, lap, wave, adj, prod, *joined)
    o_lap, o_wave, o_adj, o_prod = joined[:4]
    which = list(range(2 * REACH, courant.shape[0] - REACH))
    gradient_rows(
        scale, which, 0, full, o_wave, o_prod, o_adj, adj_old, injected, wide, tall, lap1, lap2, o_lap, adj4, adj_old, along
    )


def inner_kernel(scale, _, far, wave, prod, adj, adj_old, injected, wide, tall, lap1, lap2, lap3, adj4, adj3, *outs):
    full, along = outs[-3], outs[-2:]
    which = list(range(REACH, 2 * REACH))
    for place in range(far.shape[0]):
        full[REACH + place] = far[place]
    gradient_rows(
        scale, which, 0, full, wave, prod, adj, adj_old, injected, wide, tall, lap1, lap2, lap3, adj4, adj3, along
    )
    lay_pieces(full, outs[:-3])


def core_kernel(
    scale, from_core, wave, prod, adj, adj_old, injected, wide, tall, lap1, lap2, lap3, adj4, adj3, *outs
):
    full, along = outs[-3], outs[-2:]
    rows = adj.shape[0]
    waves = dict(core_terms(from_core, 0, rows))
    adjs = dict(core_terms(from_core, 1, rows))
    which = list(range(rows - REACH, rows))
    for place, row, start, part, lap, new in last_rows(which, wave, prod, adj, adj_old, injected, wide, tall, *along):
        known = known_terms(part, adj, lap2, lap3, adj3)
        lap = lap + waves[row][start : start + CHUNK]
        new = new + adjs[row][start : start + CHUNK]
        full[place, start : start + CHUNK, :] = scale * (known + adj4[part] * lap + new * lap1[part])
    lay_pieces(full, outs[:-3])


def chip_kernel(wave, prod, adj, adj_old, injected, wide, tall, lap1, lap2, lap3, adj4, adj3, *refs):
    o_known, o_lap, o_adj, *along = refs[-5:]
    which = list(range(REACH))
    for place, row, start, part, lap, new in last_rows(which, wave, prod, adj, adj_old, injected, wide, tall, *along):
        o_known[part] = known_terms(part, adj, lap2, lap3, adj3)
        o_lap[part] = lap
        o_adj[part] = new


def last_join_kernel(scale, from_chip, known, lap, adj, lap1, adj4, *refs):
    o_grad = refs[-1]
    waves = dict(chip_terms(from_chip, 0))
    adjs = dict(chip_terms(from_chip, 1))
    for row in range(REACH):
        last_lap = lap[row] + waves[row]
        last_adj = adj[row] + adjs[row]
        o_grad[row] = scale * (known[row] + adj4[row] * last_lap + last_adj * lap1[row])


def fold(value):
    total = value[:8]
    for start in range(8, value.shape[0], 8):
        total = total + value[start : start + 8]
    return total


PRODUCTS = [(0, a, 1, b) for a in range(PAIRS) for b in range(a, PAIRS)] + [
    (1, a, 1, b) for a in range(PAIRS) for b in range(a, PAIRS)
]
SLOT = {key: PRODUCTS.index(key) for key in PRODUCTS}
FIRST_DOT = len(PRODUCTS)


def gram_kernel(history, out):
    pairs, rows, piece = history.shape[1], history.shape[2], history.shape[3]
    width = history.shape[4]
    for group in range(0, len(PRODUCTS), 10):
        members = PRODUCTS[group : group + 10]

        def body(row, sums, members=members):
            new = list(sums)
            for start in range(0, piece, 8):
                part = {}
                for a, i, b, j in members:
                    for key in ((a, i), (b, j)):
                        if key not in part:
                            part[key] = history[key[0], key[1], row, start : start + 8, :]
                for n, (a, i, b, j) in enumerate(members):
                    new[n] = new[n] + part[a, i] * part[b, j]
            return tuple(new)

        sums = lax.fori_loop(0, rows, body, tuple(jnp.zeros((8, width), F32) for _ in members))
        for n in range(len(members)):
            out[group + n] = sums[n]


def inner_rows(rows):
    return list(range(REACH, rows - REACH))


def near_rows(rows):
    return list(range(REACH, rows))


def add_dots(sums, values, history, row):
    for kind in range(2):
        for pair in range(PAIRS):
            n = kind * PAIRS + pair
            sums[n] = sums[n] + fold(history[kind, pair, row] * values)


def chip_dots_kernel(count, grad, *refs):
    pieces, out = refs[:count], refs[-1]
    total, piece = grad.shape[0], pieces[0].shape[3]
    odd = odd_depth()
    sums = [jnp.zeros((8, grad.shape[2]), F32) for _ in range(2 * PAIRS)]
    for place in range(total):
        source = natural_row(place, total, odd)
        for turn, ref in enumerate(pieces):
            offset = lax.rem(lax.axis_index("shot") + turn, count) * piece
            values = grad[place, pl.ds(pl.multiple_of(offset, 8), piece), :]
            add_dots(sums, values, ref, source)
    for n in range(2 * PAIRS):
        out[n] = sums[n]


def line_kernel(count, chip, gram, history, *refs):
    inner, core, out, o_near = refs[:count], refs[count : 2 * count], refs[-2], refs[-1]
    rows = history.shape[2]
    odd = odd_depth()
    sums = [chip[n] for n in range(2 * PAIRS)]
    for place, row in enumerate(near_rows(rows)):
        parts, at = (inner, place) if place < inner[0].shape[0] else (core, place - inner[0].shape[0])
        values = parts[0][at]
        for other in parts[1:]:
            values = values + other[at]
        o_near[place] = values
        add_dots(sums, values, history, natural_row(row, rows, odd))
    lane = lane_ids(out.shape[1])
    line = jnp.zeros((1, out.shape[1]), F32)
    for n in range(FIRST_DOT + 2 * PAIRS):
        value = gram[n] if n < FIRST_DOT else sums[n - FIRST_DOT]
        line = line + jnp.where(lane == n, jnp.sum(value, axis=(0, 1), keepdims=True), 0.0)
    out[...] = jnp.broadcast_to(line, out.shape)


def weights(line):
    lane = lane_ids(line.shape[1])

    def number(n):
        return jnp.sum(jnp.where(lane == n, line, 0.0), axis=(0, 1), keepdims=True)

    values = [number(n) for n in range(FIRST_DOT + 2 * PAIRS)]

    def sy(a, b):
        return values[SLOT[0, a, 1, b]]

    def yy(a, b):
        return values[SLOT[1, min(a, b), 1, max(a, b)]]

    s_grad = values[FIRST_DOT : FIRST_DOT + PAIRS]
    y_grad = values[FIRST_DOT + PAIRS :]
    rho = [1.0 / sy(i, i) for i in range(PAIRS)]
    alpha = [None] * PAIRS
    for i in reversed(range(PAIRS)):
        dot = s_grad[i]
        for j in range(PAIRS - 1, i, -1):
            dot = dot - alpha[j] * sy(i, j)
        alpha[i] = rho[i] * dot
    scale = sy(PAIRS - 1, PAIRS - 1) / yy(PAIRS - 1, PAIRS - 1)
    s_weight = [None] * PAIRS
    for i in range(PAIRS):
        dot = y_grad[i]
        for j in range(PAIRS):
            dot = dot - alpha[j] * yy(i, j)
        dot = scale * dot
        for j in range(i):
            dot = dot + s_weight[j] * sy(j, i)
        s_weight[i] = alpha[i] - rho[i] * dot
    return scale, [-(scale * a) for a in alpha], s_weight


def weights_kernel(lines, near, history, *refs):
    o_weights, o_move = refs[-2:]
    rows = history.shape[2]
    piece, width = near.shape[1], near.shape[2]
    odd = odd_depth()
    total = lines[0:8]
    for start in range(8, lines.shape[0], 8):
        total = total + lines[start : start + 8]
    scale, y_weight, s_weight = weights(jnp.sum(total, axis=0, keepdims=True))
    wide = [jnp.broadcast_to(v, (8, width)) for v in [scale] + s_weight + y_weight]
    for n, value in enumerate(wide):
        o_weights[n] = value
    for place, row in enumerate(near_rows(rows)):
        source = natural_row(row, rows, odd)
        for start in range(0, piece, 8):
            at = slice(start, start + 8)
            o_move[place, at, :] = move_of(wide, near[place, at, :], history, source, at)


def move_of(wide, grad, history, row, at):
    move = wide[0] * grad
    for pair in range(PAIRS):
        move = move + wide[1 + pair] * history[0, pair, row, at, :]
        move = move + wide[1 + PAIRS + pair] * history[1, pair, row, at, :]
    return -move


def finish_kernel(count, weight, courant, near, near_move, chip, *refs):
    others, pieces = refs[: count - 1], refs[count - 1 : 2 * count - 1]
    o_grad, o_direction, o_next = refs[2 * count - 1 :]
    rows, across, width = courant.shape
    piece = across // count
    odd = odd_depth()
    wide = [weight[n] for n in range(1 + 2 * PAIRS)]
    mine = pl.ds(pl.multiple_of(lax.axis_index("shot") * piece, 8), piece)
    for place, row in enumerate(near_rows(rows)):
        source = natural_row(row, rows, odd)
        o_grad[source] = near[place]
        o_direction[source] = near_move[place]
        o_next[source, mine, :] = courant[source, mine, :] + 0.05 * near_move[place]
    for row in range(REACH):
        source = natural_row(row, rows, odd)
        kept = natural_row(row, REACH, odd)
        for turn, ref in enumerate(pieces):
            offset = lax.rem(lax.axis_index("shot") + turn, count) * piece
            for start in range(0, piece, 8):
                at = pl.ds(pl.multiple_of(offset + start, 8), 8)
                grad = chip[row, at, :]
                for other in others:
                    grad = grad + other[row, at, :]
                move = move_of(wide, grad, ref, kept, slice(start, start + 8))
                if turn == 0:
                    o_grad[source, start : start + 8, :] = grad
                    o_direction[source, start : start + 8, :] = move
                o_next[source, at, :] = courant[source, at, :] + 0.05 * move


def last_piece_kernel(count, courant, done, *refs):
    moves, o_next, buffer, sem = refs[: count - 1], refs[-3], refs[-2], refs[-1]
    rows, across, width = courant.shape
    piece = across // count
    odd = odd_depth()
    first = (1 - odd) * REACH
    copies = []
    for turn in range(1, count):
        offset = pl.multiple_of(lax.rem(lax.axis_index("shot") + turn, count) * piece, 8)
        for place, row in enumerate(near_rows(rows)):
            source = natural_row(row, rows, odd)
            value = courant[source, pl.ds(offset, piece), :] + 0.05 * moves[turn - 1][place]
            buffer[turn - 1, source - first] = value
        copies.append(
            pltpu.make_async_copy(
                buffer.at[turn - 1],
                o_next.at[pl.ds(first, rows - REACH), pl.ds(offset, piece)],
                sem.at[turn - 1],
            )
        )
        copies[-1].start()
    for copy in copies:
        copy.wait()


def call(
    kernel, name, outs, *args, specs=None, out_specs=None, aliases=None, scratch=(), cost=1 << 20
):
    return pl.pallas_call(
        kernel,
        name=name,
        out_shape=outs,
        in_specs=specs or [VM] * len(args),
        out_specs=out_specs or jax.tree.map(lambda _: VM, outs),
        input_output_aliases=aliases or {},
        scratch_shapes=list(scratch),
        compiler_params=PARAMS,
        cost_estimate=pl.CostEstimate(flops=cost, bytes_accessed=cost, transcendentals=0),
    )(*args)


def per_device(
    courant,
    wave_before,
    wave_current,
    adjoint_after,
    adjoint_current,
    source_cell,
    wavelet,
    receiver_cell,
    residual,
    history,
):
    rows, across, width = courant.shape
    depths = lax.axis_size("depth")
    shots = lax.axis_size("shot")
    devices = depths * shots
    piece = across // shots
    slab = shape(rows, across, width)
    padded = shape(rows, across + 2 * PAD, width)
    halo = shape(2 * REACH, across, width)
    on_chip = [(i, i ^ 1) for i in range(depths)]
    off_chip = [(i, i + 1 if i % 2 else i - 1) for i in range(1, depths - 1)]

    def swap_core(value):
        return lax.ppermute(value, "depth", on_chip)

    def swap_chip(value):
        return lax.ppermute(value, "depth", off_chip)

    def from_shot(value, turn):
        return lax.ppermute(value, "shot", [((i + turn) % shots, i) for i in range(shots)])

    block = pltpu.VMEM((rows, across, width), F32)
    held = [
        in_hbm(value)
        for value in (wave_current[0], wave_before[0], adjoint_current[0], adjoint_after[0], courant, history)
    ]
    bands = [jax.ShapeDtypeStruct((2 * width, n * width), jnp.bfloat16) for n in (2, 1)]
    outer_rows = pltpu.VMEM((2, REACH, across, width), F32)
    to_chip, to_core = call(
        first_send_kernel,
        "first_send",
        [halo, halo],
        held[0],
        held[2],
        held[4],
        specs=[HB] * 3,
        scratch=[outer_rows] * 3 + [pltpu.SemaphoreType.DMA((6,))],
    )
    from_chip = swap_chip(to_chip)
    from_core = swap_core(to_core)
    wave, wave_old, adj, adj_old, cour, prod, *bands = call(
        stage_kernel,
        "stage",
        [padded, padded, slab, slab, slab, padded] + bands,
        *held[:5],
        specs=[HB] * 5,
        scratch=[block] * 5 + [pltpu.SemaphoreType.DMA((5,))],
    )
    kept = call(
        keep_kernel,
        "keep",
        shape(2, PAIRS, REACH, piece, width),
        held[5],
        from_core,
        specs=[HB, VM],
        scratch=[pltpu.SemaphoreType.DMA],
    )
    kept = [kept] + [from_shot(kept, turn) for turn in range(1, shots)]
    injected = call(
        functools.partial(receiver_kernel, across),
        "receivers",
        shape(STEPS, rows * across, width),
        receiver_cell,
        residual[0],
    )

    gram = call(gram_kernel, "gram", shape(len(PRODUCTS), 8, width), history)

    scale = 1.0 / (shots * STEPS)

    def some_rows(count, copies):
        return [pltpu.VMEM((count, across, width), F32)] * copies

    laps, adjs = [], []
    for moment in range(STEPS - 1):
        lap, new_wave, new_adj, new_prod = call(
            functools.partial(local_kernel, moment),
            f"local_{moment}",
            [slab, padded, slab, padded],
            source_cell,
            wavelet,
            wave,
            wave_old,
            prod,
            adj,
            adj_old,
            cour,
            injected,
            *bands,
            *([gram] if moment == STEPS - 2 else []),
            specs=[SM, SM] + [VM] * (10 if moment == STEPS - 2 else 9),
            scratch=[block] * 2,
        )
        sends = []
        for chip, came in ((False, from_core), (True, from_chip)):
            arrays = (came, cour, *(in_vmem(value) for value in (lap, new_wave, new_adj, new_prod)))
            if moment == STEPS - 2 and not chip:
                lap, new_wave, new_adj, new_prod, send, far = call(
                    functools.partial(join_far_kernel, scale),
                    "join_far",
                    [slab, padded, slab, padded, halo, shape(rows - 3 * REACH, across, width)],
                    *arrays,
                    adj,
                    injected,
                    *bands,
                    *laps,
                    adjs[0],
                    aliases={2: 0, 3: 1, 4: 2, 5: 3},
                    scratch=some_rows(rows - 3 * REACH, 2),
                )
            else:
                lap, new_wave, new_adj, new_prod, send = call(
                    functools.partial(join_kernel, chip),
                    f"join_{'chip' if chip else 'core'}_{moment}",
                    [slab, padded, slab, padded, halo],
                    *arrays,
                    aliases={2: 0, 3: 1, 4: 2, 5: 3},
                )
            sends.append(send)
        from_core = swap_core(sends[0])
        from_chip = swap_chip(sends[1])
        laps.append(lap)
        adjs.append(new_adj)
        wave_old, wave = wave, new_wave
        adj_old, adj = adj, new_adj
        prod = new_prod

    inner_count, near_count = rows - 2 * REACH, rows - REACH
    last = (wave, prod, adj, adj_old, injected, *bands, laps[0], laps[1], laps[2], adjs[0], adjs[1])

    def sum_parts(values):
        return [values[0]] + [from_shot(values[shots - turn], turn) for turn in range(1, shots)]

    core = call(
        functools.partial(core_kernel, scale),
        "core",
        [shape(REACH, piece, width)] * shots,
        from_core,
        *last,
        scratch=some_rows(REACH, 3),
    )
    inner = call(
        functools.partial(inner_kernel, scale),
        "inner",
        [shape(inner_count, piece, width)] * shots,
        core[0],
        far,
        *last,
        scratch=some_rows(inner_count, 1) + some_rows(REACH, 2),
    )
    core, inner = sum_parts(core), sum_parts(inner)
    chip_part = shape(REACH, across, width)
    known, lap, new_adj = call(chip_kernel, "chip", [chip_part] * 3, *last, *kept[1:], scratch=some_rows(REACH, 2))
    chip = call(
        functools.partial(last_join_kernel, scale),
        "last_join",
        chip_part,
        from_chip,
        known,
        lap,
        new_adj,
        laps[0],
        adjs[0],
        *core[1:],
    )
    others = [from_shot(chip, turn) for turn in range(1, shots)]
    chip_dots = call(
        functools.partial(chip_dots_kernel, shots),
        "chip_dots",
        shape(2 * PAIRS, 8, width),
        chip,
        *kept,
        *inner[1:],
    )
    near = shape(near_count, piece, width)
    line, near_grad = call(
        functools.partial(line_kernel, shots),
        "line",
        [shape(devices, 128), near],
        chip_dots,
        gram,
        history,
        *inner,
        *core,
    )
    lines = lax.all_to_all(line, ("depth", "shot"), 0, 0, tiled=True)
    weight, move = call(
        weights_kernel,
        "weights",
        [shape(1 + 2 * PAIRS, 8, width), near],
        lines,
        near_grad,
        history,
        *others,
    )
    moves = [from_shot(move, turn) for turn in range(1, shots)]
    own = shape(rows, piece, width)
    gradient, direction, courant_next = call(
        functools.partial(finish_kernel, shots),
        "finish",
        [own, own, slab],
        weight,
        courant,
        near_grad,
        move,
        chip,
        *others,
        *kept,
    )
    courant_next = call(
        functools.partial(last_piece_kernel, shots),
        "last_piece",
        slab,
        courant,
        courant_next,
        *moves,
        specs=[VM, HB] + [VM] * (shots - 1),
        out_specs=HB,
        aliases={1: 0},
        scratch=[
            pltpu.VMEM((shots - 1, near_count, piece, width), F32),
            pltpu.SemaphoreType.DMA((shots - 1,)),
        ],
    )
    return gradient, direction, courant_next


def solution(mesh):
    return jax.shard_map(
        per_device,
        mesh=mesh,
        in_specs=(
            P("depth", None, None),
            P("shot", "depth", None, None),
            P("shot", "depth", None, None),
            P("shot", "depth", None, None),
            P("shot", "depth", None, None),
            P("shot"),
            P("shot", None),
            P("shot", None),
            P("shot", None, None),
            P(None, None, "depth", "shot", None),
        ),
        out_specs=(P("depth", "shot", None), P("depth", "shot", None), P("depth", None, None)),
        check_vma=False,
    )
```
